256 devices in a mesh: grp: 8 (over x, core), dev: 32 (over y, z).
Axes of the slice: x: 4, y: 4, z: 8, core: 2. Of those that a mesh axis runs over, the one named last changes fastest.
Arguments:
- table: bfloat16 [16384, 1024], P('dev'), may hold values from -6 to 6
- target_table: bfloat16 [16384, 256], P('dev'), may hold values from -6 to 6
- centres: bfloat16 [131072, 1024], P(('grp', 'dev')), may hold values from -6 to 6
- coefficients: float32 [131072, 256], P(('grp', 'dev')), may hold values from -6 to 6
- batch_index: int32 [2, 256], replicated, may hold values from 0 to 16383
Outputs:
- coefficients_out: float32 [131072, 256], P(('grp', 'dev'))
- residuals: float32 [2, 256, 256], replicated
The draws below stay inside these ranges and needn't reach their ends.
Inputs may be any that keep to these rules, and one draw needn't show every extreme that they name: `batch_index`: row numbers into the descriptor table.
All inputs are finite; a program needn't handle non-finite values.
Results may differ from the reference program's by a relative error of at most 0.0004.
Values may be sent and summed in bfloat16 or wider, within the bound.
A program may use at most 64 MiB of HBM per device.

```python
import math
import jax
import jax.numpy as jnp
from jax import lax

D = 1024
C = 256
BATCH = 256
STEPS = 2
CENTRES = 131072
TABLE = 16384


def feature_draw(key, count, width):
    values = jnp.clip(jax.random.normal(key, (count, width), jnp.float32), -6.0, 6.0)
    return values.astype(jnp.bfloat16)


def draw_table(key, part):
    return feature_draw(jax.random.fold_in(key, 11), TABLE, D)


def draw_centres(key, part):
    return feature_draw(jax.random.fold_in(key, 23), CENTRES, D)


def place_ends(entries, rng, smallest, largest):
    longest = entries.shape.index(max(entries.shape))
    spots = []
    for shift in (0, 1):
        where = [jax.random.randint(jax.random.fold_in(rng, axis), (), 0, length) for axis, length in enumerate(entries.shape)]
        where[longest] = (where[longest] + shift) % entries.shape[longest]
        spots.append(tuple(where))
    return entries.at[spots[0]].set(smallest).at[spots[1]].set(largest)


def steps_of(rng, extent, pieces, low, top_value):
    def one(axis_at, shards_of):
        heights = jax.random.uniform(jax.random.fold_in(jax.random.fold_in(rng, 6), axis_at), (shards_of,), jnp.float32, low / len(pieces), top_value / len(pieces))
        return jnp.repeat(jnp.exp(heights), extent[axis_at] // shards_of).reshape((-1,) + (1,) * (len(extent) - axis_at - 1))

    loudness = one(*pieces[0])
    for cut in pieces[1:]:
        loudness = loudness * one(*cut)
    return loudness


def normal_values(rng, dims, scale, most, cuts=(), kind=jnp.bfloat16):
    drawn = jax.random.normal(rng, dims, jnp.float32) * scale
    if len(cuts) > 0:
        drawn = steps_of(rng, dims, cuts, -0.22, 0.18) * drawn
    return jnp.clip(drawn, min=-most, max=most).astype(kind)


def setup_inputs(seed: int = 0) -> dict:
    arg_keys = jax.random.split(jax.random.key(seed), 6)
    return {
        "table": draw_table(jax.random.fold_in(arg_keys[5], 71), 0),
        "target_table": normal_values(arg_keys[1], (TABLE, C), 1.0, 6.0, ((0, 32),)),
        "centres": draw_centres(jax.random.fold_in(arg_keys[5], 71), 0),
        "coefficients": normal_values(arg_keys[3], (CENTRES, C), 1.0, 6.0, ((0, 256),), jnp.float32),
        "batch_index": place_ends(jax.random.randint(arg_keys[4], (STEPS, BATCH), 0, TABLE), jax.random.fold_in(arg_keys[4], 1), 0, TABLE - 1).astype(jnp.int32),
    }


SPREAD = 2.0
RATE = 2.0

def laplace(rows, centres, centre_norm, radius):
    row_norm = lax.optimization_barrier(jnp.sum(jnp.square(rows.astype(jnp.float32)), axis=1))
    cross = lax.dot_general(rows, centres, (((1,), (1,)), ((), ())), preferred_element_type=jnp.float32)
    squared = row_norm[:, None] + centre_norm[None, :] - 2.0 * cross
    dist = jnp.sqrt(jnp.maximum(squared, 0.0))
    return jnp.exp((radius - dist) / SPREAD)

def reference(table, target_table, centres, coefficients, batch_index):
    total = centres.shape[0]
    scale = 1.0 / math.sqrt(total)
    radius = math.sqrt(2.0 * centres.shape[1])
    centre_norm = lax.optimization_barrier(jnp.sum(jnp.square(centres.astype(jnp.float32)), axis=1))
    coef = coefficients
    kept = []
    for step in range(STEPS):
        index = batch_index[step]
        rows = jnp.take(table, index, axis=0)
        aims = jnp.take(target_table, index, axis=0).astype(jnp.float32)
        weights = laplace(rows, centres, centre_norm, radius)
        pred = jnp.dot(weights, coef, precision=lax.Precision.HIGHEST, preferred_element_type=jnp.float32) * scale
        mass = lax.optimization_barrier(jnp.sum(weights, axis=1)) * scale
        resid = pred - aims
        along = jnp.dot(mass, resid, precision=lax.Precision.HIGHEST) / jnp.sum(mass * mass)
        proj = resid - mass[:, None] * along[None, :]
        grad = lax.dot_general(weights, proj, (((0,), (0,)), ((), ())), precision=lax.Precision.HIGHEST, preferred_element_type=jnp.float32)
        coef = coef - grad * (RATE * scale)
        kept.append(resid)
    return (coef, jnp.stack(kept))
```

```python
import math

import jax
import jax.numpy as jnp
from jax import lax
from jax.experimental import pallas as pl
from jax.experimental.pallas import tpu as pltpu
from jax.sharding import PartitionSpec as P

MESH = pl.DeviceIdType.MESH
SPREAD = 2.0
RATE = 2.0
NX, NC, NY, NZ = 4, 2, 4, 8
NP = NX * NY
ND = NY * NZ
F32 = jnp.float32
BF16 = jnp.bfloat16
HI = lax.Precision.HIGHEST
NT = (((1,), (1,)), ((), ()))
TN = (((0,), (0,)), ((), ()))
Z_ORDER = (4, 3, 5, 2, 6, 1, 7)


def dot(a, b, dims=(((1,), (0,)), ((), ())), precision=None):
    return lax.dot_general(a, b, dims, precision=precision, preferred_element_type=F32)


def kernel(
    table, target, centres, coef, index,
    coef_out, resid_out,
    tab_v, tgt_v, cen_v, cf_v, idx_v, aims_v,
    pick, parts, rows,
    w_v, core_send, core_recv, xy_send, xy_recv, z_buf, whole,
    load_sem, a_send, a_recv, az_recv, axy_recv, ac_recv,
    cc_send, cc_recv, cxy_recv, cz_recv, gxy_recv, gc_recv,
):
    g = lax.axis_index("grp")
    d = lax.axis_index("dev")
    x, c = g // 2, g % 2
    y, z = d // NZ, d % NZ
    p = x * NY + y
    feat = c * NX + x
    chunk = z * NY + y
    radius = math.sqrt(2.0 * 1024)
    scale = 1.0 / math.sqrt(131072)

    def at_dev(k):
        return {"grp": g, "dev": k}

    def at_xy(k):
        q = lax.rem(p + k, NP)
        return q, {"grp": (q // NY) * 2 + c, "dev": (q % NY) * NZ + z}

    sibling = {"grp": x * 2 + 1 - c, "dev": d}

    barrier = pltpu.get_barrier_semaphore()

    def greet_dev(k, _):
        pl.semaphore_signal(barrier, inc=1, device_id=at_dev(lax.rem(d + k, ND)), device_id_type=MESH)
        return 0

    def greet_x(k, _):
        dx, ty = 1 + k // NY, k % NY
        tx = lax.rem(x + dx, NX)
        pl.semaphore_signal(
            barrier, inc=1, device_id={"grp": tx * 2 + c, "dev": ty * NZ + z}, device_id_type=MESH
        )
        return 0

    lax.fori_loop(1, ND, greet_dev, 0)
    lax.fori_loop(0, (NX - 1) * NY, greet_x, 0)
    pl.semaphore_signal(barrier, inc=1, device_id=sibling, device_id_type=MESH)

    loads = [
        pltpu.make_async_copy(index, idx_v, load_sem.at[0]),
        pltpu.make_async_copy(
            table.at[:, pl.ds(pl.multiple_of(feat * 128, 128), 128)], tab_v, load_sem.at[1]
        ),
        pltpu.make_async_copy(target, tgt_v, load_sem.at[2]),
        pltpu.make_async_copy(centres, cen_v, load_sem.at[3]),
        pltpu.make_async_copy(coef, cf_v, load_sem.at[4]),
    ]
    for load in loads:
        load.start()

    loads[0].wait()
    here = lax.broadcasted_iota(jnp.int32, (512, 256), 0) + d * 512
    hot = jnp.concatenate(
        [(here == idx_v[s : s + 1, :]).astype(F32).astype(BF16) for s in range(2)], axis=1
    )
    loads[1].wait()
    pick[...] = dot(hot, tab_v[...], TN).astype(BF16).reshape(ND, 16, 128)
    parts[chunk] = pick[chunk]

    pl.semaphore_wait(barrier, ND - 1 + (NX - 1) * NY + 1)

    def send_pick(k, _):
        to = lax.rem(d + k, ND)
        slot = (to % NZ) * NY + to // NZ
        pltpu.make_async_remote_copy(
            src_ref=pick.at[slot], dst_ref=parts.at[chunk], send_sem=a_send.at[0], recv_sem=a_recv,
            device_id=at_dev(to), device_id_type=MESH,
        ).start()
        return 0

    lax.fori_loop(1, ND, send_pick, 0)

    loads[2].wait()
    first = (g == 0).astype(F32)
    aims_v[...] = dot(hot, tgt_v[...], TN) * first
    loads[3].wait()
    square = jnp.square(cen_v[...].astype(F32))
    high = square.astype(BF16)
    low = (square - high.astype(F32)).astype(BF16)
    ones = jnp.ones((8, 1024), BF16)
    cnorm = (dot(ones, high, NT) + dot(ones, low, NT))[0:1, :]

    def wait_bytes(ref, sem):
        pltpu.make_async_copy(ref, ref, sem).wait()

    wait_bytes(parts.at[pl.ds(0, ND - 1)], a_recv)
    own = jnp.sum(parts[...].astype(F32), axis=0).astype(BF16)
    lane = pl.ds(pl.multiple_of(feat * 128, 128), 128)
    rows[pl.ds(pl.multiple_of(chunk * 16, 16), 16), lane] = own

    def block(zz):
        return rows.at[pl.ds(pl.multiple_of((zz * NY + y) * 16, 16), 16), lane]

    for k in Z_ORDER:
        pltpu.make_async_remote_copy(
            src_ref=block(z), dst_ref=block(z), send_sem=a_send.at[1], recv_sem=az_recv.at[k],
            device_id=at_dev(y * NZ + lax.rem(z + k, NZ)), device_id_type=MESH,
        ).start()

    def pass_on(k):
        zz = lax.rem(z + NZ - k, NZ)

        def one(j, _):
            _, to = at_xy(j)
            pltpu.make_async_remote_copy(
                src_ref=block(zz), dst_ref=block(zz), send_sem=a_send.at[2], recv_sem=axy_recv.at[k],
                device_id=to, device_id_type=MESH,
            ).start()
            return 0

        lax.fori_loop(1, NP, one, 0)

    pass_on(0)
    for k in (1, 7, 2, 6, 3, 5, 4):
        wait_bytes(block(z), az_recv.at[k])
        pass_on(k)

    half = pl.ds(pl.multiple_of(c * 512, 512), 512)
    to_core = []
    for k in (0, 1, 7, 2, 6, 3, 5, 4):
        zz = lax.rem(z + NZ - k, NZ)
        wait_bytes(parts.at[pl.ds(0, NP - 1)], axy_recv.at[k])
        strip = rows.at[pl.ds(pl.multiple_of(zz * 64, 64), 64), half]
        copy = pltpu.make_async_remote_copy(
            src_ref=strip, dst_ref=strip, send_sem=a_send.at[3], recv_sem=ac_recv,
            device_id=sibling, device_id_type=MESH,
        )
        copy.start()
    wait_bytes(rows.at[:, pl.ds(0, 512)], ac_recv)

    all_rows = rows[...]
    rnorm = jnp.sum(jnp.square(all_rows.astype(F32)), axis=1, keepdims=True)
    cross = dot(all_rows, cen_v[...], NT)
    dist = jnp.sqrt(jnp.maximum(rnorm + cnorm - 2.0 * cross, 0.0))
    w_v[...] = jnp.exp((radius - dist) / SPREAD) * scale
    loads[4].wait()

    mass0 = dot(jnp.ones((8, 512), F32), w_v[0:256, :], NT, HI)
    mass1 = dot(jnp.ones((8, 512), F32), w_v[256:512, :], NT, HI)
    mass = jnp.concatenate(
        [mass0[0:1, 0:128], mass0[0:1, 128:256], mass1[0:1, 0:128], mass1[0:1, 128:256],
         jnp.zeros((4, 128), F32)], axis=0,
    )

    def partials(h, dst):
        r0 = pl.ds(pl.multiple_of(h * 128, 128), 128)
        r1 = pl.ds(pl.multiple_of(h * 128 + 256, 128), 128)
        w0, w1 = w_v[r0, :], w_v[r1, :]
        s0 = dot(w0, cf_v[...], precision=HI) - aims_v[r0, :]
        s1 = dot(w1, cf_v[...], precision=HI) - aims_v[r1, :]
        gram = dot(w1, w_v[0:256, :], NT, HI)
        for n, part in enumerate((s0, s1, gram)):
            for m in range(2):
                at = n * 16 + m * 8
                dst[:, at : at + 8, :] = part[:, m * 128 : m * 128 + 128].reshape(NP, 8, 128)
        dst[:, 48:56, :] = jnp.broadcast_to(mass[None], (NP, 8, 128))

    partials(1 - c, core_send)
    core_copy = pltpu.make_async_remote_copy(
        src_ref=core_send, dst_ref=core_recv, send_sem=cc_send, recv_sem=cc_recv,
        device_id=sibling, device_id_type=MESH,
    )
    core_copy.start()
    partials(c, xy_send)
    core_copy.wait()
    xy_send[...] = xy_send[...] + core_recv[...]
    xy_recv[p] = xy_send[p]

    def send_sum(k, _):
        q, to = at_xy(k)
        pltpu.make_async_remote_copy(
            src_ref=xy_send.at[q], dst_ref=xy_recv.at[p], send_sem=a_send.at[4], recv_sem=cxy_recv,
            device_id=to, device_id_type=MESH,
        ).start()
        return 0

    lax.fori_loop(1, NP, send_sum, 0)
    wait_bytes(xy_recv.at[pl.ds(0, NP - 1)], cxy_recv)
    z_buf[z] = jnp.sum(xy_recv[...], axis=0)

    for k in Z_ORDER:
        pltpu.make_async_remote_copy(
            src_ref=z_buf.at[z], dst_ref=z_buf.at[z], send_sem=a_send.at[5], recv_sem=cz_recv,
            device_id=at_dev(y * NZ + lax.rem(z + k, NZ)), device_id_type=MESH,
        ).start()
    wait_bytes(z_buf.at[pl.ds(0, NZ - 1)], cz_recv)
    total = jnp.sum(z_buf[...], axis=0)
    whole[c, p] = total[0:48]

    def send_whole(k, _):
        _, to = at_xy(k)
        pltpu.make_async_remote_copy(
            src_ref=whole.at[c, p], dst_ref=whole.at[c, p], send_sem=a_send.at[6], recv_sem=gxy_recv,
            device_id=to, device_id_type=MESH,
        ).start()
        return 0

    lax.fori_loop(1, NP, send_whole, 0)
    wait_bytes(whole.at[0, pl.ds(0, NP - 1)], gxy_recv)
    last = pltpu.make_async_remote_copy(
        src_ref=whole.at[c], dst_ref=whole.at[c], send_sem=a_send.at[7], recv_sem=gc_recv,
        device_id=sibling, device_id_type=MESH,
    )
    last.start()
    last.wait()

    def piece(n):
        halves = [
            jnp.concatenate(
                [whole[h, :, n * 16 + m * 8 : n * 16 + m * 8 + 8, :].reshape(128, 128) for m in range(2)],
                axis=1,
            )
            for h in range(2)
        ]
        return jnp.concatenate(halves, axis=0)

    def project(resid, m):
        row = jnp.concatenate([total[48 + 2 * m : 49 + 2 * m], total[49 + 2 * m : 50 + 2 * m]], axis=1)
        row8 = jnp.broadcast_to(row, (8, 256))
        along = dot(row8, resid, precision=HI) / jnp.sum(row * row)
        only = (lax.broadcasted_iota(jnp.int32, (8, 256), 0) == 0).astype(F32)
        return resid - dot(row8 * only, along, TN, HI)

    resid0 = piece(0)
    resid_out[0] = resid0
    proj0 = project(resid0, 0)
    resid1 = piece(1) - RATE * dot(piece(2), proj0, precision=HI)
    resid_out[1] = resid1
    proj1 = project(resid1, 1)
    grad = dot(w_v[...], jnp.concatenate([proj0, proj1], axis=0), TN, HI)
    coef_out[...] = cf_v[...] - RATE * grad

    wait_bytes(parts.at[pl.ds(0, ND - 1)], a_send.at[0])
    wait_bytes(parts.at[pl.ds(0, NZ - 1)], a_send.at[1])
    for _ in range(1):
        wait_bytes(rows.at[pl.ds(0, 480), pl.ds(0, 512)], a_send.at[2])
    wait_bytes(rows.at[:, pl.ds(0, 512)], a_send.at[3])
    wait_bytes(xy_recv.at[pl.ds(0, NP - 1)], a_send.at[4])
    wait_bytes(z_buf.at[pl.ds(0, NZ - 1)], a_send.at[5])
    wait_bytes(whole.at[0, pl.ds(0, NP - 1)], a_send.at[6])


def body(table, target_table, centres, coefficients, batch_index):
    dma = pltpu.SemaphoreType.DMA
    return pl.pallas_call(
        kernel,
        name="regression_steps",
        out_shape=(
            jax.ShapeDtypeStruct((512, 256), F32),
            jax.ShapeDtypeStruct((2, 256, 256), F32),
        ),
        in_specs=[pl.BlockSpec(memory_space=pl.ANY)] * 5,
        out_specs=(pl.BlockSpec(memory_space=pltpu.VMEM), pl.BlockSpec(memory_space=pltpu.VMEM)),
        scratch_shapes=[
            pltpu.VMEM((512, 128), BF16),
            pltpu.VMEM((512, 256), BF16),
            pltpu.VMEM((512, 1024), BF16),
            pltpu.VMEM((512, 256), F32),
            pltpu.VMEM((2, 256), jnp.int32),
            pltpu.VMEM((512, 256), F32),
            pltpu.VMEM((ND, 16, 128), BF16),
            pltpu.VMEM((ND, 16, 128), BF16),
            pltpu.VMEM((512, 1024), BF16),
            pltpu.VMEM((512, 512), F32),
            pltpu.VMEM((NP, 56, 128), F32),
            pltpu.VMEM((NP, 56, 128), F32),
            pltpu.VMEM((NP, 56, 128), F32),
            pltpu.VMEM((NP, 56, 128), F32),
            pltpu.VMEM((NZ, 56, 128), F32),
            pltpu.VMEM((2, NP, 48, 128), F32),
            dma((5,)), dma((8,)), dma, dma((NZ,)), dma((NZ,)), dma,
            dma, dma, dma, dma, dma, dma,
        ],
        compiler_params=pltpu.CompilerParams(
            collective_id=0, has_side_effects=True, vmem_limit_bytes=56 * 2**20
        ),
    )(table, target_table, centres, coefficients, batch_index)


def solution(mesh):
    in_specs = (
        P("dev", None),
        P("dev", None),
        P(("grp", "dev"), None),
        P(("grp", "dev"), None),
        P(),
    )
    out_specs = (P(("grp", "dev"), None), P())
    return jax.shard_map(body, mesh=mesh, in_specs=in_specs, out_specs=out_specs, check_vma=False)
```

```python
import math

import jax
import jax.numpy as jnp
from jax import lax
from jax.experimental import pallas as pl
from jax.experimental.pallas import tpu as pltpu
from jax.sharding import PartitionSpec as P

MESH = pl.DeviceIdType.MESH
SPREAD = 2.0
RATE = 2.0
NX, NC, NY, NZ = 4, 2, 4, 8
NP = NX * NY
ND = NY * NZ
F32 = jnp.float32
BF16 = jnp.bfloat16
HI = lax.Precision.HIGHEST
NN = (((1,), (0,)), ((), ()))
NT = (((1,), (1,)), ((), ()))
TN = (((0,), (0,)), ((), ()))


def hops(k, n):
    return min(k, n - k)


Z_FAR = sorted(range(1, NZ), key=lambda k: -hops(k, NZ))
Z_NEAR = Z_FAR[::-1]
XY_FAR = sorted(
    [(i, j) for i in range(NX) for j in range(NY) if i or j],
    key=lambda o: -hops(o[0], NX) - hops(o[1], NY),
)
YZ_FAR = sorted(
    [(j, k) for j in range(NY) for k in range(NZ) if j or k],
    key=lambda o: -hops(o[0], NY) - hops(o[1], NZ),
)


def dot(a, b, dims=NN, precision=None):
    return lax.dot_general(a, b, dims, precision=precision, preferred_element_type=F32)


def split(a):
    high = a.astype(BF16)
    return high, (a - high.astype(F32)).astype(BF16)


def exchange(
    table, target, centres, coef, index,
    whole, mass_out, wt_high, wt_low,
    tab_v, tgt_v, cen_v, cf_v, idx_v, aims_v, cf_high, cf_low,
    pick, parts, rows,
    w_high, w_low, core_send, core_recv, xy_send, xy_recv, z_buf,
    load_sem, sent, a_recv, az_recv, axy_recv, ac_recv,
    cc_send, cc_recv, cxy_recv, cz_recv, gxy_recv, gc_recv,
):
    g = lax.axis_index("grp")
    d = lax.axis_index("dev")
    x, c = g // 2, g % 2
    y, z = d // NZ, d % NZ
    p = x * NY + y
    feat = c * NX + x
    chunk = z * NY + y
    radius = math.sqrt(2.0 * 1024)
    scale = 1.0 / math.sqrt(131072)

    xs = [lax.rem(x + k, NX) for k in range(NX)]
    ys = [lax.rem(y + k, NY) for k in range(NY)]
    zs = [lax.rem(z + k, NZ) for k in range(NZ)]
    grps = [v * 2 + c for v in xs]
    bases = [v * NZ for v in ys]

    def at_xy(o):
        return {"grp": grps[o[0]], "dev": bases[o[1]] + z}

    def at_yz(o):
        return {"grp": g, "dev": bases[o[0]] + zs[o[1]]}

    sibling = {"grp": x * 2 + 1 - c, "dev": d}

    def send(src, dst, send_sem, recv_sem, to):
        copy = pltpu.make_async_remote_copy(
            src_ref=src, dst_ref=dst, send_sem=send_sem, recv_sem=recv_sem,
            device_id=to, device_id_type=MESH,
        )
        copy.start()
        return copy

    def wait_bytes(ref, sem):
        pltpu.make_async_copy(ref, ref, sem).wait()

    barrier = pltpu.get_barrier_semaphore()
    greeted = [at_yz(o) for o in YZ_FAR] + [at_xy(o) for o in XY_FAR if o[0]] + [sibling]
    for to in greeted:
        pl.semaphore_signal(barrier, inc=1, device_id=to, device_id_type=MESH)

    loads = [
        pltpu.make_async_copy(index, idx_v, load_sem.at[0]),
        pltpu.make_async_copy(
            table.at[:, pl.ds(pl.multiple_of(feat * 128, 128), 128)], tab_v, load_sem.at[1]
        ),
        pltpu.make_async_copy(target, tgt_v, load_sem.at[2]),
        pltpu.make_async_copy(centres, cen_v, load_sem.at[3]),
        pltpu.make_async_copy(coef, cf_v, load_sem.at[4]),
    ]
    for load in loads:
        load.start()

    loads[0].wait()
    here = lax.broadcasted_iota(jnp.int32, (512, 256), 0) + d * 512
    hot = jnp.concatenate(
        [(here == idx_v[s : s + 1, :]).astype(F32).astype(BF16) for s in range(2)], axis=1
    )
    loads[1].wait()
    pick[...] = dot(hot, tab_v[...], TN).astype(BF16).reshape(ND, 16, 128)
    parts[chunk] = pick[chunk]

    pl.semaphore_wait(barrier, len(greeted))

    for o in YZ_FAR:
        send(
            pick.at[zs[o[1]] * NY + ys[o[0]]], parts.at[chunk], sent.at[0], a_recv, at_yz(o)
        )

    loads[2].wait()
    first = (g == 0).astype(F32)
    aims_v[...] = dot(hot, tgt_v[...], TN) * first
    loads[3].wait()
    high, low = split(jnp.square(cen_v[...].astype(F32)))
    ones = jnp.ones((8, 1024), BF16)
    cnorm = (dot(ones, high, NT) + dot(ones, low, NT))[0:1, :]
    loads[4].wait()
    cf_high[...], cf_low[...] = split(cf_v[...])

    wait_bytes(parts.at[pl.ds(0, ND - 1)], a_recv)
    own = jnp.sum(parts[...].astype(F32), axis=0).astype(BF16)
    lane = pl.ds(pl.multiple_of(feat * 128, 128), 128)
    rows[pl.ds(pl.multiple_of(chunk * 16, 16), 16), lane] = own

    def block(zz):
        return rows.at[pl.ds(pl.multiple_of((zz * NY + y) * 16, 16), 16), lane]

    for k in Z_FAR:
        send(block(z), block(z), sent.at[1], az_recv.at[k], at_yz((0, k)))

    def pass_on(k):
        there = block(zs[(NZ - k) % NZ])
        for o in XY_FAR:
            send(there, there, sent.at[2], axy_recv.at[k], at_xy(o))

    pass_on(0)
    for k in Z_NEAR:
        wait_bytes(block(z), az_recv.at[k])
        pass_on(k)

    half = pl.ds(pl.multiple_of(c * 512, 512), 512)
    for k in [0] + Z_NEAR:
        wait_bytes(parts.at[pl.ds(0, NP - 1)], axy_recv.at[k])
        strip = rows.at[pl.ds(pl.multiple_of(zs[(NZ - k) % NZ] * 64, 64), 64), half]
        send(strip, strip, sent.at[3], ac_recv, sibling)
    wait_bytes(rows.at[:, pl.ds(0, 512)], ac_recv)

    all_rows = rows[...]
    rnorm = jnp.sum(jnp.square(all_rows.astype(F32)), axis=1, keepdims=True)
    cross = dot(all_rows, cen_v[...], NT)
    dist = jnp.sqrt(jnp.maximum(rnorm + cnorm - 2.0 * cross, 0.0))
    w_high[...], w_low[...] = split(jnp.exp((radius - dist) / SPREAD) * scale)

    ones = jnp.ones((8, 512), BF16)
    mass = dot(ones, w_high[...], NT) + dot(ones, w_low[...], NT)
    mass = jnp.concatenate(
        [mass[0:1, n * 128 : n * 128 + 128] for n in range(4)] + [jnp.zeros((4, 128), F32)], axis=0
    )

    def partials(h, dst):
        r0 = pl.ds(pl.multiple_of(h * 128, 128), 128)
        r1 = pl.ds(pl.multiple_of(h * 128 + 256, 128), 128)
        h0, l0, h1, l1 = w_high[r0, :], w_low[r0, :], w_high[r1, :], w_low[r1, :]
        ch, cl = cf_high[...], cf_low[...]
        gh, gl = w_high[0:256, :], w_low[0:256, :]
        s0 = dot(h0, ch) + (dot(h0, cl) + dot(l0, ch)) - aims_v[r0, :]
        s1 = dot(h1, ch) + (dot(h1, cl) + dot(l1, ch)) - aims_v[r1, :]
        gram = dot(h1, gh, NT) + (dot(h1, gl, NT) + dot(l1, gh, NT))
        for n, part in enumerate((s0, s1, gram)):
            for m in range(2):
                at = n * 16 + m * 8
                dst[:, at : at + 8, :] = part[:, m * 128 : m * 128 + 128].reshape(NP, 8, 128)
        dst[:, 48:56, :] = jnp.broadcast_to(mass[None], (NP, 8, 128))

    partials(1 - c, core_send)
    core_copy = send(core_send, core_recv, cc_send, cc_recv, sibling)
    partials(c, xy_send)
    core_copy.wait()
    xy_send[...] = xy_send[...] + core_recv[...]

    for o in XY_FAR:
        send(
            xy_send.at[xs[o[0]] * NY + ys[o[1]]], xy_recv.at[p], sent.at[4], cxy_recv, at_xy(o)
        )
    xy_recv[p] = xy_send[p]
    wt_high[...] = w_high[...].T
    wt_low[...] = w_low[...].T
    wait_bytes(xy_recv.at[pl.ds(0, NP - 1)], cxy_recv)
    z_buf[z] = jnp.sum(xy_recv[...], axis=0)

    for k in Z_FAR:
        send(z_buf.at[z], z_buf.at[z], sent.at[5], cz_recv, at_yz((0, k)))
    wait_bytes(z_buf.at[pl.ds(0, NZ - 1)], cz_recv)
    total = jnp.sum(z_buf[...], axis=0)
    whole[c, p] = total[0:48]

    for o in XY_FAR:
        send(whole.at[c, p], whole.at[c, p], sent.at[6], gxy_recv, at_xy(o))
    mass_out[...] = total[48:56]
    wait_bytes(whole.at[0, pl.ds(0, NP - 1)], gxy_recv)
    send(whole.at[c], whole.at[c], sent.at[7], gc_recv, sibling)
    wait_bytes(whole.at[0], gc_recv)

    wait_bytes(parts.at[pl.ds(0, ND - 1)], sent.at[0])
    wait_bytes(parts.at[pl.ds(0, NZ - 1)], sent.at[1])
    wait_bytes(rows.at[pl.ds(0, 480), pl.ds(0, 512)], sent.at[2])
    wait_bytes(rows.at[:, pl.ds(0, 512)], sent.at[3])
    wait_bytes(xy_recv.at[pl.ds(0, NP - 1)], sent.at[4])
    wait_bytes(z_buf.at[pl.ds(0, NZ - 1)], sent.at[5])
    wait_bytes(whole.at[0, pl.ds(0, NP - 1)], sent.at[6])
    wait_bytes(whole.at[0], sent.at[7])


def update(whole, mass, wt_high, wt_low, coef, coef_out, resid_out):
    def piece(n):
        halves = [
            jnp.concatenate(
                [whole[h, :, n * 16 + m * 8 : n * 16 + m * 8 + 8, :].reshape(128, 128) for m in range(2)],
                axis=1,
            )
            for h in range(2)
        ]
        return jnp.concatenate(halves, axis=0)

    def column(s):
        tiles = [jnp.broadcast_to(mass[2 * s + m : 2 * s + m + 1, :], (128, 128)).T for m in range(2)]
        tall = jnp.concatenate(tiles, axis=0)
        return jnp.concatenate([tall, tall], axis=1)

    def project(resid, m):
        along = jnp.sum(m * resid, axis=0, keepdims=True) / jnp.sum(m * m, axis=0, keepdims=True)
        return resid - m * along

    def grad(s, proj):
        ph, pw = split(proj)
        th, tl = wt_high[:, s * 256 : s * 256 + 256], wt_low[:, s * 256 : s * 256 + 256]
        return dot(th, ph) + (dot(th, pw) + dot(tl, ph))

    m0, m1 = column(0), column(1)
    resid0 = piece(0)
    resid_out[0] = resid0
    proj0 = project(resid0, m0)
    resid1 = piece(1) - RATE * dot(piece(2), proj0, precision=HI)
    resid_out[1] = resid1
    step0 = grad(0, proj0)
    proj1 = project(resid1, m1)
    coef_out[...] = coef[...] - RATE * (step0 + grad(1, proj1))


def body(table, target_table, centres, coefficients, batch_index):
    dma = pltpu.SemaphoreType.DMA
    vmem = pl.BlockSpec(memory_space=pltpu.VMEM)
    sums = pl.pallas_call(
        exchange,
        name="exchange",
        out_shape=(
            jax.ShapeDtypeStruct((2, NP, 48, 128), F32),
            jax.ShapeDtypeStruct((8, 128), F32),
            jax.ShapeDtypeStruct((512, 512), BF16),
            jax.ShapeDtypeStruct((512, 512), BF16),
        ),
        in_specs=[pl.BlockSpec(memory_space=pltpu.HBM)] * 5,
        out_specs=(vmem,) * 4,
        scratch_shapes=[
            pltpu.VMEM((512, 128), BF16),
            pltpu.VMEM((512, 256), BF16),
            pltpu.VMEM((512, 1024), BF16),
            pltpu.VMEM((512, 256), F32),
            pltpu.VMEM((2, 256), jnp.int32),
            pltpu.VMEM((512, 256), F32),
            pltpu.VMEM((512, 256), BF16),
            pltpu.VMEM((512, 256), BF16),
            pltpu.VMEM((ND, 16, 128), BF16),
            pltpu.VMEM((ND, 16, 128), BF16),
            pltpu.VMEM((512, 1024), BF16),
            pltpu.VMEM((512, 512), BF16),
            pltpu.VMEM((512, 512), BF16),
            pltpu.VMEM((NP, 56, 128), F32),
            pltpu.VMEM((NP, 56, 128), F32),
            pltpu.VMEM((NP, 56, 128), F32),
            pltpu.VMEM((NP, 56, 128), F32),
            pltpu.VMEM((NZ, 56, 128), F32),
            dma((5,)), dma((8,)), dma, dma((NZ,)), dma((NZ,)), dma,
            dma, dma, dma, dma, dma, dma,
        ],
        compiler_params=pltpu.CompilerParams(
            collective_id=0, has_side_effects=True, vmem_limit_bytes=40 * 2**20
        ),
    )(table, target_table, centres, coefficients, batch_index)
    return pl.pallas_call(
        update,
        name="update",
        out_shape=(
            jax.ShapeDtypeStruct((512, 256), F32),
            jax.ShapeDtypeStruct((2, 256, 256), F32),
        ),
        in_specs=[vmem] * 5,
        out_specs=(vmem, vmem),
        compiler_params=pltpu.CompilerParams(vmem_limit_bytes=24 * 2**20),
    )(*sums, coefficients)


def solution(mesh):
    in_specs = (
        P("dev", None),
        P("dev", None),
        P(("grp", "dev"), None),
        P(("grp", "dev"), None),
        P(),
    )
    out_specs = (P(("grp", "dev"), None), P())
    return jax.shard_map(body, mesh=mesh, in_specs=in_specs, out_specs=out_specs, check_vma=False)
```

```python
import math

import jax
import jax.numpy as jnp
from jax import lax
from jax.experimental import pallas as pl
from jax.experimental.pallas import tpu as pltpu
from jax.sharding import PartitionSpec as P

MESH = pl.DeviceIdType.MESH
SPREAD = 2.0
RATE = 2.0
NX, NC, NY, NZ = 4, 2, 4, 8
NP = NX * NY
ND = NY * NZ
F32 = jnp.float32
BF16 = jnp.bfloat16
HI = lax.Precision.HIGHEST
NN = (((1,), (0,)), ((), ()))
NT = (((1,), (1,)), ((), ()))
TN = (((0,), (0,)), ((), ()))


def hops(k, n):
    return min(k, n - k)


Z_FAR = sorted(range(1, NZ), key=lambda k: -hops(k, NZ))
Z_NEAR = Z_FAR[::-1]
XY_FAR = sorted(
    [(i, j) for i in range(NX) for j in range(NY) if i or j],
    key=lambda o: -hops(o[0], NX) - hops(o[1], NY),
)
YZ_FAR = sorted(
    [(j, k) for j in range(NY) for k in range(NZ) if j or k],
    key=lambda o: -hops(o[0], NY) - hops(o[1], NZ),
)


def dot(a, b, dims=NN, precision=None):
    return lax.dot_general(a, b, dims, precision=precision, preferred_element_type=F32)


def split(a):
    high = a.astype(BF16)
    return high, (a - high.astype(F32)).astype(BF16)


def exchange(
    table, target, centres, coef, index,
    whole, mass_out, wt_high, wt_low,
    tab_v, tgt_v, cen_v, cf_v, idx_v, aims_v, cf_high, cf_low,
    pick, parts, rows,
    w_high, w_low, core_send, core_recv, xy_send, xy_recv, z_buf,
    load_sem, sent, a_recv, az_recv, axy_recv, ac_recv,
    cc_send, cc_recv, cxy_recv, cz_recv, gxy_recv, gc_recv,
):
    g = lax.axis_index("grp")
    d = lax.axis_index("dev")
    x, c = g // 2, g % 2
    y, z = d // NZ, d % NZ
    p = x * NY + y
    feat = c * NX + x
    chunk = z * NY + y
    radius = math.sqrt(2.0 * 1024)
    scale = 1.0 / math.sqrt(131072)

    xs = [lax.rem(x + k, NX) for k in range(NX)]
    ys = [lax.rem(y + k, NY) for k in range(NY)]
    zs = [lax.rem(z + k, NZ) for k in range(NZ)]
    grps = [v * 2 + c for v in xs]
    bases = [v * NZ for v in ys]

    def at_xy(o):
        return {"grp": grps[o[0]], "dev": bases[o[1]] + z}

    def at_yz(o):
        return {"grp": g, "dev": bases[o[0]] + zs[o[1]]}

    sibling = {"grp": x * 2 + 1 - c, "dev": d}

    def send(src, dst, send_sem, recv_sem, to):
        copy = pltpu.make_async_remote_copy(
            src_ref=src, dst_ref=dst, send_sem=send_sem, recv_sem=recv_sem,
            device_id=to, device_id_type=MESH,
        )
        copy.start()
        return copy

    def wait_bytes(ref, sem):
        pltpu.make_async_copy(ref, ref, sem).wait()

    barrier = pltpu.get_barrier_semaphore()
    greeted = [at_yz(o) for o in YZ_FAR] + [at_xy(o) for o in XY_FAR if o[0]] + [sibling]
    for to in greeted:
        pl.semaphore_signal(barrier, inc=1, device_id=to, device_id_type=MESH)

    loads = [
        pltpu.make_async_copy(index, idx_v, load_sem.at[0]),
        pltpu.make_async_copy(
            table.at[:, pl.ds(pl.multiple_of(feat * 128, 128), 128)], tab_v, load_sem.at[1]
        ),
        pltpu.make_async_copy(target, tgt_v, load_sem.at[2]),
        pltpu.make_async_copy(centres, cen_v, load_sem.at[3]),
        pltpu.make_async_copy(coef, cf_v, load_sem.at[4]),
    ]
    for load in loads:
        load.start()

    loads[0].wait()
    here = lax.broadcasted_iota(jnp.int32, (512, 256), 0) + d * 512
    hot = jnp.concatenate(
        [(here == idx_v[s : s + 1, :]).astype(F32).astype(BF16) for s in range(2)], axis=1
    )
    loads[1].wait()
    pick[...] = dot(hot, tab_v[...], TN).astype(BF16).reshape(ND, 16, 128)
    parts[chunk] = pick[chunk]

    pl.semaphore_wait(barrier, len(greeted))

    for o in YZ_FAR:
        send(
            pick.at[zs[o[1]] * NY + ys[o[0]]], parts.at[chunk], sent.at[0], a_recv, at_yz(o)
        )

    loads[2].wait()
    first = (g == 0).astype(F32)
    aims_v[...] = dot(hot, tgt_v[...], TN) * first
    loads[3].wait()
    high, low = split(jnp.square(cen_v[...].astype(F32)))
    ones = jnp.ones((8, 1024), BF16)
    cnorm = (dot(ones, high, NT) + dot(ones, low, NT))[0:1, :]
    loads[4].wait()
    cf_high[...], cf_low[...] = split(cf_v[...])

    wait_bytes(parts.at[pl.ds(0, ND - 1)], a_recv)
    own = jnp.sum(parts[...].astype(F32), axis=0).astype(BF16)
    lane = pl.ds(pl.multiple_of(feat * 128, 128), 128)
    rows[pl.ds(pl.multiple_of(chunk * 16, 16), 16), lane] = own

    def block(zz):
        return rows.at[pl.ds(pl.multiple_of((zz * NY + y) * 16, 16), 16), lane]

    for k in Z_FAR:
        send(block(z), block(z), sent.at[1], az_recv.at[k], at_yz((0, k)))

    def pass_on(k):
        there = block(zs[(NZ - k) % NZ])
        for o in XY_FAR:
            send(there, there, sent.at[2], axy_recv.at[k], at_xy(o))

    pass_on(0)
    for k in Z_NEAR:
        wait_bytes(block(z), az_recv.at[k])
        pass_on(k)

    half = pl.ds(pl.multiple_of(c * 512, 512), 512)
    for k in [0] + Z_NEAR:
        wait_bytes(parts.at[pl.ds(0, NP - 1)], axy_recv.at[k])
        strip = rows.at[pl.ds(pl.multiple_of(zs[(NZ - k) % NZ] * 64, 64), 64), half]
        send(strip, strip, sent.at[3], ac_recv, sibling)
    wait_bytes(rows.at[:, pl.ds(0, 512)], ac_recv)

    all_rows = rows[...]
    rnorm = jnp.sum(jnp.square(all_rows.astype(F32)), axis=1, keepdims=True)
    cross = dot(all_rows, cen_v[...], NT)
    dist = jnp.sqrt(jnp.maximum(rnorm + cnorm - 2.0 * cross, 0.0))
    w_high[...], w_low[...] = split(jnp.exp((radius - dist) / SPREAD) * scale)

    ones = jnp.ones((8, 512), BF16)
    mass = dot(ones, w_high[...], NT) + dot(ones, w_low[...], NT)
    mass = jnp.concatenate(
        [mass[0:1, n * 128 : n * 128 + 128] for n in range(4)] + [jnp.zeros((4, 128), F32)], axis=0
    )

    def partials(h, dst):
        r0 = pl.ds(pl.multiple_of(h * 128, 128), 128)
        r1 = pl.ds(pl.multiple_of(h * 128 + 256, 128), 128)
        h0, l0, h1, l1 = w_high[r0, :], w_low[r0, :], w_high[r1, :], w_low[r1, :]
        ch, cl = cf_high[...], cf_low[...]
        gh, gl = w_high[0:256, :], w_low[0:256, :]
        s0 = dot(h0, ch) + (dot(h0, cl) + dot(l0, ch)) - aims_v[r0, :]
        s1 = dot(h1, ch) + (dot(h1, cl) + dot(l1, ch)) - aims_v[r1, :]
        gram = dot(h1, gh, NT) + (dot(h1, gl, NT) + dot(l1, gh, NT))
        for n, part in enumerate((s0, s1, gram)):
            for m in range(2):
                at = n * 16 + m * 8
                dst[:, at : at + 8, :] = part[:, m * 128 : m * 128 + 128].reshape(NP, 8, 128)
        dst[:, 48:56, :] = jnp.broadcast_to(mass[None], (NP, 8, 128))

    partials(1 - c, core_send)
    core_copy = send(core_send, core_recv, cc_send, cc_recv, sibling)
    partials(c, xy_send)
    core_copy.wait()
    xy_send[...] = xy_send[...] + core_recv[...]

    for o in XY_FAR:
        send(
            xy_send.at[xs[o[0]] * NY + ys[o[1]]], xy_recv.at[p], sent.at[4], cxy_recv, at_xy(o)
        )
    xy_recv[p] = xy_send[p]
    wt_high[...] = w_high[...].T
    wt_low[...] = w_low[...].T
    wait_bytes(xy_recv.at[pl.ds(0, NP - 1)], cxy_recv)
    z_buf[z] = jnp.sum(xy_recv[...], axis=0)

    for k in Z_FAR:
        send(z_buf.at[z], z_buf.at[z], sent.at[5], cz_recv, at_yz((0, k)))
    wait_bytes(z_buf.at[pl.ds(0, NZ - 1)], cz_recv)
    total = jnp.sum(z_buf[...], axis=0)
    whole[c, p] = total[0:48]

    for o in XY_FAR:
        send(whole.at[c, p], whole.at[c, p], sent.at[6], gxy_recv, at_xy(o))
    mass_out[...] = total[48:56]
    wait_bytes(whole.at[0, pl.ds(0, NP - 1)], gxy_recv)
    send(whole.at[c], whole.at[c], sent.at[7], gc_recv, sibling)
    wait_bytes(whole.at[0], gc_recv)

    wait_bytes(parts.at[pl.ds(0, ND - 1)], sent.at[0])
    wait_bytes(parts.at[pl.ds(0, NZ - 1)], sent.at[1])
    wait_bytes(rows.at[pl.ds(0, 480), pl.ds(0, 512)], sent.at[2])
    wait_bytes(rows.at[:, pl.ds(0, 512)], sent.at[3])
    wait_bytes(xy_recv.at[pl.ds(0, NP - 1)], sent.at[4])
    wait_bytes(z_buf.at[pl.ds(0, NZ - 1)], sent.at[5])
    wait_bytes(whole.at[0, pl.ds(0, NP - 1)], sent.at[6])
    wait_bytes(whole.at[0], sent.at[7])


def update(whole, mass, wt_high, wt_low, coef, coef_out, resid_out):
    def piece(n):
        halves = [
            jnp.concatenate(
                [whole[h, :, n * 16 + m * 8 : n * 16 + m * 8 + 8, :].reshape(128, 128) for m in range(2)],
                axis=1,
            )
            for h in range(2)
        ]
        return jnp.concatenate(halves, axis=0)

    def column(s):
        tiles = [jnp.broadcast_to(mass[2 * s + m : 2 * s + m + 1, :], (128, 128)).T for m in range(2)]
        tall = jnp.concatenate(tiles, axis=0)
        return jnp.concatenate([tall, tall], axis=1)

    def project(resid, m):
        along = jnp.sum(m * resid, axis=0, keepdims=True) / jnp.sum(m * m, axis=0, keepdims=True)
        return resid - m * along

    def grad(s, proj):
        ph, pw = split(proj)
        th, tl = wt_high[:, s * 256 : s * 256 + 256], wt_low[:, s * 256 : s * 256 + 256]
        return dot(th, ph) + (dot(th, pw) + dot(tl, ph))

    m0, m1 = column(0), column(1)
    resid0 = piece(0)
    resid_out[0] = resid0
    proj0 = project(resid0, m0)
    resid1 = piece(1) - RATE * dot(piece(2), proj0, precision=HI)
    resid_out[1] = resid1
    step0 = grad(0, proj0)
    proj1 = project(resid1, m1)
    coef_out[...] = coef[...] - RATE * (step0 + grad(1, proj1))


def body(table, target_table, centres, coefficients, batch_index):
    dma = pltpu.SemaphoreType.DMA
    vmem = pl.BlockSpec(memory_space=pltpu.VMEM)
    sums = pl.pallas_call(
        exchange,
        name="exchange",
        out_shape=(
            jax.ShapeDtypeStruct((2, NP, 48, 128), F32),
            jax.ShapeDtypeStruct((8, 128), F32),
            jax.ShapeDtypeStruct((512, 512), BF16),
            jax.ShapeDtypeStruct((512, 512), BF16),
        ),
        in_specs=[pl.BlockSpec(memory_space=pltpu.HBM)] * 5,
        out_specs=(vmem,) * 4,
        scratch_shapes=[
            pltpu.VMEM((512, 128), BF16),
            pltpu.VMEM((512, 256), BF16),
            pltpu.VMEM((512, 1024), BF16),
            pltpu.VMEM((512, 256), F32),
            pltpu.VMEM((2, 256), jnp.int32),
            pltpu.VMEM((512, 256), F32),
            pltpu.VMEM((512, 256), BF16),
            pltpu.VMEM((512, 256), BF16),
            pltpu.VMEM((ND, 16, 128), BF16),
            pltpu.VMEM((ND, 16, 128), BF16),
            pltpu.VMEM((512, 1024), BF16),
            pltpu.VMEM((512, 512), BF16),
            pltpu.VMEM((512, 512), BF16),
            pltpu.VMEM((NP, 56, 128), F32),
            pltpu.VMEM((NP, 56, 128), F32),
            pltpu.VMEM((NP, 56, 128), F32),
            pltpu.VMEM((NP, 56, 128), F32),
            pltpu.VMEM((NZ, 56, 128), F32),
            dma((5,)), dma((8,)), dma, dma((NZ,)), dma((NZ,)), dma,
            dma, dma, dma, dma, dma, dma,
        ],
        compiler_params=pltpu.CompilerParams(
            collective_id=0, has_side_effects=True, vmem_limit_bytes=40 * 2**20
        ),
    )(*[
        pltpu.with_memory_space_constraint(a, pltpu.HBM)
        for a in (table, target_table, centres, coefficients, batch_index)
    ])
    return pl.pallas_call(
        update,
        name="update",
        out_shape=(
            jax.ShapeDtypeStruct((512, 256), F32),
            jax.ShapeDtypeStruct((2, 256, 256), F32),
        ),
        in_specs=[vmem] * 5,
        out_specs=(vmem, vmem),
        compiler_params=pltpu.CompilerParams(vmem_limit_bytes=24 * 2**20),
    )(*sums, coefficients)


def solution(mesh):
    in_specs = (
        P("dev", None),
        P("dev", None),
        P(("grp", "dev"), None),
        P(("grp", "dev"), None),
        P(),
    )
    out_specs = (P(("grp", "dev"), None), P())
    return jax.shard_map(body, mesh=mesh, in_specs=in_specs, out_specs=out_specs, check_vma=False)
```

```python
import math

import jax
import jax.numpy as jnp
from jax import lax
from jax.experimental import pallas as pl
from jax.experimental.pallas import tpu as pltpu
from jax.sharding import PartitionSpec as P

MESH = pl.DeviceIdType.MESH
SPREAD = 2.0
RATE = 2.0
NX, NC, NY, NZ = 4, 2, 4, 8
NP = NX * NY
ND = NY * NZ
F32 = jnp.float32
BF16 = jnp.bfloat16
HI = lax.Precision.HIGHEST
NN = (((1,), (0,)), ((), ()))
NT = (((1,), (1,)), ((), ()))
TN = (((0,), (0,)), ((), ()))


def hops(k, n):
    return min(k, n - k)


Z_FAR = sorted(range(1, NZ), key=lambda k: -hops(k, NZ))
Z_NEAR = Z_FAR[::-1]
XY_FAR = sorted(
    [(i, j) for i in range(NX) for j in range(NY) if i or j],
    key=lambda o: -hops(o[0], NX) - hops(o[1], NY),
)
YZ_FAR = sorted(
    [(j, k) for j in range(NY) for k in range(NZ) if j or k],
    key=lambda o: -hops(o[0], NY) - hops(o[1], NZ),
)


def dot(a, b, dims=NN, precision=None):
    return lax.dot_general(a, b, dims, precision=precision, preferred_element_type=F32)


def split(a):
    high = a.astype(BF16)
    return high, (a - high.astype(F32)).astype(BF16)


SLOTS = [0, 1, 7, 2, 6, 3, 5, 4]
GROUPS = [(0, 3), (3, 7), (7, 8)]
SHARE = (16, 24, 16)


def pieces_to_whole(whole):
    halves = [
        jnp.concatenate([whole[h, :, m * 8 : m * 8 + 8, :].reshape(128, 128) for m in range(2)], axis=1)
        for h in range(2)
    ]
    return jnp.concatenate(halves, axis=0)


def column(mass, s):
    tiles = [jnp.broadcast_to(mass[2 * s + m : 2 * s + m + 1, :], (128, 128)).T for m in range(2)]
    tall = jnp.concatenate(tiles, axis=0)
    return jnp.concatenate([tall, tall], axis=1)


def project(resid, m):
    along = jnp.sum(m * resid, axis=0, keepdims=True) / jnp.sum(m * m, axis=0, keepdims=True)
    return resid - m * along


def grad(high, low, proj):
    ph, pw = split(proj)
    return dot(high, ph) + (dot(high, pw) + dot(low, ph))


def exchange(
    table, target, centres, coef, index,
    whole2, turn_out, mass_out, wt_high, wt_low, coef_half, resid0_out,
    tab_v, tgt_v, cen_v, cf_v, idx_v, aims_v, cf_high, cf_low,
    pick, parts, rows, w_high, w_low, wt0_high, wt0_low,
    core_send0, core_send1, core_send2, core_recv0, core_recv1, core_recv2,
    xy_send0, xy_send1, xy_send2, xy_recv0, xy_recv1, xy_recv2,
    z_buf0, z_buf1, z_buf2, whole0, whole1,
    load_sem, a_sent, a_recv, az_recv, axy_recv, ac_recv,
    c_sent, cc_recv, cxy_recv, cz_recv, gxy_recv, gc_recv,
):
    core_send, core_recv = (core_send0, core_send1, core_send2), (core_recv0, core_recv1, core_recv2)
    xy_send, xy_recv = (xy_send0, xy_send1, xy_send2), (xy_recv0, xy_recv1, xy_recv2)
    z_buf, whole = (z_buf0, z_buf1, z_buf2), (whole0, whole1, whole2)
    g = lax.axis_index("grp")
    d = lax.axis_index("dev")
    x, c = g // 2, g % 2
    y, z = d // NZ, d % NZ
    p = x * NY + y
    feat = c * NX + x
    chunk = z * NY + y
    radius = math.sqrt(2.0 * 1024)
    scale = 1.0 / math.sqrt(131072)

    xs = [lax.rem(x + k, NX) for k in range(NX)]
    ys = [lax.rem(y + k, NY) for k in range(NY)]
    zs = [lax.rem(z + k, NZ) for k in range(NZ)]
    grps = [v * 2 + c for v in xs]
    bases = [v * NZ for v in ys]

    def at_xy(o):
        return {"grp": grps[o[0]], "dev": bases[o[1]] + z}

    def at_yz(o):
        return {"grp": g, "dev": bases[o[0]] + zs[o[1]]}

    sibling = {"grp": x * 2 + 1 - c, "dev": d}

    def send(src, dst, send_sem, recv_sem, to):
        copy = pltpu.make_async_remote_copy(
            src_ref=src, dst_ref=dst, send_sem=send_sem, recv_sem=recv_sem,
            device_id=to, device_id_type=MESH,
        )
        copy.start()
        return copy

    def wait_bytes(ref, sem):
        pltpu.make_async_copy(ref, ref, sem).wait()

    barrier = pltpu.get_barrier_semaphore()
    greeted = [at_yz(o) for o in YZ_FAR] + [at_xy(o) for o in XY_FAR if o[0]] + [sibling]
    for to in greeted:
        pl.semaphore_signal(barrier, inc=1, device_id=to, device_id_type=MESH)

    loads = [
        pltpu.make_async_copy(index, idx_v, load_sem.at[0]),
        pltpu.make_async_copy(
            table.at[:, pl.ds(pl.multiple_of(feat * 128, 128), 128)], tab_v, load_sem.at[1]
        ),
        pltpu.make_async_copy(target, tgt_v, load_sem.at[2]),
        pltpu.make_async_copy(centres, cen_v, load_sem.at[3]),
        pltpu.make_async_copy(coef, cf_v, load_sem.at[4]),
    ]
    for load in loads:
        load.start()

    loads[0].wait()
    here = lax.broadcasted_iota(jnp.int32, (512, 256), 0) + d * 512
    hot = jnp.concatenate(
        [(here == idx_v[s : s + 1, :]).astype(F32).astype(BF16) for s in range(2)], axis=1
    )
    loads[1].wait()
    pick[...] = dot(hot, tab_v[...], TN).astype(BF16).reshape(ND, 16, 128)
    parts[chunk] = pick[chunk]

    pl.semaphore_wait(barrier, len(greeted))

    for o in YZ_FAR:
        send(
            pick.at[zs[o[1]] * NY + ys[o[0]]], parts.at[chunk], a_sent.at[0], a_recv, at_yz(o)
        )

    loads[2].wait()
    first = (g == 0).astype(F32)
    aims_v[...] = dot(hot, tgt_v[...], TN) * first

    wait_bytes(parts.at[pl.ds(0, ND - 1)], a_recv)
    own = jnp.sum(parts[...].astype(F32), axis=0).astype(BF16)
    lane = pl.ds(pl.multiple_of(feat * 128, 128), 128)
    rows[0, y, :, lane] = own

    mine = rows.at[0, y, :, lane]
    for k in Z_FAR:
        there = rows.at[SLOTS.index(NZ - k), y, :, lane]
        send(mine, there, a_sent.at[1], az_recv.at[NZ - k], at_yz((0, k)))
    for n, (b, e) in enumerate(GROUPS):
        for r in SLOTS[b:e]:
            if r:
                wait_bytes(parts.at[0], az_recv.at[r])
        group = rows.at[pl.ds(b, e - b), y, :, lane]
        for o in XY_FAR:
            send(group, group, a_sent.at[2], axy_recv.at[n], at_xy(o))

    loads[3].wait()
    high, low = split(jnp.square(cen_v[...].astype(F32)))
    ones = jnp.ones((8, 1024), BF16)
    cnorm = (dot(ones, high, NT) + dot(ones, low, NT))[0:1, :]
    loads[4].wait()
    cf_high[...], cf_low[...] = split(cf_v[...])

    half = pl.ds(pl.multiple_of(c * 512, 512), 512)
    for n, (b, e) in enumerate(GROUPS):
        wait_bytes(rows.at[pl.ds(0, e - b), pl.ds(0, 3), :, pl.ds(0, 640)], axy_recv.at[n])
        strip = rows.at[pl.ds(b, e - b), :, :, half]
        send(strip, strip, a_sent.at[3], ac_recv.at[n], sibling)

    for n, (b, e) in enumerate(GROUPS):
        wait_bytes(rows.at[pl.ds(0, e - b), :, :, pl.ds(0, 512)], ac_recv.at[n])
        some = rows[b:e].reshape((e - b) * 64, 1024)
        rnorm = jnp.sum(jnp.square(some.astype(F32)), axis=1, keepdims=True)
        cross = dot(some, cen_v[...], NT)
        dist = jnp.sqrt(jnp.maximum(rnorm + cnorm - 2.0 * cross, 0.0))
        high, low = split(jnp.exp((radius - dist) / SPREAD) * scale)
        for r in range(b, e):
            at = pl.ds(pl.multiple_of(zs[SLOTS[r]] * 64, 64), 64)
            w_high[at, :] = high[(r - b) * 64 : (r - b) * 64 + 64]
            w_low[at, :] = low[(r - b) * 64 : (r - b) * 64 + 64]

    def terms(n, h, dst):
        s = n // 2
        at = pl.ds(pl.multiple_of(h * 128 + (0, 256, 256)[n], 128), 128)
        high, low = w_high[at, :], w_low[at, :]
        if n == 1:
            gh, gl = w_high[0:256, :], w_low[0:256, :]
            part = dot(high, gh, NT) + (dot(high, gl, NT) + dot(low, gh, NT))
        else:
            ch, cl = cf_high[...], cf_low[...]
            part = dot(high, ch) + (dot(high, cl) + dot(low, ch)) - aims_v[at, :]
        for m in range(2):
            dst[:, m * 8 : m * 8 + 8, :] = part[:, m * 128 : m * 128 + 128].reshape(NP, 8, 128)

    for n in range(3):
        terms(n, 1 - c, core_send[n])
        if n == 1:
            ones = jnp.ones((8, 512), BF16)
            mass = dot(ones, w_high[...], NT) + dot(ones, w_low[...], NT)
            mass = jnp.concatenate(
                [mass[0:1, m * 128 : m * 128 + 128] for m in range(4)] + [jnp.zeros((4, 128), F32)],
                axis=0,
            )
            mass = jnp.broadcast_to(mass[None], (NP, 8, 128))
            core_send[1][:, 16:24, :] = mass
            xy_send[1][:, 16:24, :] = mass
        send(core_send[n], core_recv[n], c_sent.at[n], cc_recv.at[n], sibling)
    for n in range(3):
        terms(n, c, xy_send[n])
        wait_bytes(core_recv[n], cc_recv.at[n])
        xy_send[n][...] = xy_send[n][...] + core_recv[n][...]
        for o in XY_FAR:
            send(
                xy_send[n].at[xs[o[0]] * NY + ys[o[1]]], xy_recv[n].at[p],
                c_sent.at[3 + n], cxy_recv.at[n], at_xy(o),
            )
        xy_recv[n][p] = xy_send[n][p]

    wt0_high[...] = w_high[0:256, :].T
    wt0_low[...] = w_low[0:256, :].T
    wt_high[...] = w_high[256:512, :].T
    wt_low[...] = w_low[256:512, :].T

    for n in range(3):
        wait_bytes(xy_recv[n].at[pl.ds(0, NP - 1)], cxy_recv.at[n])
        z_buf[n][z] = jnp.sum(xy_recv[n][...], axis=0)
        for k in Z_FAR:
            send(z_buf[n].at[z], z_buf[n].at[z], c_sent.at[6 + n], cz_recv.at[n], at_yz((0, k)))
    for n in range(3):
        wait_bytes(z_buf[n].at[pl.ds(0, NZ - 1)], cz_recv.at[n])
        total = jnp.sum(z_buf[n][...], axis=0)
        whole[n][c, p] = total[0:16]
        for o in XY_FAR:
            send(whole[n].at[c, p], whole[n].at[c, p], c_sent.at[9 + n], gxy_recv.at[n], at_xy(o))
        if n == 1:
            mass = total[16:24]
            mass_out[...] = mass
            m0 = column(mass, 0)
    for n in range(3):
        wait_bytes(whole[n].at[0, pl.ds(0, NP - 1)], gxy_recv.at[n])
        send(whole[n].at[c], whole[n].at[c], c_sent.at[12 + n], gc_recv.at[n], sibling)

    wait_bytes(whole[0].at[0], gc_recv.at[0])
    resid0 = pieces_to_whole(whole0)
    resid0_out[...] = resid0
    proj0 = project(resid0, m0)
    wait_bytes(whole[1].at[0], gc_recv.at[1])
    turn_out[...] = RATE * dot(pieces_to_whole(whole1), proj0, precision=HI)
    coef_half[...] = cf_v[...] - RATE * grad(wt0_high[...], wt0_low[...], proj0)
    wait_bytes(whole[2].at[0], gc_recv.at[2])

    wait_bytes(parts.at[pl.ds(0, ND - 1)], a_sent.at[0])
    wait_bytes(parts.at[pl.ds(0, NZ - 1)], a_sent.at[1])
    wait_bytes(rows.at[:, pl.ds(0, 3), :, pl.ds(0, 640)], a_sent.at[2])
    wait_bytes(rows.at[:, :, :, pl.ds(0, 512)], a_sent.at[3])
    for n in range(3):
        wait_bytes(core_recv[n], c_sent.at[n])
        wait_bytes(xy_recv[n].at[pl.ds(0, NP - 1)], c_sent.at[3 + n])
        wait_bytes(z_buf[n].at[pl.ds(0, NZ - 1)], c_sent.at[6 + n])
        wait_bytes(whole[n].at[0, pl.ds(0, NP - 1)], c_sent.at[9 + n])
        wait_bytes(whole[n].at[0], c_sent.at[12 + n])


def update(whole2, turn, mass, wt_high, wt_low, coef_half, resid0, coef_out, resid_out):
    resid1 = pieces_to_whole(whole2) - turn[...]
    resid_out[0] = resid0[...]
    resid_out[1] = resid1
    proj1 = project(resid1, column(mass[...], 1))
    coef_out[...] = coef_half[...] - RATE * grad(wt_high[...], wt_low[...], proj1)


def body(table, target_table, centres, coefficients, batch_index):
    dma = pltpu.SemaphoreType.DMA
    vmem = pl.BlockSpec(memory_space=pltpu.VMEM)
    square = jax.ShapeDtypeStruct((256, 256), F32)
    turned = jax.ShapeDtypeStruct((512, 256), BF16)
    per_peer = [pltpu.VMEM((NP, n, 128), F32) for n in SHARE]
    sums = pl.pallas_call(
        exchange,
        name="exchange",
        out_shape=(
            jax.ShapeDtypeStruct((2, NP, 16, 128), F32),
            square,
            jax.ShapeDtypeStruct((8, 128), F32),
            turned,
            turned,
            jax.ShapeDtypeStruct((512, 256), F32),
            square,
        ),
        in_specs=[pl.BlockSpec(memory_space=pl.ANY)] * 5,
        out_specs=(vmem,) * 7,
        scratch_shapes=[
            pltpu.VMEM((512, 128), BF16),
            pltpu.VMEM((512, 256), BF16),
            pltpu.VMEM((512, 1024), BF16),
            pltpu.VMEM((512, 256), F32),
            pltpu.VMEM((2, 256), jnp.int32),
            pltpu.VMEM((512, 256), F32),
            pltpu.VMEM((512, 256), BF16),
            pltpu.VMEM((512, 256), BF16),
            pltpu.VMEM((ND, 16, 128), BF16),
            pltpu.VMEM((ND, 16, 128), BF16),
            pltpu.VMEM((NZ, NY, 16, 1024), BF16),
            pltpu.VMEM((512, 512), BF16),
            pltpu.VMEM((512, 512), BF16),
            pltpu.VMEM((512, 256), BF16),
            pltpu.VMEM((512, 256), BF16),
            *per_peer, *per_peer, *per_peer, *per_peer,
            *[pltpu.VMEM((NZ, n, 128), F32) for n in SHARE],
            pltpu.VMEM((2, NP, 16, 128), F32),
            pltpu.VMEM((2, NP, 16, 128), F32),
            dma((5,)), dma((4,)), dma, dma((NZ,)), dma((3,)), dma((3,)),
            dma((15,)), dma((3,)), dma((3,)), dma((3,)), dma((3,)), dma((3,)),
        ],
        compiler_params=pltpu.CompilerParams(
            collective_id=0, has_side_effects=True, vmem_limit_bytes=40 * 2**20
        ),
    )(*[
        pltpu.with_memory_space_constraint(a, pltpu.HBM)
        for a in (table, target_table, centres, coefficients, batch_index)
    ])
    return pl.pallas_call(
        update,
        name="update",
        out_shape=(
            jax.ShapeDtypeStruct((512, 256), F32),
            jax.ShapeDtypeStruct((2, 256, 256), F32),
        ),
        in_specs=[vmem] * 7,
        out_specs=(vmem, vmem),
        compiler_params=pltpu.CompilerParams(vmem_limit_bytes=24 * 2**20),
    )(*sums)


def solution(mesh):
    in_specs = (
        P("dev", None),
        P("dev", None),
        P(("grp", "dev"), None),
        P(("grp", "dev"), None),
        P(),
    )
    out_specs = (P(("grp", "dev"), None), P())
    return jax.shard_map(body, mesh=mesh, in_specs=in_specs, out_specs=out_specs, check_vma=False)
```

```python
import math

import jax
import jax.numpy as jnp
from jax import lax
from jax.experimental import pallas as pl
from jax.experimental.pallas import tpu as pltpu
from jax.sharding import PartitionSpec as P

MESH = pl.DeviceIdType.MESH
SPREAD = 2.0
RATE = 2.0
NX, NC, NY, NZ = 4, 2, 4, 8
NP = NX * NY
ND = NY * NZ
F32 = jnp.float32
BF16 = jnp.bfloat16
HI = lax.Precision.HIGHEST
NN = (((1,), (0,)), ((), ()))
NT = (((1,), (1,)), ((), ()))
TN = (((0,), (0,)), ((), ()))


def hops(k, n):
    return min(k, n - k)


Z_FAR = sorted(range(1, NZ), key=lambda k: -hops(k, NZ))
Z_NEAR = Z_FAR[::-1]
XY_FAR = sorted(
    [(i, j) for i in range(NX) for j in range(NY) if i or j],
    key=lambda o: -hops(o[0], NX) - hops(o[1], NY),
)
YZ_FAR = sorted(
    [(j, k) for j in range(NY) for k in range(NZ) if j or k],
    key=lambda o: -hops(o[0], NY) - hops(o[1], NZ),
)


def dot(a, b, dims=NN, precision=None):
    return lax.dot_general(a, b, dims, precision=precision, preferred_element_type=F32)


def split(a):
    high = a.astype(BF16)
    return high, (a - high.astype(F32)).astype(BF16)


SLOTS = [0, 2, 6, 3, 5, 4, 1, 7]
GROUPS = [(0, 1), (1, 2), (2, 3), (3, 6)]
SHARE = (16, 24, 16)


def pieces_to_whole(whole):
    halves = [
        jnp.concatenate([whole[h, :, m * 8 : m * 8 + 8, :].reshape(128, 128) for m in range(2)], axis=1)
        for h in range(2)
    ]
    return jnp.concatenate(halves, axis=0)


def column(mass, s):
    tiles = [jnp.broadcast_to(mass[2 * s + m : 2 * s + m + 1, :], (128, 128)).T for m in range(2)]
    tall = jnp.concatenate(tiles, axis=0)
    return jnp.concatenate([tall, tall], axis=1)


def project(resid, m):
    along = jnp.sum(m * resid, axis=0, keepdims=True) / jnp.sum(m * m, axis=0, keepdims=True)
    return resid - m * along


def grad(high, low, proj):
    ph, pw = split(proj)
    return dot(high, ph) + (dot(high, pw) + dot(low, ph))


def exchange(
    table, target, centres, coef, index,
    whole2, turn_out, mass_out, wt_high, wt_low, coef_half, resid0_out,
    tab_v, tgt_v, cen_v, cf_v, idx_v, aims_v, cf_high, cf_low,
    pick, parts, rows, w_high, w_low, wt0_high, wt0_low,
    core_send0, core_send1, core_send2, core_recv0, core_recv1, core_recv2,
    xy_send0, xy_send1, xy_send2, xy_recv0, xy_recv1, xy_recv2,
    z_buf0, z_buf1, z_buf2, whole0, whole1,
    load_sem, a_sent, a_recv, az_recv, axy_recv, ac_recv,
    c_sent, cc_recv, cxy_recv, cz_recv, gxy_recv, gc_recv,
):
    core_send, core_recv = (core_send0, core_send1, core_send2), (core_recv0, core_recv1, core_recv2)
    xy_send, xy_recv = (xy_send0, xy_send1, xy_send2), (xy_recv0, xy_recv1, xy_recv2)
    z_buf, whole = (z_buf0, z_buf1, z_buf2), (whole0, whole1, whole2)
    g = lax.axis_index("grp")
    d = lax.axis_index("dev")
    x, c = g // 2, g % 2
    y, z = d // NZ, d % NZ
    p = x * NY + y
    feat = c * NX + x
    chunk = z * NY + y
    radius = math.sqrt(2.0 * 1024)
    scale = 1.0 / math.sqrt(131072)

    xs = [lax.rem(x + k, NX) for k in range(NX)]
    ys = [lax.rem(y + k, NY) for k in range(NY)]
    zs = [lax.rem(z + k, NZ) for k in range(NZ)]
    grps = [v * 2 + c for v in xs]
    bases = [v * NZ for v in ys]

    def at_xy(o):
        return {"grp": grps[o[0]], "dev": bases[o[1]] + z}

    def at_yz(o):
        return {"grp": g, "dev": bases[o[0]] + zs[o[1]]}

    sibling = {"grp": x * 2 + 1 - c, "dev": d}

    def send(src, dst, send_sem, recv_sem, to):
        copy = pltpu.make_async_remote_copy(
            src_ref=src, dst_ref=dst, send_sem=send_sem, recv_sem=recv_sem,
            device_id=to, device_id_type=MESH,
        )
        copy.start()
        return copy

    def wait_bytes(ref, sem):
        pltpu.make_async_copy(ref, ref, sem).wait()

    loads = [
        pltpu.make_async_copy(index, idx_v, load_sem.at[0]),
        pltpu.make_async_copy(
            table.at[:, pl.ds(pl.multiple_of(feat * 128, 128), 128)], tab_v, load_sem.at[1]
        ),
        pltpu.make_async_copy(target, tgt_v, load_sem.at[2]),
        pltpu.make_async_copy(centres, cen_v, load_sem.at[3]),
        pltpu.make_async_copy(coef, cf_v, load_sem.at[4]),
    ]
    for load in loads:
        load.start()

    barrier = pltpu.get_barrier_semaphore()
    greeted = [at_yz(o) for o in YZ_FAR] + [at_xy(o) for o in XY_FAR if o[0]] + [sibling]
    for to in greeted:
        pl.semaphore_signal(barrier, inc=1, device_id=to, device_id_type=MESH)

    loads[0].wait()
    here = lax.broadcasted_iota(jnp.int32, (512, 256), 0) + d * 512
    hot = jnp.concatenate(
        [(here == idx_v[s : s + 1, :]).astype(F32).astype(BF16) for s in range(2)], axis=1
    )
    loads[1].wait()
    pick[...] = dot(hot, tab_v[...], TN).astype(BF16).reshape(ND, 16, 128)
    parts[chunk] = pick[chunk]

    pl.semaphore_wait(barrier, len(greeted))

    for o in YZ_FAR:
        send(
            pick.at[zs[o[1]] * NY + ys[o[0]]], parts.at[chunk], a_sent.at[0], a_recv, at_yz(o)
        )

    loads[2].wait()
    first = (g == 0).astype(F32)
    aims_v[...] = dot(hot, tgt_v[...], TN) * first
    loads[3].wait()
    high, low = split(jnp.square(cen_v[...].astype(F32)))
    ones = jnp.ones((8, 1024), BF16)
    cnorm = (dot(ones, high, NT) + dot(ones, low, NT))[0:1, :]
    loads[4].wait()
    cf_high[...], cf_low[...] = split(cf_v[...])

    wait_bytes(parts.at[pl.ds(0, ND - 1)], a_recv)
    own = jnp.sum(parts[...].astype(F32), axis=0).astype(BF16)
    rows[0, feat, y] = own

    mine = rows.at[0, feat, y]
    for k in Z_FAR:
        slot = SLOTS.index(NZ - k)
        if slot < 6:
            send(mine, rows.at[slot, feat, y], a_sent.at[1], az_recv.at[NZ - k], at_yz((0, k)))
    for n, (b, e) in enumerate(GROUPS):
        for r in SLOTS[b:e]:
            if r:
                wait_bytes(parts.at[0], az_recv.at[r])
        group = rows.at[pl.ds(b, e - b), feat, y]
        for o in XY_FAR:
            send(group, group, a_sent.at[2], axy_recv.at[n], at_xy(o))

    half = pl.ds(c * NX, NX)

    def to_sibling(b, e, n):
        strip = rows.at[pl.ds(b, e - b), half]
        send(strip, strip, a_sent.at[3], ac_recv.at[n], sibling)

    def wait_group(n):
        b, e = GROUPS[n]
        wait_bytes(rows.at[pl.ds(0, e - b), pl.ds(0, 5), pl.ds(0, 3)], axy_recv.at[n])
        if n == 0:
            strip = rows.at[0, half]
            for k, slot in ((1, 7), (7, 6)):
                send(strip, rows.at[slot, half], a_sent.at[4], az_recv.at[NZ - k], at_yz((0, k)))
        to_sibling(b, e, n)

    for n in range(3):
        wait_group(n)
    for slot in (6, 7):
        wait_bytes(rows.at[0, pl.ds(0, NX)], az_recv.at[SLOTS[slot]])
        to_sibling(slot, slot + 1, slot - 2)
    wait_group(3)

    for b, e, arrivals in ((0, 3, ((0, 1), (1, 1), (2, 1))), (6, 8, ((4, 1), (5, 1))), (3, 6, ((3, 3),))):
        for n, blocks in arrivals:
            wait_bytes(rows.at[pl.ds(0, blocks), pl.ds(0, NX)], ac_recv.at[n])
        some = jnp.concatenate([rows[b:e, f].reshape((e - b) * 64, 128) for f in range(8)], axis=1)
        rnorm = jnp.sum(jnp.square(some.astype(F32)), axis=1, keepdims=True)
        cross = dot(some, cen_v[...], NT)
        dist = jnp.sqrt(jnp.maximum(rnorm + cnorm - 2.0 * cross, 0.0))
        high, low = split(jnp.exp((radius - dist) / SPREAD) * scale)
        for r in range(b, e):
            at = pl.ds(pl.multiple_of(zs[SLOTS[r]] * 64, 64), 64)
            w_high[at, :] = high[(r - b) * 64 : (r - b) * 64 + 64]
            w_low[at, :] = low[(r - b) * 64 : (r - b) * 64 + 64]

    def terms(n, h, dst):
        s = n // 2
        at = pl.ds(pl.multiple_of(h * 128 + (0, 256, 256)[n], 128), 128)
        high, low = w_high[at, :], w_low[at, :]
        if n == 1:
            gh, gl = w_high[0:256, :], w_low[0:256, :]
            part = dot(high, gh, NT) + (dot(high, gl, NT) + dot(low, gh, NT))
        else:
            ch, cl = cf_high[...], cf_low[...]
            part = dot(high, ch) + (dot(high, cl) + dot(low, ch)) - aims_v[at, :]
        for m in range(2):
            dst[:, m * 8 : m * 8 + 8, :] = part[:, m * 128 : m * 128 + 128].reshape(NP, 8, 128)

    for n in range(3):
        terms(n, 1 - c, core_send[n])
        if n == 1:
            ones = jnp.ones((8, 512), BF16)
            mass = dot(ones, w_high[...], NT) + dot(ones, w_low[...], NT)
            mass = jnp.concatenate(
                [mass[0:1, m * 128 : m * 128 + 128] for m in range(4)] + [jnp.zeros((4, 128), F32)],
                axis=0,
            )
            mass = jnp.broadcast_to(mass[None], (NP, 8, 128))
            core_send[1][:, 16:24, :] = mass
            xy_send[1][:, 16:24, :] = mass
        send(core_send[n], core_recv[n], c_sent.at[n], cc_recv.at[n], sibling)
    for n in range(3):
        terms(n, c, xy_send[n])
        wait_bytes(core_recv[n], cc_recv.at[n])
        xy_send[n][...] = xy_send[n][...] + core_recv[n][...]
        for o in XY_FAR:
            send(
                xy_send[n].at[xs[o[0]] * NY + ys[o[1]]], xy_recv[n].at[p],
                c_sent.at[3 + n], cxy_recv.at[n], at_xy(o),
            )
        xy_recv[n][p] = xy_send[n][p]

    wt0_high[...] = w_high[0:256, :].T
    wt0_low[...] = w_low[0:256, :].T
    wt_high[...] = w_high[256:512, :].T
    wt_low[...] = w_low[256:512, :].T

    for n in range(3):
        wait_bytes(xy_recv[n].at[pl.ds(0, NP - 1)], cxy_recv.at[n])
        z_buf[n][z] = jnp.sum(xy_recv[n][...], axis=0)
        for k in Z_FAR:
            send(z_buf[n].at[z], z_buf[n].at[z], c_sent.at[6 + n], cz_recv.at[n], at_yz((0, k)))
    for n in range(3):
        wait_bytes(z_buf[n].at[pl.ds(0, NZ - 1)], cz_recv.at[n])
        total = jnp.sum(z_buf[n][...], axis=0)
        whole[n][c, p] = total[0:16]
        for o in XY_FAR:
            send(whole[n].at[c, p], whole[n].at[c, p], c_sent.at[9 + n], gxy_recv.at[n], at_xy(o))
        if n == 1:
            mass = total[16:24]
            mass_out[...] = mass
            m0 = column(mass, 0)
    def whole_to_sibling(n):
        wait_bytes(whole[n].at[0, pl.ds(0, NP - 1)], gxy_recv.at[n])
        send(whole[n].at[c], whole[n].at[c], c_sent.at[12 + n], gc_recv.at[n], sibling)

    whole_to_sibling(0)
    whole_to_sibling(1)
    wait_bytes(whole[0].at[0], gc_recv.at[0])
    resid0 = pieces_to_whole(whole0)
    resid0_out[...] = resid0
    proj0 = project(resid0, m0)
    whole_to_sibling(2)
    wait_bytes(whole[1].at[0], gc_recv.at[1])
    turn_out[...] = RATE * dot(pieces_to_whole(whole1), proj0, precision=HI)
    coef_half[...] = cf_v[...] - RATE * grad(wt0_high[...], wt0_low[...], proj0)
    wait_bytes(whole[2].at[0], gc_recv.at[2])

    wait_bytes(parts.at[pl.ds(0, ND - 1)], a_sent.at[0])
    wait_bytes(parts.at[pl.ds(0, 5)], a_sent.at[1])
    wait_bytes(rows.at[pl.ds(0, 6), pl.ds(0, 5), pl.ds(0, 3)], a_sent.at[2])
    wait_bytes(rows.at[:, pl.ds(0, NX)], a_sent.at[3])
    wait_bytes(rows.at[pl.ds(0, 2), pl.ds(0, NX)], a_sent.at[4])
    for n in range(3):
        wait_bytes(core_recv[n], c_sent.at[n])
        wait_bytes(xy_recv[n].at[pl.ds(0, NP - 1)], c_sent.at[3 + n])
        wait_bytes(z_buf[n].at[pl.ds(0, NZ - 1)], c_sent.at[6 + n])
        wait_bytes(whole[n].at[0, pl.ds(0, NP - 1)], c_sent.at[9 + n])
        wait_bytes(whole[n].at[0], c_sent.at[12 + n])


def update(
    whole2, turn, mass, wt_high, wt_low, coef_half, resid0, coef_out, resid_out, coef_v, resid1_v, out_sem
):
    copies = [pltpu.make_async_copy(resid0, resid_out.at[0], out_sem.at[0])]
    copies[0].start()
    resid1 = pieces_to_whole(whole2) - turn[...]
    resid1_v[...] = resid1
    copies.append(pltpu.make_async_copy(resid1_v, resid_out.at[1], out_sem.at[1]))
    copies[1].start()
    proj1 = project(resid1, column(mass[...], 1))
    for m in range(2):
        at = pl.ds(m * 256, 256)
        coef_v[at, :] = coef_half[at, :] - RATE * grad(wt_high[at, :], wt_low[at, :], proj1)
        copies.append(pltpu.make_async_copy(coef_v.at[at], coef_out.at[at], out_sem.at[2 + m]))
        copies[2 + m].start()
    for copy in copies:
        copy.wait()


def body(table, target_table, centres, coefficients, batch_index):
    dma = pltpu.SemaphoreType.DMA
    vmem = pl.BlockSpec(memory_space=pltpu.VMEM)
    square = jax.ShapeDtypeStruct((256, 256), F32)
    turned = jax.ShapeDtypeStruct((512, 256), BF16)
    per_peer = [pltpu.VMEM((NP, n, 128), F32) for n in SHARE]
    sums = pl.pallas_call(
        exchange,
        name="exchange",
        out_shape=(
            jax.ShapeDtypeStruct((2, NP, 16, 128), F32),
            square,
            jax.ShapeDtypeStruct((8, 128), F32),
            turned,
            turned,
            jax.ShapeDtypeStruct((512, 256), F32),
            square,
        ),
        in_specs=[pl.BlockSpec(memory_space=pl.ANY)] * 5,
        out_specs=(vmem,) * 7,
        scratch_shapes=[
            pltpu.VMEM((512, 128), BF16),
            pltpu.VMEM((512, 256), BF16),
            pltpu.VMEM((512, 1024), BF16),
            pltpu.VMEM((512, 256), F32),
            pltpu.VMEM((2, 256), jnp.int32),
            pltpu.VMEM((512, 256), F32),
            pltpu.VMEM((512, 256), BF16),
            pltpu.VMEM((512, 256), BF16),
            pltpu.VMEM((ND, 16, 128), BF16),
            pltpu.VMEM((ND, 16, 128), BF16),
            pltpu.VMEM((NZ, 8, NY, 16, 128), BF16),
            pltpu.VMEM((512, 512), BF16),
            pltpu.VMEM((512, 512), BF16),
            pltpu.VMEM((512, 256), BF16),
            pltpu.VMEM((512, 256), BF16),
            *per_peer, *per_peer, *per_peer, *per_peer,
            *[pltpu.VMEM((NZ, n, 128), F32) for n in SHARE],
            pltpu.VMEM((2, NP, 16, 128), F32),
            pltpu.VMEM((2, NP, 16, 128), F32),
            dma((5,)), dma((5,)), dma, dma((NZ,)), dma((4,)), dma((6,)),
            dma((15,)), dma((3,)), dma((3,)), dma((3,)), dma((3,)), dma((3,)),
        ],
        compiler_params=pltpu.CompilerParams(
            collective_id=0, has_side_effects=True, vmem_limit_bytes=40 * 2**20
        ),
    )(*[
        pltpu.with_memory_space_constraint(a, pltpu.HBM)
        for a in (table, target_table, centres, coefficients, batch_index)
    ])
    return pl.pallas_call(
        update,
        name="update",
        out_shape=(
            jax.ShapeDtypeStruct((512, 256), F32),
            jax.ShapeDtypeStruct((2, 256, 256), F32),
        ),
        in_specs=[vmem] * 7,
        out_specs=(pl.BlockSpec(memory_space=pl.ANY), pl.BlockSpec(memory_space=pl.ANY)),
        scratch_shapes=[pltpu.VMEM((512, 256), F32), pltpu.VMEM((256, 256), F32), dma((4,))],
        compiler_params=pltpu.CompilerParams(vmem_limit_bytes=24 * 2**20),
    )(*sums)


def solution(mesh):
    in_specs = (
        P("dev", None),
        P("dev", None),
        P(("grp", "dev"), None),
        P(("grp", "dev"), None),
        P(),
    )
    out_specs = (P(("grp", "dev"), None), P())
    return jax.shard_map(body, mesh=mesh, in_specs=in_specs, out_specs=out_specs, check_vma=False)
```

```python
import math

import jax
import jax.numpy as jnp
from jax import lax
from jax.experimental import pallas as pl
from jax.experimental.pallas import tpu as pltpu
from jax.sharding import PartitionSpec as P

MESH = pl.DeviceIdType.MESH
SPREAD = 2.0
RATE = 2.0
NX, NC, NY, NZ = 4, 2, 4, 8
NP = NX * NY
ND = NY * NZ
F32 = jnp.float32
BF16 = jnp.bfloat16
HI = lax.Precision.HIGHEST
NN = (((1,), (0,)), ((), ()))
NT = (((1,), (1,)), ((), ()))
TN = (((0,), (0,)), ((), ()))


def hops(k, n):
    return min(k, n - k)


Z_FAR = sorted(range(1, NZ), key=lambda k: -hops(k, NZ))
Z_NEAR = Z_FAR[::-1]
XY_FAR = sorted(
    [(i, j) for i in range(NX) for j in range(NY) if i or j],
    key=lambda o: -hops(o[0], NX) - hops(o[1], NY),
)
YZ_FAR = sorted(
    [(j, k) for j in range(NY) for k in range(NZ) if j or k],
    key=lambda o: -hops(o[0], NY) - hops(o[1], NZ),
)


def dot(a, b, dims=NN, precision=None):
    return lax.dot_general(a, b, dims, precision=precision, preferred_element_type=F32)


def split(a):
    high = a.astype(BF16)
    return high, (a - high.astype(F32)).astype(BF16)


SLOTS = [0, 2, 6, 3, 5, 4, 1, 7]
GROUPS = [(0, 1), (1, 2), (2, 3), (3, 5), (5, 6)]
SHARE = (16, 16, 24)


def pieces_to_whole(whole):
    halves = [
        jnp.concatenate([whole[h, :, m * 8 : m * 8 + 8, :].reshape(128, 128) for m in range(2)], axis=1)
        for h in range(2)
    ]
    return jnp.concatenate(halves, axis=0)


def column(mass, s):
    tiles = [jnp.broadcast_to(mass[2 * s + m : 2 * s + m + 1, :], (128, 128)).T for m in range(2)]
    tall = jnp.concatenate(tiles, axis=0)
    return jnp.concatenate([tall, tall], axis=1)


def project(resid, m):
    along = jnp.sum(m * resid, axis=0, keepdims=True) / jnp.sum(m * m, axis=0, keepdims=True)
    return resid - m * along


def grad(high, low, proj):
    ph, pw = split(proj)
    return dot(high, ph) + (dot(high, pw) + dot(low, ph))


def exchange(
    table, target, centres, coef, index,
    whole2, turn_out, mass_out, wt_high, wt_low, coef_half, resid0_out,
    tab_v, tgt_v, cen_v, cf_v, idx_v, aims_v, cf_high, cf_low,
    pick, parts, rows, w_high, w_low, wt0_high, wt0_low,
    terms0, terms1, terms2, core_recv0, core_recv1, core_recv2,
    xy_send0, xy_send1, xy_send2, xy_recv0, xy_recv1, xy_recv2,
    z_buf0, z_buf1, z_buf2, whole0, whole1,
    load_sem, a_sent, a_recv, az_recv, axy_recv, ac_recv,
    c_sent, cc_recv, cxy_recv, cz_recv, gxy_recv, gc_recv,
):
    terms, core_recv = (terms0, terms1, terms2), (core_recv0, core_recv1, core_recv2)
    xy_send, xy_recv = (xy_send0, xy_send1, xy_send2), (xy_recv0, xy_recv1, xy_recv2)
    z_buf, whole = (z_buf0, z_buf1, z_buf2), (whole0, whole1, whole2)
    g = lax.axis_index("grp")
    d = lax.axis_index("dev")
    x, c = g // 2, g % 2
    y, z = d // NZ, d % NZ
    p = x * NY + y
    feat = c * NX + x
    chunk = z * NY + y
    radius = math.sqrt(2.0 * 1024)
    scale = 1.0 / math.sqrt(131072)

    xs = [lax.rem(x + k, NX) for k in range(NX)]
    ys = [lax.rem(y + k, NY) for k in range(NY)]
    zs = [lax.rem(z + k, NZ) for k in range(NZ)]
    grps = [v * 2 + c for v in xs]
    bases = [v * NZ for v in ys]

    def at_xy(o):
        return {"grp": grps[o[0]], "dev": bases[o[1]] + z}

    def at_yz(o):
        return {"grp": g, "dev": bases[o[0]] + zs[o[1]]}

    sibling = {"grp": x * 2 + 1 - c, "dev": d}

    def send(src, dst, send_sem, recv_sem, to):
        copy = pltpu.make_async_remote_copy(
            src_ref=src, dst_ref=dst, send_sem=send_sem, recv_sem=recv_sem,
            device_id=to, device_id_type=MESH,
        )
        copy.start()
        return copy

    def wait_bytes(ref, sem):
        pltpu.make_async_copy(ref, ref, sem).wait()

    loads = [
        pltpu.make_async_copy(index, idx_v, load_sem.at[0]),
        pltpu.make_async_copy(
            table.at[:, pl.ds(pl.multiple_of(feat * 128, 128), 128)], tab_v, load_sem.at[1]
        ),
        pltpu.make_async_copy(target, tgt_v, load_sem.at[2]),
        pltpu.make_async_copy(centres, cen_v, load_sem.at[3]),
        pltpu.make_async_copy(coef, cf_v, load_sem.at[4]),
    ]
    for load in loads:
        load.start()

    barrier = pltpu.get_barrier_semaphore()
    greeted = [at_yz(o) for o in YZ_FAR] + [at_xy(o) for o in XY_FAR if o[0]] + [sibling]
    for to in greeted:
        pl.semaphore_signal(barrier, inc=1, device_id=to, device_id_type=MESH)

    loads[0].wait()
    here = lax.broadcasted_iota(jnp.int32, (512, 256), 0) + d * 512
    hot = jnp.concatenate(
        [(here == idx_v[s : s + 1, :]).astype(F32).astype(BF16) for s in range(2)], axis=1
    )
    loads[1].wait()
    pick[...] = dot(hot, tab_v[...], TN).astype(BF16).reshape(ND, 16, 128)
    parts[chunk] = pick[chunk]

    pl.semaphore_wait(barrier, len(greeted))

    for o in YZ_FAR:
        send(
            pick.at[zs[o[1]] * NY + ys[o[0]]], parts.at[chunk], a_sent.at[0], a_recv, at_yz(o)
        )

    loads[2].wait()
    first = (g == 0).astype(F32)
    aims_v[...] = dot(hot, tgt_v[...], TN) * first
    loads[3].wait()
    high, low = split(jnp.square(cen_v[...].astype(F32)))
    ones = jnp.ones((8, 1024), BF16)
    cnorm = (dot(ones, high, NT) + dot(ones, low, NT))[0:1, :]
    loads[4].wait()
    cf_high[...], cf_low[...] = split(cf_v[...])

    wait_bytes(parts.at[pl.ds(0, ND - 1)], a_recv)
    own = jnp.sum(parts[...].astype(F32), axis=0).astype(BF16)
    rows[0, feat, y] = own

    mine = rows.at[0, feat, y]
    for k in Z_FAR:
        slot = SLOTS.index(NZ - k)
        if slot < 6:
            send(mine, rows.at[slot, feat, y], a_sent.at[1], az_recv.at[NZ - k], at_yz((0, k)))
    for n, (b, e) in enumerate(GROUPS):
        for r in SLOTS[b:e]:
            if r:
                wait_bytes(parts.at[0], az_recv.at[r])
        group = rows.at[pl.ds(b, e - b), feat, y]
        for o in XY_FAR:
            send(group, group, a_sent.at[2], axy_recv.at[n], at_xy(o))

    half = pl.ds(c * NX, NX)

    def to_sibling(b, e, n):
        strip = rows.at[pl.ds(b, e - b), half]
        send(strip, strip, a_sent.at[3], ac_recv.at[n], sibling)

    def wait_group(n):
        b, e = GROUPS[n]
        wait_bytes(rows.at[pl.ds(0, e - b), pl.ds(0, 5), pl.ds(0, 3)], axy_recv.at[n])
        if n == 0:
            strip = rows.at[0, half]
            for k, slot in ((1, 7), (7, 6)):
                send(strip, rows.at[slot, half], a_sent.at[4], az_recv.at[NZ - k], at_yz((0, k)))
        to_sibling(b, e, n)

    for n in range(3):
        wait_group(n)
    for slot in (6, 7):
        wait_bytes(rows.at[0, pl.ds(0, NX)], az_recv.at[SLOTS[slot]])
        to_sibling(slot, slot + 1, slot - 1)
    wait_group(3)
    wait_group(4)

    for b, e, arrivals in (
        (0, 3, ((0, 1), (1, 1), (2, 1))),
        (6, 8, ((5, 1), (6, 1))),
        (3, 5, ((3, 2),)),
        (5, 6, ((4, 1),)),
    ):
        for n, blocks in arrivals:
            wait_bytes(rows.at[pl.ds(0, blocks), pl.ds(0, NX)], ac_recv.at[n])
        some = jnp.concatenate([rows[b:e, f].reshape((e - b) * 64, 128) for f in range(8)], axis=1)
        rnorm = jnp.sum(jnp.square(some.astype(F32)), axis=1, keepdims=True)
        cross = dot(some, cen_v[...], NT)
        dist = jnp.sqrt(jnp.maximum(rnorm + cnorm - 2.0 * cross, 0.0))
        high, low = split(jnp.exp((radius - dist) / SPREAD) * scale)
        for r in range(b, e):
            at = pl.ds(pl.multiple_of(zs[SLOTS[r]] * 64, 64), 64)
            w_high[at, :] = high[(r - b) * 64 : (r - b) * 64 + 64]
            w_low[at, :] = low[(r - b) * 64 : (r - b) * 64 + 64]

    for n in range(3):
        at = pl.ds(256 if n else 0, 256)
        high, low = w_high[at, :], w_low[at, :]
        if n == 1:
            gh, gl = w_high[0:256, :], w_low[0:256, :]
            part = dot(high, gh, NT) + (dot(high, gl, NT) + dot(low, gh, NT))
        else:
            ch, cl = cf_high[...], cf_low[...]
            part = dot(high, ch) + (dot(high, cl) + dot(low, ch)) - aims_v[at, :]
        for h in range(2):
            for m in range(2):
                tiles = part[h * 128 : h * 128 + 128, m * 128 : m * 128 + 128].reshape(NP, 8, 128)
                terms[n][h, :, m * 8 : m * 8 + 8, :] = tiles
        if n == 2:
            ones = jnp.ones((8, 512), BF16)
            mass = dot(ones, w_high[...], NT) + dot(ones, w_low[...], NT)
            mass = jnp.concatenate(
                [mass[0:1, m * 128 : m * 128 + 128] for m in range(4)] + [jnp.zeros((4, 128), F32)],
                axis=0,
            )
            terms[2][:, :, 16:24, :] = jnp.broadcast_to(mass[None, None], (2, NP, 8, 128))
        send(terms[n].at[1 - c], core_recv[n], c_sent.at[n], cc_recv.at[n], sibling)
    for n in range(3):
        wait_bytes(core_recv[n], cc_recv.at[n])
        xy_send[n][...] = terms[n][c] + core_recv[n][...]
        for o in XY_FAR:
            send(
                xy_send[n].at[xs[o[0]] * NY + ys[o[1]]], xy_recv[n].at[p],
                c_sent.at[3 + n], cxy_recv.at[n], at_xy(o),
            )
        xy_recv[n][p] = xy_send[n][p]

    wt0_high[...] = w_high[0:256, :].T
    wt0_low[...] = w_low[0:256, :].T
    wt_high[...] = w_high[256:512, :].T
    wt_low[...] = w_low[256:512, :].T

    for n in range(3):
        wait_bytes(xy_recv[n].at[pl.ds(0, NP - 1)], cxy_recv.at[n])
        z_buf[n][z] = jnp.sum(xy_recv[n][...], axis=0)
        for k in Z_FAR:
            send(z_buf[n].at[z], z_buf[n].at[z], c_sent.at[6 + n], cz_recv.at[n], at_yz((0, k)))
    for n in range(3):
        wait_bytes(z_buf[n].at[pl.ds(0, NZ - 1)], cz_recv.at[n])
        total = jnp.sum(z_buf[n][...], axis=0)
        whole[n][c, p] = total[0:16]
        for o in XY_FAR:
            send(whole[n].at[c, p], whole[n].at[c, p], c_sent.at[9 + n], gxy_recv.at[n], at_xy(o))
        if n == 2:
            mass = total[16:24]
    def whole_to_sibling(n):
        wait_bytes(whole[n].at[0, pl.ds(0, NP - 1)], gxy_recv.at[n])
        send(whole[n].at[c], whole[n].at[c], c_sent.at[12 + n], gc_recv.at[n], sibling)

    m0 = column(mass, 0)
    mass_out[...] = column(mass, 1)
    whole_to_sibling(0)
    whole_to_sibling(1)
    wait_bytes(whole[0].at[0], gc_recv.at[0])
    resid0 = pieces_to_whole(whole0)
    resid0_out[...] = resid0
    proj0 = project(resid0, m0)
    whole_to_sibling(2)
    wait_bytes(whole[1].at[0], gc_recv.at[1])
    turn_out[...] = RATE * dot(pieces_to_whole(whole1), proj0, precision=HI)
    coef_half[...] = cf_v[...] - RATE * grad(wt0_high[...], wt0_low[...], proj0)
    wait_bytes(whole[2].at[0], gc_recv.at[2])

    wait_bytes(parts.at[pl.ds(0, ND - 1)], a_sent.at[0])
    wait_bytes(parts.at[pl.ds(0, 5)], a_sent.at[1])
    wait_bytes(rows.at[pl.ds(0, 6), pl.ds(0, 5), pl.ds(0, 3)], a_sent.at[2])
    wait_bytes(rows.at[:, pl.ds(0, NX)], a_sent.at[3])
    wait_bytes(rows.at[pl.ds(0, 2), pl.ds(0, NX)], a_sent.at[4])
    for n in range(3):
        wait_bytes(core_recv[n], c_sent.at[n])
        wait_bytes(xy_recv[n].at[pl.ds(0, NP - 1)], c_sent.at[3 + n])
        wait_bytes(z_buf[n].at[pl.ds(0, NZ - 1)], c_sent.at[6 + n])
        wait_bytes(whole[n].at[0, pl.ds(0, NP - 1)], c_sent.at[9 + n])
        wait_bytes(whole[n].at[0], c_sent.at[12 + n])


def update(
    whole2, turn, mass, wt_high, wt_low, coef_half, resid0, coef_out, resid_out, coef_v, resid1_v, out_sem
):
    copies = [pltpu.make_async_copy(resid0, resid_out.at[0], out_sem.at[0])]
    copies[0].start()
    resid1 = pieces_to_whole(whole2) - turn[...]
    resid1_v[...] = resid1
    copies.append(pltpu.make_async_copy(resid1_v, resid_out.at[1], out_sem.at[1]))
    copies[1].start()
    proj1 = project(resid1, mass[...])
    for m in range(2):
        at = pl.ds(m * 256, 256)
        coef_v[at, :] = coef_half[at, :] - RATE * grad(wt_high[at, :], wt_low[at, :], proj1)
        copies.append(pltpu.make_async_copy(coef_v.at[at], coef_out.at[at], out_sem.at[2 + m]))
        copies[2 + m].start()
    for copy in copies:
        copy.wait()


def body(table, target_table, centres, coefficients, batch_index):
    dma = pltpu.SemaphoreType.DMA
    vmem = pl.BlockSpec(memory_space=pltpu.VMEM)
    square = jax.ShapeDtypeStruct((256, 256), F32)
    turned = jax.ShapeDtypeStruct((512, 256), BF16)
    per_peer = [pltpu.VMEM((NP, n, 128), F32) for n in SHARE]
    sums = pl.pallas_call(
        exchange,
        name="exchange",
        out_shape=(
            jax.ShapeDtypeStruct((2, NP, 16, 128), F32),
            square,
            square,
            turned,
            turned,
            jax.ShapeDtypeStruct((512, 256), F32),
            square,
        ),
        in_specs=[pl.BlockSpec(memory_space=pl.ANY)] * 5,
        out_specs=(vmem,) * 7,
        scratch_shapes=[
            pltpu.VMEM((512, 128), BF16),
            pltpu.VMEM((512, 256), BF16),
            pltpu.VMEM((512, 1024), BF16),
            pltpu.VMEM((512, 256), F32),
            pltpu.VMEM((2, 256), jnp.int32),
            pltpu.VMEM((512, 256), F32),
            pltpu.VMEM((512, 256), BF16),
            pltpu.VMEM((512, 256), BF16),
            pltpu.VMEM((ND, 16, 128), BF16),
            pltpu.VMEM((ND, 16, 128), BF16),
            pltpu.VMEM((NZ, 8, NY, 16, 128), BF16),
            pltpu.VMEM((512, 512), BF16),
            pltpu.VMEM((512, 512), BF16),
            pltpu.VMEM((512, 256), BF16),
            pltpu.VMEM((512, 256), BF16),
            *[pltpu.VMEM((2, NP, n, 128), F32) for n in SHARE],
            *per_peer, *per_peer, *per_peer,
            *[pltpu.VMEM((NZ, n, 128), F32) for n in SHARE],
            pltpu.VMEM((2, NP, 16, 128), F32),
            pltpu.VMEM((2, NP, 16, 128), F32),
            dma((5,)), dma((5,)), dma, dma((NZ,)), dma((5,)), dma((7,)),
            dma((15,)), dma((3,)), dma((3,)), dma((3,)), dma((3,)), dma((3,)),
        ],
        compiler_params=pltpu.CompilerParams(
            collective_id=0, has_side_effects=True, vmem_limit_bytes=40 * 2**20
        ),
    )(*[
        pltpu.with_memory_space_constraint(a, pltpu.HBM)
        for a in (table, target_table, centres, coefficients, batch_index)
    ])
    return pl.pallas_call(
        update,
        name="update",
        out_shape=(
            jax.ShapeDtypeStruct((512, 256), F32),
            jax.ShapeDtypeStruct((2, 256, 256), F32),
        ),
        in_specs=[vmem] * 7,
        out_specs=(pl.BlockSpec(memory_space=pl.ANY), pl.BlockSpec(memory_space=pl.ANY)),
        scratch_shapes=[pltpu.VMEM((512, 256), F32), pltpu.VMEM((256, 256), F32), dma((4,))],
        compiler_params=pltpu.CompilerParams(vmem_limit_bytes=24 * 2**20),
    )(*sums)


def solution(mesh):
    in_specs = (
        P("dev", None),
        P("dev", None),
        P(("grp", "dev"), None),
        P(("grp", "dev"), None),
        P(),
    )
    out_specs = (P(("grp", "dev"), None), P())
    return jax.shard_map(body, mesh=mesh, in_specs=in_specs, out_specs=out_specs, check_vma=False)
```

```python
import math

import jax
import jax.numpy as jnp
from jax import lax
from jax.experimental import pallas as pl
from jax.experimental.pallas import tpu as pltpu
from jax.sharding import PartitionSpec as P

MESH = pl.DeviceIdType.MESH
SPREAD = 2.0
RATE = 2.0
NX, NC, NY, NZ = 4, 2, 4, 8
NP = NX * NY
ND = NY * NZ
F32 = jnp.float32
BF16 = jnp.bfloat16
HI = lax.Precision.HIGHEST
NN = (((1,), (0,)), ((), ()))
NT = (((1,), (1,)), ((), ()))
TN = (((0,), (0,)), ((), ()))


def hops(k, n):
    return min(k, n - k)


Z_FAR = sorted(range(1, NZ), key=lambda k: -hops(k, NZ))
Z_NEAR = Z_FAR[::-1]
XY_FAR = sorted(
    [(i, j) for i in range(NX) for j in range(NY) if i or j],
    key=lambda o: -hops(o[0], NX) - hops(o[1], NY),
)
YZ_FAR = sorted(
    [(j, k) for j in range(NY) for k in range(NZ) if j or k],
    key=lambda o: -hops(o[0], NY) - hops(o[1], NZ),
)


def dot(a, b, dims=NN, precision=None):
    return lax.dot_general(a, b, dims, precision=precision, preferred_element_type=F32)


def split(a):
    high = a.astype(BF16)
    return high, (a - high.astype(F32)).astype(BF16)


SLOTS = [0, 2, 6, 3, 5, 4, 1, 7]
GROUPS = [(0, 1), (1, 2), (2, 3), (3, 6)]
SHARE = (16, 16, 24)


def pieces_to_whole(whole):
    halves = [
        jnp.concatenate([whole[h, :, m * 8 : m * 8 + 8, :].reshape(128, 128) for m in range(2)], axis=1)
        for h in range(2)
    ]
    return jnp.concatenate(halves, axis=0)


def column(mass, s):
    tiles = [jnp.broadcast_to(mass[2 * s + m : 2 * s + m + 1, :], (128, 128)).T for m in range(2)]
    tall = jnp.concatenate(tiles, axis=0)
    return jnp.concatenate([tall, tall], axis=1)


def project(resid, m):
    along = jnp.sum(m * resid, axis=0, keepdims=True) / jnp.sum(m * m, axis=0, keepdims=True)
    return resid - m * along


def grad(high, low, proj):
    ph, pw = split(proj)
    return dot(high, ph) + (dot(high, pw) + dot(low, ph))


def exchange(
    table, target, centres, coef, index,
    whole2, turn_out, mass_out, wt_high, wt_low, coef_half, resid0_out,
    tab_v, tgt_v, cen_v, cf_v, idx_v, aims_v, cf_high, cf_low,
    pick, parts, rows, w_high, w_low, wt0_high, wt0_low,
    terms0, terms1, terms2, core_recv0, core_recv1, core_recv2,
    xy_send0, xy_send1, xy_send2, xy_recv0, xy_recv1, xy_recv2,
    z_buf0, z_buf1, z_buf2, whole0, whole1,
    load_sem, a_sent, a_recv, az_recv, axy_recv, ac_recv,
    c_sent, cc_recv, cxy_recv, cz_recv, gxy_recv, gc_recv,
):
    terms, core_recv = (terms0, terms1, terms2), (core_recv0, core_recv1, core_recv2)
    xy_send, xy_recv = (xy_send0, xy_send1, xy_send2), (xy_recv0, xy_recv1, xy_recv2)
    z_buf, whole = (z_buf0, z_buf1, z_buf2), (whole0, whole1, whole2)
    g = lax.axis_index("grp")
    d = lax.axis_index("dev")
    x, c = g // 2, g % 2
    y, z = d // NZ, d % NZ
    p = x * NY + y
    feat = c * NX + x
    chunk = z * NY + y
    radius = math.sqrt(2.0 * 1024)
    scale = 1.0 / math.sqrt(131072)

    xs = [lax.rem(x + k, NX) for k in range(NX)]
    ys = [lax.rem(y + k, NY) for k in range(NY)]
    zs = [lax.rem(z + k, NZ) for k in range(NZ)]
    grps = [v * 2 + c for v in xs]
    bases = [v * NZ for v in ys]

    def at_xy(o):
        return {"grp": grps[o[0]], "dev": bases[o[1]] + z}

    def at_yz(o):
        return {"grp": g, "dev": bases[o[0]] + zs[o[1]]}

    sibling = {"grp": x * 2 + 1 - c, "dev": d}

    def send(src, dst, send_sem, recv_sem, to):
        copy = pltpu.make_async_remote_copy(
            src_ref=src, dst_ref=dst, send_sem=send_sem, recv_sem=recv_sem,
            device_id=to, device_id_type=MESH,
        )
        copy.start()
        return copy

    def wait_bytes(ref, sem):
        pltpu.make_async_copy(ref, ref, sem).wait()

    loads = [
        pltpu.make_async_copy(index, idx_v, load_sem.at[0]),
        pltpu.make_async_copy(
            table.at[:, pl.ds(pl.multiple_of(feat * 128, 128), 128)], tab_v, load_sem.at[1]
        ),
        pltpu.make_async_copy(target, tgt_v, load_sem.at[2]),
        pltpu.make_async_copy(centres, cen_v, load_sem.at[3]),
        pltpu.make_async_copy(coef, cf_v, load_sem.at[4]),
    ]
    for load in loads:
        load.start()

    barrier = pltpu.get_barrier_semaphore()
    greeted = [at_yz(o) for o in YZ_FAR] + [at_xy(o) for o in XY_FAR if o[0]] + [sibling]
    for to in greeted:
        pl.semaphore_signal(barrier, inc=1, device_id=to, device_id_type=MESH)

    loads[0].wait()
    here = lax.broadcasted_iota(jnp.int32, (512, 256), 0) + d * 512
    hot = jnp.concatenate(
        [(here == idx_v[s : s + 1, :]).astype(F32).astype(BF16) for s in range(2)], axis=1
    )
    loads[1].wait()
    pick[...] = dot(hot, tab_v[...], TN).astype(BF16).reshape(ND, 16, 128)
    parts[chunk] = pick[chunk]

    pl.semaphore_wait(barrier, len(greeted))

    for o in YZ_FAR:
        send(
            pick.at[zs[o[1]] * NY + ys[o[0]]], parts.at[chunk], a_sent.at[0], a_recv, at_yz(o)
        )

    loads[2].wait()
    first = (g == 0).astype(F32)
    aims_v[...] = dot(hot, tgt_v[...], TN) * first
    loads[3].wait()
    high, low = split(jnp.square(cen_v[...].astype(F32)))
    ones = jnp.ones((8, 1024), BF16)
    cnorm = (dot(ones, high, NT) + dot(ones, low, NT))[0:1, :]
    loads[4].wait()
    cf_high[...], cf_low[...] = split(cf_v[...])

    wait_bytes(parts.at[pl.ds(0, ND - 1)], a_recv)
    own = jnp.sum(parts[...].astype(F32), axis=0).astype(BF16)
    rows[0, feat, y] = own

    mine = rows.at[0, feat, y]
    for k in Z_FAR:
        slot = SLOTS.index(NZ - k)
        if slot < 6:
            send(mine, rows.at[slot, feat, y], a_sent.at[1], az_recv.at[NZ - k], at_yz((0, k)))
    for n, (b, e) in enumerate(GROUPS):
        for r in SLOTS[b:e]:
            if r:
                wait_bytes(parts.at[0], az_recv.at[r])
        group = rows.at[pl.ds(b, e - b), feat, y]
        for o in XY_FAR:
            send(group, group, a_sent.at[2], axy_recv.at[n], at_xy(o))

    half = pl.ds(c * NX, NX)

    def to_sibling(b, e, n):
        strip = rows.at[pl.ds(b, e - b), half]
        send(strip, strip, a_sent.at[3], ac_recv.at[n], sibling)

    def wait_group(n):
        b, e = GROUPS[n]
        wait_bytes(rows.at[pl.ds(0, e - b), pl.ds(0, 5), pl.ds(0, 3)], axy_recv.at[n])
        if n == 0:
            strip = rows.at[0, half]
            for k, slot in ((1, 7), (7, 6)):
                send(strip, rows.at[slot, half], a_sent.at[4], az_recv.at[NZ - k], at_yz((0, k)))
        to_sibling(b, e, n)

    for n in range(3):
        wait_group(n)
    for slot in (6, 7):
        wait_bytes(rows.at[0, pl.ds(0, NX)], az_recv.at[SLOTS[slot]])
        to_sibling(slot, slot + 1, slot - 2)
    wait_group(3)

    for b, e, arrivals in (
        (0, 3, ((0, 1), (1, 1), (2, 1))),
        (6, 8, ((4, 1), (5, 1))),
        (3, 6, ((3, 3),)),
    ):
        for n, blocks in arrivals:
            wait_bytes(rows.at[pl.ds(0, blocks), pl.ds(0, NX)], ac_recv.at[n])
        some = jnp.concatenate([rows[b:e, f].reshape((e - b) * 64, 128) for f in range(8)], axis=1)
        rnorm = jnp.sum(jnp.square(some.astype(F32)), axis=1, keepdims=True)
        cross = dot(some, cen_v[...], NT)
        dist = jnp.sqrt(jnp.maximum(rnorm + cnorm - 2.0 * cross, 0.0))
        high, low = split(jnp.exp((radius - dist) / SPREAD) * scale)
        for r in range(b, e):
            at = pl.ds(pl.multiple_of(zs[SLOTS[r]] * 64, 64), 64)
            w_high[at, :] = high[(r - b) * 64 : (r - b) * 64 + 64]
            w_low[at, :] = low[(r - b) * 64 : (r - b) * 64 + 64]

    for n in range(3):
        at = pl.ds(256 if n else 0, 256)
        high, low = w_high[at, :], w_low[at, :]
        if n == 1:
            gh, gl = w_high[0:256, :], w_low[0:256, :]
            part = dot(high, gh, NT) + (dot(high, gl, NT) + dot(low, gh, NT))
        else:
            ch, cl = cf_high[...], cf_low[...]
            part = dot(high, ch) + (dot(high, cl) + dot(low, ch)) - aims_v[at, :]
        for h in range(2):
            for m in range(2):
                tiles = part[h * 128 : h * 128 + 128, m * 128 : m * 128 + 128].reshape(NP, 8, 128)
                terms[n][h, :, m * 8 : m * 8 + 8, :] = tiles
        if n == 2:
            ones = jnp.ones((8, 512), BF16)
            mass = dot(ones, w_high[...], NT) + dot(ones, w_low[...], NT)
            mass = jnp.concatenate(
                [mass[0:1, m * 128 : m * 128 + 128] for m in range(4)] + [jnp.zeros((4, 128), F32)],
                axis=0,
            )
            terms[2][:, :, 16:24, :] = jnp.broadcast_to(mass[None, None], (2, NP, 8, 128))
        send(terms[n].at[1 - c], core_recv[n], c_sent.at[n], cc_recv.at[n], sibling)
    for n in range(3):
        wait_bytes(core_recv[n], cc_recv.at[n])
        xy_send[n][...] = terms[n][c] + core_recv[n][...]
        for o in XY_FAR:
            send(
                xy_send[n].at[xs[o[0]] * NY + ys[o[1]]], xy_recv[n].at[p],
                c_sent.at[3 + n], cxy_recv.at[n], at_xy(o),
            )
        xy_recv[n][p] = xy_send[n][p]

    wt0_high[...] = w_high[0:256, :].T
    wt0_low[...] = w_low[0:256, :].T
    wt_high[...] = w_high[256:512, :].T
    wt_low[...] = w_low[256:512, :].T

    for n in range(3):
        wait_bytes(xy_recv[n].at[pl.ds(0, NP - 1)], cxy_recv.at[n])
        z_buf[n][z] = jnp.sum(xy_recv[n][...], axis=0)
        for k in Z_FAR:
            send(z_buf[n].at[z], z_buf[n].at[z], c_sent.at[6 + n], cz_recv.at[n], at_yz((0, k)))
    for n in range(3):
        wait_bytes(z_buf[n].at[pl.ds(0, NZ - 1)], cz_recv.at[n])
        total = jnp.sum(z_buf[n][...], axis=0)
        whole[n][c, p] = total[0:16]
        for o in XY_FAR:
            send(whole[n].at[c, p], whole[n].at[c, p], c_sent.at[9 + n], gxy_recv.at[n], at_xy(o))
        if n == 2:
            mass = total[16:24]
    def whole_to_sibling(n):
        wait_bytes(whole[n].at[0, pl.ds(0, NP - 1)], gxy_recv.at[n])
        send(whole[n].at[c], whole[n].at[c], c_sent.at[12 + n], gc_recv.at[n], sibling)

    m0 = column(mass, 0)
    mass_out[...] = column(mass, 1)
    whole_to_sibling(0)
    whole_to_sibling(1)
    wait_bytes(whole[0].at[0], gc_recv.at[0])
    resid0 = pieces_to_whole(whole0)
    resid0_out[...] = resid0
    proj0 = project(resid0, m0)
    whole_to_sibling(2)
    wait_bytes(whole[1].at[0], gc_recv.at[1])
    turn_out[...] = RATE * dot(pieces_to_whole(whole1), proj0, precision=HI)
    coef_half[...] = cf_v[...] - RATE * grad(wt0_high[...], wt0_low[...], proj0)
    wait_bytes(whole[2].at[0], gc_recv.at[2])

    wait_bytes(parts.at[pl.ds(0, ND - 1)], a_sent.at[0])
    wait_bytes(parts.at[pl.ds(0, 5)], a_sent.at[1])
    wait_bytes(rows.at[pl.ds(0, 6), pl.ds(0, 5), pl.ds(0, 3)], a_sent.at[2])
    wait_bytes(rows.at[:, pl.ds(0, NX)], a_sent.at[3])
    wait_bytes(rows.at[pl.ds(0, 2), pl.ds(0, NX)], a_sent.at[4])
    for n in range(3):
        wait_bytes(core_recv[n], c_sent.at[n])
        wait_bytes(xy_recv[n].at[pl.ds(0, NP - 1)], c_sent.at[3 + n])
        wait_bytes(z_buf[n].at[pl.ds(0, NZ - 1)], c_sent.at[6 + n])
        wait_bytes(whole[n].at[0, pl.ds(0, NP - 1)], c_sent.at[9 + n])
        wait_bytes(whole[n].at[0], c_sent.at[12 + n])


def update(
    whole2, turn, mass, wt_high, wt_low, coef_half, resid0, coef_out, resid_out, coef_v, resid1_v, out_sem
):
    copies = [pltpu.make_async_copy(resid0, resid_out.at[0], out_sem.at[0])]
    copies[0].start()
    resid1 = pieces_to_whole(whole2) - turn[...]
    resid1_v[...] = resid1
    copies.append(pltpu.make_async_copy(resid1_v, resid_out.at[1], out_sem.at[1]))
    copies[1].start()
    proj1 = project(resid1, mass[...])
    for m in range(2):
        at = pl.ds(m * 256, 256)
        coef_v[at, :] = coef_half[at, :] - RATE * grad(wt_high[at, :], wt_low[at, :], proj1)
        copies.append(pltpu.make_async_copy(coef_v.at[at], coef_out.at[at], out_sem.at[2 + m]))
        copies[2 + m].start()
    for copy in copies:
        copy.wait()


def body(table, target_table, centres, coefficients, batch_index):
    dma = pltpu.SemaphoreType.DMA
    vmem = pl.BlockSpec(memory_space=pltpu.VMEM)
    square = jax.ShapeDtypeStruct((256, 256), F32)
    turned = jax.ShapeDtypeStruct((512, 256), BF16)
    per_peer = [pltpu.VMEM((NP, n, 128), F32) for n in SHARE]
    sums = pl.pallas_call(
        exchange,
        name="exchange",
        out_shape=(
            jax.ShapeDtypeStruct((2, NP, 16, 128), F32),
            square,
            square,
            turned,
            turned,
            jax.ShapeDtypeStruct((512, 256), F32),
            square,
        ),
        in_specs=[pl.BlockSpec(memory_space=pl.ANY)] * 5,
        out_specs=(vmem,) * 7,
        scratch_shapes=[
            pltpu.VMEM((512, 128), BF16),
            pltpu.VMEM((512, 256), BF16),
            pltpu.VMEM((512, 1024), BF16),
            pltpu.VMEM((512, 256), F32),
            pltpu.VMEM((2, 256), jnp.int32),
            pltpu.VMEM((512, 256), F32),
            pltpu.VMEM((512, 256), BF16),
            pltpu.VMEM((512, 256), BF16),
            pltpu.VMEM((ND, 16, 128), BF16),
            pltpu.VMEM((ND, 16, 128), BF16),
            pltpu.VMEM((NZ, 8, NY, 16, 128), BF16),
            pltpu.VMEM((512, 512), BF16),
            pltpu.VMEM((512, 512), BF16),
            pltpu.VMEM((512, 256), BF16),
            pltpu.VMEM((512, 256), BF16),
            *[pltpu.VMEM((2, NP, n, 128), F32) for n in SHARE],
            *per_peer, *per_peer, *per_peer,
            *[pltpu.VMEM((NZ, n, 128), F32) for n in SHARE],
            pltpu.VMEM((2, NP, 16, 128), F32),
            pltpu.VMEM((2, NP, 16, 128), F32),
            dma((5,)), dma((5,)), dma, dma((NZ,)), dma((4,)), dma((6,)),
            dma((15,)), dma((3,)), dma((3,)), dma((3,)), dma((3,)), dma((3,)),
        ],
        compiler_params=pltpu.CompilerParams(
            collective_id=0, has_side_effects=True, vmem_limit_bytes=40 * 2**20
        ),
    )(*[
        pltpu.with_memory_space_constraint(a, pltpu.HBM)
        for a in (table, target_table, centres, coefficients, batch_index)
    ])
    return pl.pallas_call(
        update,
        name="update",
        out_shape=(
            jax.ShapeDtypeStruct((512, 256), F32),
            jax.ShapeDtypeStruct((2, 256, 256), F32),
        ),
        in_specs=[vmem] * 7,
        out_specs=(pl.BlockSpec(memory_space=pl.ANY), pl.BlockSpec(memory_space=pl.ANY)),
        scratch_shapes=[pltpu.VMEM((512, 256), F32), pltpu.VMEM((256, 256), F32), dma((4,))],
        compiler_params=pltpu.CompilerParams(vmem_limit_bytes=24 * 2**20),
    )(*sums)


def solution(mesh):
    in_specs = (
        P("dev", None),
        P("dev", None),
        P(("grp", "dev"), None),
        P(("grp", "dev"), None),
        P(),
    )
    out_specs = (P(("grp", "dev"), None), P())
    return jax.shard_map(body, mesh=mesh, in_specs=in_specs, out_specs=out_specs, check_vma=False)
```

```python
import math

import jax
import jax.numpy as jnp
from jax import lax
from jax.experimental import pallas as pl
from jax.experimental.pallas import tpu as pltpu
from jax.sharding import PartitionSpec as P

MESH = pl.DeviceIdType.MESH
SPREAD = 2.0
RATE = 2.0
NX, NC, NY, NZ = 4, 2, 4, 8
NP = NX * NY
ND = NY * NZ
F32 = jnp.float32
BF16 = jnp.bfloat16
HI = lax.Precision.HIGHEST
NN = (((1,), (0,)), ((), ()))
NT = (((1,), (1,)), ((), ()))
TN = (((0,), (0,)), ((), ()))


def hops(k, n):
    return min(k, n - k)


Z_FAR = sorted(range(1, NZ), key=lambda k: -hops(k, NZ))
Z_NEAR = Z_FAR[::-1]
XY_FAR = sorted(
    [(i, j) for i in range(NX) for j in range(NY) if i or j],
    key=lambda o: -hops(o[0], NX) - hops(o[1], NY),
)
YZ_FAR = sorted(
    [(j, k) for j in range(NY) for k in range(NZ) if j or k],
    key=lambda o: -hops(o[0], NY) - hops(o[1], NZ),
)


def dot(a, b, dims=NN, precision=None):
    return lax.dot_general(a, b, dims, precision=precision, preferred_element_type=F32)


def split(a):
    high = a.astype(BF16)
    return high, (a - high.astype(F32)).astype(BF16)


SLOTS = [0, 2, 6, 3, 5, 4, 1, 7]
GROUPS = [(0, 1), (1, 2), (2, 3), (3, 6)]
SHARE = (16, 16, 24)


def pieces_to_whole(whole):
    halves = [
        jnp.concatenate([whole[h, :, m * 8 : m * 8 + 8, :].reshape(128, 128) for m in range(2)], axis=1)
        for h in range(2)
    ]
    return jnp.concatenate(halves, axis=0)


def column(mass, s):
    tiles = [jnp.broadcast_to(mass[h, s : s + 1, :], (128, 128)).T for h in range(2)]
    tall = jnp.concatenate(tiles, axis=0)
    return jnp.concatenate([tall, tall], axis=1)


def project(resid, m):
    along = jnp.sum(m * resid, axis=0, keepdims=True) / jnp.sum(m * m, axis=0, keepdims=True)
    return resid - m * along


def grad(high, low, proj):
    ph, pw = split(proj)
    return dot(high, ph) + (dot(high, pw) + dot(low, ph))


def exchange(
    table, target, centres, coef, index,
    resid1_out, mass_out, wt_high, wt_low, coef_half, resid0_out,
    tab_v, tgt_v, cen_v, cnorm_v, cf_v, idx_v, aims_v, cf_high, cf_low,
    pick, parts, rows, w_high, w_low, w0_high, w0_low, w0_other_high, w0_other_low, w1_high, w1_low,
    wt0_high, wt0_low, mass_all,
    xy_send0, xy_send1, xy_send2, xy_recv0, xy_recv1, xy_recv2,
    z_buf0, z_buf1, z_buf2, whole0, whole1, whole2,
    load_sem, a_sent, a_recv, az_recv, axy_recv, pair_sent, pair_recv,
    c_sent, cxy_recv, cz_recv, gxy_recv, gc_recv,
):
    xy_send, xy_recv = (xy_send0, xy_send1, xy_send2), (xy_recv0, xy_recv1, xy_recv2)
    z_buf, whole = (z_buf0, z_buf1, z_buf2), (whole0, whole1, whole2)
    g = lax.axis_index("grp")
    d = lax.axis_index("dev")
    x, c = g // 2, g % 2
    y, z = d // NZ, d % NZ
    p = x * NY + y
    chunk = z * NY + y
    radius = math.sqrt(2.0 * 1024)
    scale = 1.0 / math.sqrt(131072)

    xs = [lax.rem(x + k, NX) for k in range(NX)]
    ys = [lax.rem(y + k, NY) for k in range(NY)]
    zs = [lax.rem(z + k, NZ) for k in range(NZ)]
    grps = [v * 2 + c for v in xs]
    bases = [v * NZ for v in ys]

    def at_xy(o):
        return {"grp": grps[o[0]], "dev": bases[o[1]] + z}

    def at_yz(o):
        return {"grp": g, "dev": bases[o[0]] + zs[o[1]]}

    sibling = {"grp": x * 2 + 1 - c, "dev": d}

    def send(src, dst, send_sem, recv_sem, to):
        copy = pltpu.make_async_remote_copy(
            src_ref=src, dst_ref=dst, send_sem=send_sem, recv_sem=recv_sem,
            device_id=to, device_id_type=MESH,
        )
        copy.start()
        return copy

    def wait_bytes(ref, sem):
        pltpu.make_async_copy(ref, ref, sem).wait()

    loads = [
        pltpu.make_async_copy(index, idx_v, load_sem.at[0]),
        pltpu.make_async_copy(
            table.at[:, pl.ds(pl.multiple_of(x * 256, 256), 256)], tab_v, load_sem.at[1]
        ),
        pltpu.make_async_copy(target, tgt_v, load_sem.at[2]),
        pltpu.make_async_copy(centres, cen_v.at[c], load_sem.at[3]),
        pltpu.make_async_copy(coef, cf_v, load_sem.at[4]),
    ]
    for load in loads:
        load.start()

    barrier = pltpu.get_barrier_semaphore()
    greeted = [at_yz(o) for o in YZ_FAR] + [at_xy(o) for o in XY_FAR if o[0]] + [sibling]
    for to in greeted:
        pl.semaphore_signal(barrier, inc=1, device_id=to, device_id_type=MESH)

    loads[0].wait()
    here = lax.broadcasted_iota(jnp.int32, (512, 128), 0) + d * 512
    half = pl.ds(pl.multiple_of(c * 128, 128), 128)
    hot = jnp.concatenate(
        [(here == idx_v[s : s + 1, half]).astype(F32).astype(BF16) for s in range(2)], axis=1
    )
    loads[1].wait()
    mine = dot(hot, tab_v[...], TN).astype(BF16).reshape(NZ, 2, 16, 256)
    for k in range(NY):
        pick[:, k] = mine[:, k // 2, :, k % 2 * 128 : k % 2 * 128 + 128]
    parts[chunk] = pick[z, y]

    pl.semaphore_wait(barrier, len(greeted))

    for o in YZ_FAR:
        send(
            pick.at[zs[o[1]], ys[o[0]]], parts.at[chunk], a_sent.at[0], a_recv, at_yz(o)
        )

    def to_sibling(src, dst, n):
        send(src, dst, pair_sent.at[n], pair_recv.at[n], sibling)

    loads[3].wait()
    to_sibling(cen_v.at[c], cen_v.at[c], 0)
    loads[4].wait()
    cf_high[c], cf_low[c] = split(cf_v[...])
    to_sibling(cf_high.at[c], cf_high.at[c], 1)
    to_sibling(cf_low.at[c], cf_low.at[c], 2)
    high, low = split(jnp.square(cen_v[c].astype(F32)))
    ones = jnp.ones((8, 1024), BF16)
    cnorm_v[c] = dot(ones, high, NT) + dot(ones, low, NT)
    to_sibling(cnorm_v.at[c], cnorm_v.at[c], 3)
    loads[2].wait()
    aims_v[...] = dot(hot, tgt_v[...], TN) * (x == 0).astype(F32)

    wait_bytes(parts.at[pl.ds(0, ND - 1)], a_recv)
    own = jnp.sum(parts[...].astype(F32), axis=0).astype(BF16)
    rows[0, x, y] = own

    mine = rows.at[0, x, y]
    for k in Z_FAR:
        slot = SLOTS.index(NZ - k)
        if slot < 6:
            send(mine, rows.at[slot, x, y], a_sent.at[1], az_recv.at[NZ - k], at_yz((0, k)))
    for n, (b, e) in enumerate(GROUPS):
        for r in SLOTS[b:e]:
            if r:
                wait_bytes(parts.at[0], az_recv.at[r])
        group = rows.at[pl.ds(b, e - b), x, y]
        for o in XY_FAR:
            send(group, group, a_sent.at[2 + n // 3], axy_recv.at[n], at_xy(o))

    def arrived(n):
        if n == 3:
            wait_bytes(xy_recv[2].at[pl.ds(0, NP - 1)], axy_recv.at[n])
        else:
            wait_bytes(parts.at[pl.ds(0, NP - 1)], axy_recv.at[n])

    arrived(0)
    for k, slot in ((1, 7), (7, 6)):
        send(rows.at[0], rows.at[slot], a_sent.at[4], az_recv.at[NZ - k], at_yz((0, k)))
    wait_bytes(cen_v.at[0], pair_recv.at[0])
    wait_bytes(cf_high.at[0], pair_recv.at[1])
    wait_bytes(cf_low.at[0], pair_recv.at[2])
    wait_bytes(cnorm_v.at[0], pair_recv.at[3])
    arrived(1)
    arrived(2)

    def values(b, e):
        n = e - b
        some = jnp.concatenate(
            [
                jnp.concatenate(
                    [rows[b:e, i, 2 * q + f].reshape(n * 16, 128) for i in range(NX) for f in range(2)],
                    axis=1,
                )
                for q in range(2)
            ],
            axis=0,
        )
        rnorm = jnp.sum(jnp.square(some.astype(F32)), axis=1, keepdims=True)
        for k in range(NC):
            cross = dot(some, cen_v[k], NT)
            dist = jnp.sqrt(jnp.maximum(rnorm + cnorm_v[k, 0:1, :] - 2.0 * cross, 0.0))
            high, low = split(jnp.exp((radius - dist) / SPREAD) * scale)
            for q in range(2):
                for r in range(b, e):
                    at = pl.ds(pl.multiple_of(zs[SLOTS[r]] * 32 + q * 16, 16), 16)
                    o = (q * n + r - b) * 16
                    w_high[k, at, :] = high[o : o + 16]
                    w_low[k, at, :] = low[o : o + 16]

    values(0, 3)
    for slot in (6, 7):
        wait_bytes(rows.at[0], az_recv.at[SLOTS[slot]])
    values(6, 8)
    arrived(3)
    values(3, 6)

    first, second = pl.ds(0, 128), pl.ds(128, 128)
    to_sibling(w_high.at[:, first], w0_other_high, 4)
    to_sibling(w_low.at[:, first], w0_other_low, 5)

    def put(part, dst, lane):
        dst[:, lane, :] = part.reshape(NP, 8, 128)

    def share_out(n):
        for o in XY_FAR:
            send(
                xy_send[n].at[xs[o[0]] * NY + ys[o[1]]], xy_recv[n].at[p],
                c_sent.at[n], cxy_recv.at[n], at_xy(o),
            )
        xy_recv[n][p] = xy_send[n][p]

    for s in range(2):
        at = pl.ds(s * 128, 128)
        part = -aims_v[at, :]
        for k in range(NC):
            high, low = w_high[k, at, :], w_low[k, at, :]
            ch, cl = cf_high[k], cf_low[k]
            part = part + (dot(high, ch) + (dot(high, cl) + dot(low, ch)))
        for m in range(2):
            put(part[:, m * 128 : m * 128 + 128], xy_send[s], pl.ds(m * 8, 8))
        share_out(s)
    to_sibling(w_high.at[1 - c, second], w1_high.at[c], 6)
    to_sibling(w_low.at[1 - c, second], w1_low.at[c], 7)

    ones = jnp.ones((8, 512), BF16)
    mass = sum(dot(ones, w_high[k], NT) + dot(ones, w_low[k], NT) for k in range(NC))
    mass = jnp.concatenate([mass[0:1, 0:128], mass[0:1, 128:256], jnp.zeros((6, 128), F32)], axis=0)
    xy_send[2][:, 16:24, :] = jnp.broadcast_to(mass[None], (NP, 8, 128))

    def gram(others):
        part = jnp.zeros((128, 128), F32)
        for k in range(NC):
            high, low = w_high[k, second, :], w_low[k, second, :]
            gh, gl = others(k)
            part = part + (dot(high, gh, NT) + (dot(high, gl, NT) + dot(low, gh, NT)))
        return part

    own_lanes = pl.ds(pl.multiple_of(c * 8, 8), 8)
    other_lanes = pl.ds(pl.multiple_of(8 - c * 8, 8), 8)
    put(gram(lambda k: (w_high[k, first, :], w_low[k, first, :])), xy_send[2], own_lanes)
    wait_bytes(w0_other_high, pair_recv.at[4])
    wait_bytes(w0_other_low, pair_recv.at[5])
    put(gram(lambda k: (w0_other_high[k], w0_other_low[k])), xy_send[2], other_lanes)
    share_out(2)

    w0_high[c], w0_low[c] = w_high[c, first, :], w_low[c, first, :]
    w0_high[1 - c], w0_low[1 - c] = w0_other_high[c], w0_other_low[c]
    wt0_high[...] = w0_high[...].reshape(256, 512).T
    wt0_low[...] = w0_low[...].reshape(256, 512).T
    wait_bytes(w1_high.at[0], pair_recv.at[6])
    wait_bytes(w1_low.at[0], pair_recv.at[7])
    wait_bytes(w1_high.at[0], pair_sent.at[6])
    wait_bytes(w1_low.at[0], pair_sent.at[7])
    w1_high[c], w1_low[c] = w_high[c, second, :], w_low[c, second, :]
    wt_high[...] = w1_high[...].reshape(256, 512).T
    wt_low[...] = w1_low[...].reshape(256, 512).T

    for n in range(3):
        wait_bytes(xy_recv[n].at[pl.ds(0, NP - 1)], cxy_recv.at[n])
        z_buf[n][z] = jnp.sum(xy_recv[n][...], axis=0)
        for k in Z_FAR:
            send(z_buf[n].at[z], z_buf[n].at[z], c_sent.at[3 + n], cz_recv.at[n], at_yz((0, k)))
    for n in range(3):
        wait_bytes(z_buf[n].at[pl.ds(0, NZ - 1)], cz_recv.at[n])
        total = jnp.sum(z_buf[n][...], axis=0)
        whole[n][c, p] = total[0:16]
        for o in XY_FAR:
            send(whole[n].at[c, p], whole[n].at[c, p], c_sent.at[6 + n], gxy_recv.at[n], at_xy(o))
        if n == 2:
            mass_all[c] = total[16:24]
            to_sibling(mass_all.at[c], mass_all.at[c], 8)
    def whole_to_sibling(n):
        wait_bytes(whole[n].at[0, pl.ds(0, NP - 1)], gxy_recv.at[n])
        send(whole[n].at[c], whole[n].at[c], c_sent.at[9 + n], gc_recv.at[n], sibling)

    whole_to_sibling(0)
    wait_bytes(mass_all.at[0], pair_recv.at[8])
    m0 = column(mass_all, 0)
    mass_out[...] = column(mass_all, 1)
    whole_to_sibling(1)
    wait_bytes(whole[0].at[0], gc_recv.at[0])
    resid0 = pieces_to_whole(whole0)
    resid0_out[...] = resid0
    proj0 = project(resid0, m0)
    whole_to_sibling(2)
    coef_half[...] = cf_v[...] - RATE * grad(wt0_high[...], wt0_low[...], proj0)
    wait_bytes(whole[1].at[0], gc_recv.at[1])
    wait_bytes(whole[2].at[0], gc_recv.at[2])
    resid1_out[...] = pieces_to_whole(whole1) - RATE * dot(pieces_to_whole(whole2), proj0, precision=HI)

    wait_bytes(parts.at[pl.ds(0, ND - 1)], a_sent.at[0])
    wait_bytes(parts.at[pl.ds(0, 5)], a_sent.at[1])
    wait_bytes(xy_recv[2].at[pl.ds(0, NP - 1)], a_sent.at[2])
    wait_bytes(xy_recv[2].at[pl.ds(0, NP - 1)], a_sent.at[3])
    wait_bytes(rows.at[pl.ds(0, 2)], a_sent.at[4])
    for n, ref in enumerate((
        cen_v.at[0], cf_high.at[0], cf_low.at[0], cnorm_v.at[0], w0_other_high, w0_other_low, None, None,
        mass_all.at[0],
    )):
        if ref is not None:
            wait_bytes(ref, pair_sent.at[n])
    for n in range(3):
        wait_bytes(xy_recv[n].at[pl.ds(0, NP - 1)], c_sent.at[n])
        wait_bytes(z_buf[n].at[pl.ds(0, NZ - 1)], c_sent.at[3 + n])
        wait_bytes(whole[n].at[0, pl.ds(0, NP - 1)], c_sent.at[6 + n])
        wait_bytes(whole[n].at[0], c_sent.at[9 + n])


def update(
    resid1, mass, wt_high, wt_low, coef_half, resid0, coef_out, resid_out, coef_v, out_sem
):
    copies = [pltpu.make_async_copy(resid0, resid_out.at[0], out_sem.at[0])]
    copies[0].start()
    copies.append(pltpu.make_async_copy(resid1, resid_out.at[1], out_sem.at[1]))
    copies[1].start()
    proj1 = project(resid1[...], mass[...])
    for m in range(2):
        at = pl.ds(m * 256, 256)
        coef_v[at, :] = coef_half[at, :] - RATE * grad(wt_high[at, :], wt_low[at, :], proj1)
        copies.append(pltpu.make_async_copy(coef_v.at[at], coef_out.at[at], out_sem.at[2 + m]))
        copies[2 + m].start()
    for copy in copies:
        copy.wait()


def body(table, target_table, centres, coefficients, batch_index):
    dma = pltpu.SemaphoreType.DMA
    vmem = pl.BlockSpec(memory_space=pltpu.VMEM)
    square = jax.ShapeDtypeStruct((256, 256), F32)
    turned = jax.ShapeDtypeStruct((512, 256), BF16)
    per_peer = [pltpu.VMEM((NP, n, 128), F32) for n in SHARE]
    sums = pl.pallas_call(
        exchange,
        name="exchange",
        out_shape=(
            square,
            square,
            turned,
            turned,
            jax.ShapeDtypeStruct((512, 256), F32),
            square,
        ),
        in_specs=[pl.BlockSpec(memory_space=pl.ANY)] * 5,
        out_specs=(vmem,) * 6,
        scratch_shapes=[
            pltpu.VMEM((512, 256), BF16),
            pltpu.VMEM((512, 256), BF16),
            pltpu.VMEM((NC, 512, 1024), BF16),
            pltpu.VMEM((NC, 8, 512), F32),
            pltpu.VMEM((512, 256), F32),
            pltpu.VMEM((2, 256), jnp.int32),
            pltpu.VMEM((256, 256), F32),
            pltpu.VMEM((NC, 512, 256), BF16),
            pltpu.VMEM((NC, 512, 256), BF16),
            pltpu.VMEM((NZ, NY, 16, 128), BF16),
            pltpu.VMEM((ND, 16, 128), BF16),
            pltpu.VMEM((NZ, NX, NY, 16, 128), BF16),
            *[pltpu.VMEM((NC, 256, 512), BF16) for _ in range(2)],
            *[pltpu.VMEM((NC, 128, 512), BF16) for _ in range(6)],
            *[pltpu.VMEM((512, 256), BF16) for _ in range(2)],
            pltpu.VMEM((NC, 8, 128), F32),
            *per_peer, *per_peer,
            *[pltpu.VMEM((NZ, n, 128), F32) for n in SHARE],
            *[pltpu.VMEM((2, NP, 16, 128), F32) for _ in range(3)],
            dma((5,)), dma((5,)), dma, dma((NZ,)), dma((4,)), dma((9,)), dma((9,)),
            dma((12,)), dma((3,)), dma((3,)), dma((3,)), dma((3,)),
        ],
        compiler_params=pltpu.CompilerParams(
            collective_id=0, has_side_effects=True, vmem_limit_bytes=40 * 2**20
        ),
    )(*[
        pltpu.with_memory_space_constraint(a, pltpu.HBM)
        for a in (table, target_table, centres, coefficients, batch_index)
    ])
    return pl.pallas_call(
        update,
        name="update",
        out_shape=(
            jax.ShapeDtypeStruct((512, 256), F32),
            jax.ShapeDtypeStruct((2, 256, 256), F32),
        ),
        in_specs=[vmem] * 6,
        out_specs=(pl.BlockSpec(memory_space=pl.ANY), pl.BlockSpec(memory_space=pl.ANY)),
        scratch_shapes=[pltpu.VMEM((512, 256), F32), dma((4,))],
        compiler_params=pltpu.CompilerParams(vmem_limit_bytes=24 * 2**20),
    )(*sums)


def solution(mesh):
    in_specs = (
        P("dev", None),
        P("dev", None),
        P(("grp", "dev"), None),
        P(("grp", "dev"), None),
        P(),
    )
    out_specs = (P(("grp", "dev"), None), P())
    return jax.shard_map(body, mesh=mesh, in_specs=in_specs, out_specs=out_specs, check_vma=False)
```

```python
import math

import jax
import jax.numpy as jnp
from jax import lax
from jax.experimental import pallas as pl
from jax.experimental.pallas import tpu as pltpu
from jax.sharding import PartitionSpec as P

MESH = pl.DeviceIdType.MESH
SPREAD = 2.0
RATE = 2.0
NX, NC, NY, NZ = 4, 2, 4, 8
NP = NX * NY
ND = NY * NZ
F32 = jnp.float32
BF16 = jnp.bfloat16
HI = lax.Precision.HIGHEST
NN = (((1,), (0,)), ((), ()))
NT = (((1,), (1,)), ((), ()))
TN = (((0,), (0,)), ((), ()))


def hops(k, n):
    return min(k, n - k)


Z_FAR = sorted(range(1, NZ), key=lambda k: -hops(k, NZ))
Z_NEAR = Z_FAR[::-1]
XY_FAR = sorted(
    [(i, j) for i in range(NX) for j in range(NY) if i or j],
    key=lambda o: -hops(o[0], NX) - hops(o[1], NY),
)
YZ_FAR = sorted(
    [(j, k) for j in range(NY) for k in range(NZ) if j or k],
    key=lambda o: -hops(o[0], NY) - hops(o[1], NZ),
)


def dot(a, b, dims=NN, precision=None):
    return lax.dot_general(a, b, dims, precision=precision, preferred_element_type=F32)


def split(a):
    high = a.astype(BF16)
    return high, (a - high.astype(F32)).astype(BF16)


SLOTS = [0, 2, 6, 3, 5, 4, 1, 7]
GROUPS = [(0, 1), (1, 2), (2, 3), (3, 6)]
SHARE = (16, 16, 24)


def rows_of(whole, h):
    return jnp.concatenate([whole[h, :, m * 8 : m * 8 + 8, :].reshape(128, 128) for m in range(2)], axis=1)


def pieces_to_whole(whole):
    return jnp.concatenate([rows_of(whole, h) for h in range(2)], axis=0)


def column(mass, s):
    tiles = [jnp.broadcast_to(mass[h, s : s + 1, :], (128, 128)).T for h in range(2)]
    tall = jnp.concatenate(tiles, axis=0)
    return jnp.concatenate([tall, tall], axis=1)


def project(resid, m):
    along = jnp.sum(m * resid, axis=0, keepdims=True) / jnp.sum(m * m, axis=0, keepdims=True)
    return resid - m * along


def grad(high, low, proj):
    ph, pw = split(proj)
    return dot(high, ph) + (dot(high, pw) + dot(low, ph))


def exchange(
    table, target, centres, coef, index,
    resid1_out, mass_out, wt_high, wt_low, coef_half, resid0_out,
    tab_v, tgt_v, cen_v, cnorm_v, cf_v, idx_v, aims_v, cf_high, cf_low,
    pick, parts, rows, w_high, w_low, w0_high, w0_low, w0_other_high, w0_other_low, w1_high, w1_low,
    wt0_high, wt0_low, mass_all,
    xy_send0, xy_send1, xy_send2, xy_recv0, xy_recv1, xy_recv2,
    z_buf0, z_buf1, z_buf2, whole0, whole1, whole2,
    load_sem, a_sent, a_recv, az_recv, axy_recv, pair_sent, pair_recv,
    c_sent, cxy_recv, cz_recv, gxy_recv, gc_recv,
):
    xy_send, xy_recv = (xy_send0, xy_send1, xy_send2), (xy_recv0, xy_recv1, xy_recv2)
    z_buf, whole = (z_buf0, z_buf1, z_buf2), (whole0, whole1, whole2)
    g = lax.axis_index("grp")
    d = lax.axis_index("dev")
    x, c = g // 2, g % 2
    y, z = d // NZ, d % NZ
    p = x * NY + y
    chunk = z * NY + y
    radius = math.sqrt(2.0 * 1024)
    scale = 1.0 / math.sqrt(131072)

    xs = [lax.rem(x + k, NX) for k in range(NX)]
    ys = [lax.rem(y + k, NY) for k in range(NY)]
    zs = [lax.rem(z + k, NZ) for k in range(NZ)]
    grps = [v * 2 + c for v in xs]
    bases = [v * NZ for v in ys]

    def at_xy(o):
        return {"grp": grps[o[0]], "dev": bases[o[1]] + z}

    def at_yz(o):
        return {"grp": g, "dev": bases[o[0]] + zs[o[1]]}

    sibling = {"grp": x * 2 + 1 - c, "dev": d}

    def send(src, dst, send_sem, recv_sem, to):
        copy = pltpu.make_async_remote_copy(
            src_ref=src, dst_ref=dst, send_sem=send_sem, recv_sem=recv_sem,
            device_id=to, device_id_type=MESH,
        )
        copy.start()
        return copy

    def wait_bytes(ref, sem):
        pltpu.make_async_copy(ref, ref, sem).wait()

    loads = [
        pltpu.make_async_copy(index, idx_v, load_sem.at[0]),
        pltpu.make_async_copy(
            table.at[:, pl.ds(pl.multiple_of(x * 256, 256), 256)], tab_v, load_sem.at[1]
        ),
        pltpu.make_async_copy(target, tgt_v, load_sem.at[2]),
        pltpu.make_async_copy(centres, cen_v.at[c], load_sem.at[3]),
        pltpu.make_async_copy(coef, cf_v, load_sem.at[4]),
    ]
    for load in loads:
        load.start()

    barrier = pltpu.get_barrier_semaphore()
    greeted = [at_yz(o) for o in YZ_FAR] + [at_xy(o) for o in XY_FAR if o[0]] + [sibling]
    for to in greeted:
        pl.semaphore_signal(barrier, inc=1, device_id=to, device_id_type=MESH)

    loads[0].wait()
    here = lax.broadcasted_iota(jnp.int32, (512, 128), 0) + d * 512
    half = pl.ds(pl.multiple_of(c * 128, 128), 128)
    hot = jnp.concatenate(
        [(here == idx_v[s : s + 1, half]).astype(F32).astype(BF16) for s in range(2)], axis=1
    )
    loads[1].wait()
    mine = dot(hot, tab_v[...], TN).astype(BF16).reshape(NZ, 2, 16, 256)
    for k in range(NY):
        pick[:, k] = mine[:, k // 2, :, k % 2 * 128 : k % 2 * 128 + 128]
    parts[chunk] = pick[z, y]

    pl.semaphore_wait(barrier, len(greeted))

    for o in YZ_FAR:
        send(
            pick.at[zs[o[1]], ys[o[0]]], parts.at[chunk], a_sent.at[0], a_recv, at_yz(o)
        )

    def to_sibling(src, dst, n):
        send(src, dst, pair_sent.at[n], pair_recv.at[n], sibling)

    loads[3].wait()
    to_sibling(cen_v.at[c], cen_v.at[c], 0)
    loads[4].wait()
    cf_high[c], cf_low[c] = split(cf_v[...])
    to_sibling(cf_high.at[c], cf_high.at[c], 1)
    to_sibling(cf_low.at[c], cf_low.at[c], 2)
    high, low = split(jnp.square(cen_v[c].astype(F32)))
    ones = jnp.ones((8, 1024), BF16)
    cnorm_v[c] = dot(ones, high, NT) + dot(ones, low, NT)
    to_sibling(cnorm_v.at[c], cnorm_v.at[c], 3)
    loads[2].wait()
    aims_v[...] = dot(hot, tgt_v[...], TN) * (x == 0).astype(F32)

    wait_bytes(parts.at[pl.ds(0, ND - 1)], a_recv)
    own = jnp.sum(parts[...].astype(F32), axis=0).astype(BF16)
    rows[0, x, y] = own

    mine = rows.at[0, x, y]
    for k in Z_FAR:
        slot = SLOTS.index(NZ - k)
        if slot < 6:
            send(mine, rows.at[slot, x, y], a_sent.at[1], az_recv.at[NZ - k], at_yz((0, k)))
    for n, (b, e) in enumerate(GROUPS):
        for r in SLOTS[b:e]:
            if r:
                wait_bytes(parts.at[0], az_recv.at[r])
        group = rows.at[pl.ds(b, e - b), x, y]
        for o in XY_FAR:
            send(group, group, a_sent.at[2 + n // 3], axy_recv.at[n], at_xy(o))

    def arrived(n):
        if n == 3:
            wait_bytes(xy_recv[2].at[pl.ds(0, NP - 1)], axy_recv.at[n])
        else:
            wait_bytes(parts.at[pl.ds(0, NP - 1)], axy_recv.at[n])

    arrived(0)
    for k, slot in ((1, 7), (7, 6)):
        send(rows.at[0], rows.at[slot], a_sent.at[4], az_recv.at[NZ - k], at_yz((0, k)))
    wait_bytes(cen_v.at[0], pair_recv.at[0])
    wait_bytes(cf_high.at[0], pair_recv.at[1])
    wait_bytes(cf_low.at[0], pair_recv.at[2])
    wait_bytes(cnorm_v.at[0], pair_recv.at[3])
    arrived(1)
    arrived(2)

    def values(b, e):
        n = e - b
        some = jnp.concatenate(
            [
                jnp.concatenate(
                    [rows[b:e, i, 2 * q + f].reshape(n * 16, 128) for i in range(NX) for f in range(2)],
                    axis=1,
                )
                for q in range(2)
            ],
            axis=0,
        )
        rnorm = jnp.sum(jnp.square(some.astype(F32)), axis=1, keepdims=True)
        for k in range(NC):
            cross = dot(some, cen_v[k], NT)
            dist = jnp.sqrt(jnp.maximum(rnorm + cnorm_v[k, 0:1, :] - 2.0 * cross, 0.0))
            high, low = split(jnp.exp((radius - dist) / SPREAD) * scale)
            for q in range(2):
                for r in range(b, e):
                    at = pl.ds(pl.multiple_of(zs[SLOTS[r]] * 32 + q * 16, 16), 16)
                    o = (q * n + r - b) * 16
                    w_high[k, at, :] = high[o : o + 16]
                    w_low[k, at, :] = low[o : o + 16]

    values(0, 3)
    for slot in (6, 7):
        wait_bytes(rows.at[0], az_recv.at[SLOTS[slot]])
    values(6, 8)
    arrived(3)
    values(3, 6)

    first, second = pl.ds(0, 128), pl.ds(128, 128)
    to_sibling(w_high.at[:, first], w0_other_high, 4)
    to_sibling(w_low.at[:, first], w0_other_low, 5)

    def put(part, dst, lane):
        dst[:, lane, :] = part.reshape(NP, 8, 128)

    def share_out(n):
        for o in XY_FAR:
            send(
                xy_send[n].at[xs[o[0]] * NY + ys[o[1]]], xy_recv[n].at[p],
                c_sent.at[n], cxy_recv.at[n], at_xy(o),
            )
        xy_recv[n][p] = xy_send[n][p]

    for s in range(2):
        at = pl.ds(s * 128, 128)
        part = -aims_v[at, :]
        for k in range(NC):
            high, low = w_high[k, at, :], w_low[k, at, :]
            ch, cl = cf_high[k], cf_low[k]
            part = part + (dot(high, ch) + (dot(high, cl) + dot(low, ch)))
        for m in range(2):
            put(part[:, m * 128 : m * 128 + 128], xy_send[s], pl.ds(m * 8, 8))
        share_out(s)
    to_sibling(w_high.at[1 - c, second], w1_high.at[c], 6)
    to_sibling(w_low.at[1 - c, second], w1_low.at[c], 7)

    ones = jnp.ones((8, 512), BF16)
    mass = sum(dot(ones, w_high[k], NT) + dot(ones, w_low[k], NT) for k in range(NC))
    mass = jnp.concatenate([mass[0:1, 0:128], mass[0:1, 128:256], jnp.zeros((6, 128), F32)], axis=0)
    xy_send[2][:, 16:24, :] = jnp.broadcast_to(mass[None], (NP, 8, 128))

    def gram(others):
        part = jnp.zeros((128, 128), F32)
        for k in range(NC):
            high, low = w_high[k, second, :], w_low[k, second, :]
            gh, gl = others(k)
            part = part + (dot(high, gh, NT) + (dot(high, gl, NT) + dot(low, gh, NT)))
        return part

    own_lanes = pl.ds(pl.multiple_of(c * 8, 8), 8)
    other_lanes = pl.ds(pl.multiple_of(8 - c * 8, 8), 8)
    put(gram(lambda k: (w_high[k, first, :], w_low[k, first, :])), xy_send[2], own_lanes)
    wait_bytes(w0_other_high, pair_recv.at[4])
    wait_bytes(w0_other_low, pair_recv.at[5])
    put(gram(lambda k: (w0_other_high[k], w0_other_low[k])), xy_send[2], other_lanes)
    share_out(2)

    w0_high[c], w0_low[c] = w_high[c, first, :], w_low[c, first, :]
    w0_high[1 - c], w0_low[1 - c] = w0_other_high[c], w0_other_low[c]
    wt0_high[...] = w0_high[...].reshape(256, 512).T
    wt0_low[...] = w0_low[...].reshape(256, 512).T
    wait_bytes(w1_high.at[0], pair_recv.at[6])
    wait_bytes(w1_low.at[0], pair_recv.at[7])
    wait_bytes(w1_high.at[0], pair_sent.at[6])
    wait_bytes(w1_low.at[0], pair_sent.at[7])
    w1_high[c], w1_low[c] = w_high[c, second, :], w_low[c, second, :]
    wt_high[...] = w1_high[...].reshape(256, 512).T
    wt_low[...] = w1_low[...].reshape(256, 512).T

    for n in range(3):
        wait_bytes(xy_recv[n].at[pl.ds(0, NP - 1)], cxy_recv.at[n])
        z_buf[n][z] = jnp.sum(xy_recv[n][...], axis=0)
        for k in Z_FAR:
            send(z_buf[n].at[z], z_buf[n].at[z], c_sent.at[3 + n], cz_recv.at[n], at_yz((0, k)))
    for n in range(3):
        wait_bytes(z_buf[n].at[pl.ds(0, NZ - 1)], cz_recv.at[n])
        total = jnp.sum(z_buf[n][...], axis=0)
        whole[n][c, p] = total[0:16]
        for o in XY_FAR:
            send(whole[n].at[c, p], whole[n].at[c, p], c_sent.at[6 + n], gxy_recv.at[n], at_xy(o))
        if n == 2:
            mass_all[c] = total[16:24]
            to_sibling(mass_all.at[c], mass_all.at[c], 8)
    wait_bytes(whole[0].at[0, pl.ds(0, NP - 1)], gxy_recv.at[0])
    send(whole[0].at[c], whole[0].at[c], c_sent.at[9], gc_recv.at[0], sibling)
    wait_bytes(mass_all.at[0], pair_recv.at[8])
    m0 = column(mass_all, 0)
    mass_out[...] = column(mass_all, 1)
    wait_bytes(whole[0].at[0], gc_recv.at[0])
    resid0 = pieces_to_whole(whole0)
    resid0_out[...] = resid0
    proj0 = project(resid0, m0)
    wait_bytes(whole[1].at[0, pl.ds(0, NP - 1)], gxy_recv.at[1])
    wait_bytes(whole[2].at[0, pl.ds(0, NP - 1)], gxy_recv.at[2])
    own_rows = pl.ds(pl.multiple_of(c * 128, 128), 128)
    resid1_out[own_rows, :] = rows_of(whole1, c) - RATE * dot(rows_of(whole2, c), proj0, precision=HI)
    send(resid1_out.at[own_rows], resid1_out.at[own_rows], c_sent.at[10], gc_recv.at[1], sibling)
    coef_half[...] = cf_v[...] - RATE * grad(wt0_high[...], wt0_low[...], proj0)
    wait_bytes(resid1_out.at[pl.ds(0, 128)], gc_recv.at[1])

    wait_bytes(parts.at[pl.ds(0, ND - 1)], a_sent.at[0])
    wait_bytes(parts.at[pl.ds(0, 5)], a_sent.at[1])
    wait_bytes(xy_recv[2].at[pl.ds(0, NP - 1)], a_sent.at[2])
    wait_bytes(xy_recv[2].at[pl.ds(0, NP - 1)], a_sent.at[3])
    wait_bytes(rows.at[pl.ds(0, 2)], a_sent.at[4])
    for n, ref in enumerate((
        cen_v.at[0], cf_high.at[0], cf_low.at[0], cnorm_v.at[0], w0_other_high, w0_other_low, None, None,
        mass_all.at[0],
    )):
        if ref is not None:
            wait_bytes(ref, pair_sent.at[n])
    for n in range(3):
        wait_bytes(xy_recv[n].at[pl.ds(0, NP - 1)], c_sent.at[n])
        wait_bytes(z_buf[n].at[pl.ds(0, NZ - 1)], c_sent.at[3 + n])
        wait_bytes(whole[n].at[0, pl.ds(0, NP - 1)], c_sent.at[6 + n])
    wait_bytes(whole[0].at[0], c_sent.at[9])
    wait_bytes(resid1_out.at[pl.ds(0, 128)], c_sent.at[10])


def update(
    resid1, mass, wt_high, wt_low, coef_half, resid0, coef_out, resid_out, coef_v, out_sem
):
    copies = [pltpu.make_async_copy(resid0, resid_out.at[0], out_sem.at[0])]
    copies[0].start()
    copies.append(pltpu.make_async_copy(resid1, resid_out.at[1], out_sem.at[1]))
    copies[1].start()
    proj1 = project(resid1[...], mass[...])
    for m in range(2):
        at = pl.ds(m * 256, 256)
        coef_v[at, :] = coef_half[at, :] - RATE * grad(wt_high[at, :], wt_low[at, :], proj1)
        copies.append(pltpu.make_async_copy(coef_v.at[at], coef_out.at[at], out_sem.at[2 + m]))
        copies[2 + m].start()
    for copy in copies:
        copy.wait()


def body(table, target_table, centres, coefficients, batch_index):
    dma = pltpu.SemaphoreType.DMA
    vmem = pl.BlockSpec(memory_space=pltpu.VMEM)
    square = jax.ShapeDtypeStruct((256, 256), F32)
    turned = jax.ShapeDtypeStruct((512, 256), BF16)
    per_peer = [pltpu.VMEM((NP, n, 128), F32) for n in SHARE]
    sums = pl.pallas_call(
        exchange,
        name="exchange",
        out_shape=(
            square,
            square,
            turned,
            turned,
            jax.ShapeDtypeStruct((512, 256), F32),
            square,
        ),
        in_specs=[pl.BlockSpec(memory_space=pl.ANY)] * 5,
        out_specs=(vmem,) * 6,
        scratch_shapes=[
            pltpu.VMEM((512, 256), BF16),
            pltpu.VMEM((512, 256), BF16),
            pltpu.VMEM((NC, 512, 1024), BF16),
            pltpu.VMEM((NC, 8, 512), F32),
            pltpu.VMEM((512, 256), F32),
            pltpu.VMEM((2, 256), jnp.int32),
            pltpu.VMEM((256, 256), F32),
            pltpu.VMEM((NC, 512, 256), BF16),
            pltpu.VMEM((NC, 512, 256), BF16),
            pltpu.VMEM((NZ, NY, 16, 128), BF16),
            pltpu.VMEM((ND, 16, 128), BF16),
            pltpu.VMEM((NZ, NX, NY, 16, 128), BF16),
            *[pltpu.VMEM((NC, 256, 512), BF16) for _ in range(2)],
            *[pltpu.VMEM((NC, 128, 512), BF16) for _ in range(6)],
            *[pltpu.VMEM((512, 256), BF16) for _ in range(2)],
            pltpu.VMEM((NC, 8, 128), F32),
            *per_peer, *per_peer,
            *[pltpu.VMEM((NZ, n, 128), F32) for n in SHARE],
            *[pltpu.VMEM((2, NP, 16, 128), F32) for _ in range(3)],
            dma((5,)), dma((5,)), dma, dma((NZ,)), dma((4,)), dma((9,)), dma((9,)),
            dma((11,)), dma((3,)), dma((3,)), dma((3,)), dma((2,)),
        ],
        compiler_params=pltpu.CompilerParams(
            collective_id=0, has_side_effects=True, vmem_limit_bytes=40 * 2**20
        ),
    )(*[
        pltpu.with_memory_space_constraint(a, pltpu.HBM)
        for a in (table, target_table, centres, coefficients, batch_index)
    ])
    return pl.pallas_call(
        update,
        name="update",
        out_shape=(
            jax.ShapeDtypeStruct((512, 256), F32),
            jax.ShapeDtypeStruct((2, 256, 256), F32),
        ),
        in_specs=[vmem] * 6,
        out_specs=(pl.BlockSpec(memory_space=pl.ANY), pl.BlockSpec(memory_space=pl.ANY)),
        scratch_shapes=[pltpu.VMEM((512, 256), F32), dma((4,))],
        compiler_params=pltpu.CompilerParams(vmem_limit_bytes=24 * 2**20),
    )(*sums)


def solution(mesh):
    in_specs = (
        P("dev", None),
        P("dev", None),
        P(("grp", "dev"), None),
        P(("grp", "dev"), None),
        P(),
    )
    out_specs = (P(("grp", "dev"), None), P())
    return jax.shard_map(body, mesh=mesh, in_specs=in_specs, out_specs=out_specs, check_vma=False)
```

```python
import math

import jax
import jax.numpy as jnp
from jax import lax
from jax.experimental import pallas as pl
from jax.experimental.pallas import tpu as pltpu
from jax.sharding import PartitionSpec as P

MESH = pl.DeviceIdType.MESH
SPREAD = 2.0
RATE = 2.0
NX, NC, NY, NZ = 4, 2, 4, 8
NP = NX * NY
ND = NY * NZ
F32 = jnp.float32
BF16 = jnp.bfloat16
HI = lax.Precision.HIGHEST
NN = (((1,), (0,)), ((), ()))
NT = (((1,), (1,)), ((), ()))
TN = (((0,), (0,)), ((), ()))


def hops(k, n):
    return min(k, n - k)


Z_FAR = sorted(range(1, NZ), key=lambda k: -hops(k, NZ))
Z_NEAR = Z_FAR[::-1]
XY_FAR = sorted(
    [(i, j) for i in range(NX) for j in range(NY) if i or j],
    key=lambda o: -hops(o[0], NX) - hops(o[1], NY),
)
YZ_FAR = sorted(
    [(j, k) for j in range(NY) for k in range(NZ) if j or k],
    key=lambda o: -hops(o[0], NY) - hops(o[1], NZ),
)


def dot(a, b, dims=NN, precision=None):
    return lax.dot_general(a, b, dims, precision=precision, preferred_element_type=F32)


def split(a):
    high = a.astype(BF16)
    return high, (a - high.astype(F32)).astype(BF16)


SLOTS = [0, 2, 6, 3, 5, 4, 1, 7]
GROUPS = [(0, 1), (1, 2), (2, 3), (3, 6)]
SHARE = (16, 16, 24)


def rows_of(whole, h):
    return jnp.concatenate([whole[h, :, m * 8 : m * 8 + 8, :].reshape(128, 128) for m in range(2)], axis=1)


def pieces_to_whole(whole):
    return jnp.concatenate([rows_of(whole, h) for h in range(2)], axis=0)


def column(mass, s):
    tiles = [jnp.broadcast_to(mass[h, s : s + 1, :], (128, 128)).T for h in range(2)]
    tall = jnp.concatenate(tiles, axis=0)
    return jnp.concatenate([tall, tall], axis=1)


def project(resid, m):
    along = jnp.sum(m * resid, axis=0, keepdims=True) / jnp.sum(m * m, axis=0, keepdims=True)
    return resid - m * along


def grad(high, low, proj):
    ph, pw = split(proj)
    return dot(high, ph) + (dot(high, pw) + dot(low, ph))


def exchange(
    table, target, centres, coef, index,
    resid1_out, mass_out, wt_high, wt_low, coef_half, resid0_out,
    tab_v, tgt_v, cen_v, cnorm_v, cf_v, idx_v, aims_v, cf_high, cf_low,
    pick, parts, rows, w_high, w_low, w0_high, w0_low, w0_other_high, w0_other_low, w1_high, w1_low,
    wt0_high, wt0_low, mass_all,
    xy_send0, xy_send1, xy_send2, xy_recv0, xy_recv1, xy_recv2,
    z_buf0, z_buf1, z_buf2, whole0, whole1, whole2,
    load_sem, a_sent, a_recv, az_recv, axy_recv, pair_sent, pair_recv,
    c_sent, cxy_recv, cz_recv, gxy_recv, gc_recv,
):
    xy_send, xy_recv = (xy_send0, xy_send1, xy_send2), (xy_recv0, xy_recv1, xy_recv2)
    z_buf, whole = (z_buf0, z_buf1, z_buf2), (whole0, whole1, whole2)
    g = lax.axis_index("grp")
    d = lax.axis_index("dev")
    x, c = g // 2, g % 2
    y, z = d // NZ, d % NZ
    p = x * NY + y
    chunk = z * NY + y
    radius = math.sqrt(2.0 * 1024)
    scale = 1.0 / math.sqrt(131072)

    xs = [lax.rem(x + k, NX) for k in range(NX)]
    ys = [lax.rem(y + k, NY) for k in range(NY)]
    zs = [lax.rem(z + k, NZ) for k in range(NZ)]
    grps = [v * 2 + c for v in xs]
    bases = [v * NZ for v in ys]

    def at_xy(o):
        return {"grp": grps[o[0]], "dev": bases[o[1]] + z}

    def at_yz(o):
        return {"grp": g, "dev": bases[o[0]] + zs[o[1]]}

    sibling = {"grp": x * 2 + 1 - c, "dev": d}

    def send(src, dst, send_sem, recv_sem, to):
        copy = pltpu.make_async_remote_copy(
            src_ref=src, dst_ref=dst, send_sem=send_sem, recv_sem=recv_sem,
            device_id=to, device_id_type=MESH,
        )
        copy.start()
        return copy

    def wait_bytes(ref, sem):
        pltpu.make_async_copy(ref, ref, sem).wait()

    loads = [
        pltpu.make_async_copy(index, idx_v, load_sem.at[0]),
        pltpu.make_async_copy(
            table.at[:, pl.ds(pl.multiple_of(x * 256, 256), 256)], tab_v, load_sem.at[1]
        ),
        pltpu.make_async_copy(target, tgt_v, load_sem.at[2]),
        pltpu.make_async_copy(centres, cen_v.at[c], load_sem.at[3]),
        pltpu.make_async_copy(coef, cf_v, load_sem.at[4]),
    ]
    for load in loads:
        load.start()

    barrier = pltpu.get_barrier_semaphore()
    greeted = [at_yz(o) for o in YZ_FAR] + [at_xy(o) for o in XY_FAR if o[0]] + [sibling]
    for to in greeted:
        pl.semaphore_signal(barrier, inc=1, device_id=to, device_id_type=MESH)

    loads[0].wait()
    here = lax.broadcasted_iota(jnp.int32, (512, 128), 0) + d * 512
    half = pl.ds(pl.multiple_of(c * 128, 128), 128)
    hot = jnp.concatenate(
        [(here == idx_v[s : s + 1, half]).astype(F32).astype(BF16) for s in range(2)], axis=1
    )
    loads[1].wait()
    mine = dot(hot, tab_v[...], TN).astype(BF16).reshape(NZ, 2, 16, 256)
    for k in range(NY):
        pick[:, k] = mine[:, k // 2, :, k % 2 * 128 : k % 2 * 128 + 128]
    parts[chunk] = pick[z, y]

    pl.semaphore_wait(barrier, len(greeted))

    for o in YZ_FAR:
        send(
            pick.at[zs[o[1]], ys[o[0]]], parts.at[chunk], a_sent.at[0], a_recv, at_yz(o)
        )

    def to_sibling(src, dst, n):
        send(src, dst, pair_sent.at[n], pair_recv.at[n], sibling)

    loads[3].wait()
    to_sibling(cen_v.at[c], cen_v.at[c], 0)
    loads[4].wait()
    cf_high[c], cf_low[c] = split(cf_v[...])
    to_sibling(cf_high.at[c], cf_high.at[c], 1)
    to_sibling(cf_low.at[c], cf_low.at[c], 2)
    high, low = split(jnp.square(cen_v[c].astype(F32)))
    ones = jnp.ones((8, 1024), BF16)
    cnorm_v[c] = dot(ones, high, NT) + dot(ones, low, NT)
    to_sibling(cnorm_v.at[c], cnorm_v.at[c], 3)
    loads[2].wait()
    aims_v[...] = dot(hot, tgt_v[...], TN) * (x == 0).astype(F32)

    wait_bytes(parts.at[pl.ds(0, ND - 1)], a_recv)
    own = jnp.sum(parts[...].astype(F32), axis=0).astype(BF16)
    rows[0, x, y] = own

    mine = rows.at[0, x, y]
    for k in Z_FAR:
        slot = SLOTS.index(NZ - k)
        if slot < 6:
            send(mine, rows.at[slot, x, y], a_sent.at[1], az_recv.at[NZ - k], at_yz((0, k)))
    for n, (b, e) in enumerate(GROUPS):
        for r in SLOTS[b:e]:
            if r:
                wait_bytes(parts.at[0], az_recv.at[r])
        group = rows.at[pl.ds(b, e - b), x, y]
        for o in XY_FAR:
            send(group, group, a_sent.at[2 + n // 3], axy_recv.at[n], at_xy(o))

    def arrived(n):
        if n == 3:
            wait_bytes(xy_recv[2].at[pl.ds(0, NP - 1)], axy_recv.at[n])
        else:
            wait_bytes(parts.at[pl.ds(0, NP - 1)], axy_recv.at[n])

    arrived(0)
    for k, slot in ((1, 7), (7, 6)):
        send(rows.at[0], rows.at[slot], a_sent.at[4], az_recv.at[NZ - k], at_yz((0, k)))
    wait_bytes(cen_v.at[0], pair_recv.at[0])
    wait_bytes(cf_high.at[0], pair_recv.at[1])
    wait_bytes(cf_low.at[0], pair_recv.at[2])
    wait_bytes(cnorm_v.at[0], pair_recv.at[3])
    arrived(1)
    arrived(2)

    def values(b, e):
        n = e - b
        some = jnp.concatenate(
            [
                jnp.concatenate(
                    [rows[b:e, i, 2 * q + f].reshape(n * 16, 128) for i in range(NX) for f in range(2)],
                    axis=1,
                )
                for q in range(2)
            ],
            axis=0,
        )
        rnorm = jnp.sum(jnp.square(some.astype(F32)), axis=1, keepdims=True)
        for k in range(NC):
            cross = dot(some, cen_v[k], NT)
            dist = jnp.sqrt(jnp.maximum(rnorm + cnorm_v[k, 0:1, :] - 2.0 * cross, 0.0))
            high, low = split(jnp.exp((radius - dist) / SPREAD) * scale)
            for q in range(2):
                for r in range(b, e):
                    at = pl.ds(pl.multiple_of(zs[SLOTS[r]] * 32 + q * 16, 16), 16)
                    o = (q * n + r - b) * 16
                    w_high[k, at, :] = high[o : o + 16]
                    w_low[k, at, :] = low[o : o + 16]

    values(0, 3)
    for slot in (6, 7):
        wait_bytes(rows.at[0], az_recv.at[SLOTS[slot]])
    values(6, 8)
    arrived(3)
    values(3, 6)

    first, second = pl.ds(0, 128), pl.ds(128, 128)
    to_sibling(w_high.at[:, first], w0_other_high, 4)
    to_sibling(w_low.at[:, first], w0_other_low, 5)

    def put(part, dst, lane):
        dst[:, lane, :] = part.reshape(NP, 8, 128)

    def share_out(n):
        for o in XY_FAR:
            send(
                xy_send[n].at[xs[o[0]] * NY + ys[o[1]]], xy_recv[n].at[p],
                c_sent.at[n], cxy_recv.at[n], at_xy(o),
            )
        xy_recv[n][p] = xy_send[n][p]

    part = -aims_v[...]
    for k in range(NC):
        high, low, ch, cl = w_high[k], w_low[k], cf_high[k], cf_low[k]
        part = part + (dot(high, ch) + (dot(high, cl) + dot(low, ch)))
    for n in range(2):
        for m in range(2):
            put(part[n * 128 : n * 128 + 128, m * 128 : m * 128 + 128], xy_send[n], pl.ds(m * 8, 8))
        share_out(n)
    to_sibling(w_high.at[1 - c, second], w1_high.at[c], 6)
    to_sibling(w_low.at[1 - c, second], w1_low.at[c], 7)

    ones = jnp.ones((8, 512), BF16)
    mass = sum(dot(ones, w_high[k], NT) + dot(ones, w_low[k], NT) for k in range(NC))
    mass = jnp.concatenate([mass[0:1, 0:128], mass[0:1, 128:256], jnp.zeros((6, 128), F32)], axis=0)
    xy_send[2][:, 16:24, :] = jnp.broadcast_to(mass[None], (NP, 8, 128))

    def gram(others):
        part = jnp.zeros((128, 128), F32)
        for k in range(NC):
            high, low = w_high[k, second, :], w_low[k, second, :]
            gh, gl = others(k)
            part = part + (dot(high, gh, NT) + (dot(high, gl, NT) + dot(low, gh, NT)))
        return part

    own_lanes = pl.ds(pl.multiple_of(c * 8, 8), 8)
    other_lanes = pl.ds(pl.multiple_of(8 - c * 8, 8), 8)
    put(gram(lambda k: (w_high[k, first, :], w_low[k, first, :])), xy_send[2], own_lanes)
    wait_bytes(w0_other_high, pair_recv.at[4])
    wait_bytes(w0_other_low, pair_recv.at[5])
    put(gram(lambda k: (w0_other_high[k], w0_other_low[k])), xy_send[2], other_lanes)
    share_out(2)

    w0_high[c], w0_low[c] = w_high[c, first, :], w_low[c, first, :]
    w0_high[1 - c], w0_low[1 - c] = w0_other_high[c], w0_other_low[c]
    wt0_high[...] = w0_high[...].reshape(256, 512).T
    wt0_low[...] = w0_low[...].reshape(256, 512).T
    wait_bytes(w1_high.at[0], pair_recv.at[6])
    wait_bytes(w1_low.at[0], pair_recv.at[7])
    wait_bytes(w1_high.at[0], pair_sent.at[6])
    wait_bytes(w1_low.at[0], pair_sent.at[7])
    w1_high[c], w1_low[c] = w_high[c, second, :], w_low[c, second, :]
    wt_high[...] = w1_high[...].reshape(256, 512).T
    wt_low[...] = w1_low[...].reshape(256, 512).T

    for n in range(3):
        wait_bytes(xy_recv[n].at[pl.ds(0, NP - 1)], cxy_recv.at[n])
        z_buf[n][z] = jnp.sum(xy_recv[n][...], axis=0)
        for k in Z_FAR:
            send(z_buf[n].at[z], z_buf[n].at[z], c_sent.at[3 + n], cz_recv.at[n], at_yz((0, k)))
    for n in range(3):
        wait_bytes(z_buf[n].at[pl.ds(0, NZ - 1)], cz_recv.at[n])
        total = jnp.sum(z_buf[n][...], axis=0)
        whole[n][c, p] = total[0:16]
        for o in XY_FAR:
            send(whole[n].at[c, p], whole[n].at[c, p], c_sent.at[6 + n], gxy_recv.at[n], at_xy(o))
        if n == 2:
            mass_all[c] = total[16:24]
            to_sibling(mass_all.at[c], mass_all.at[c], 8)
    wait_bytes(whole[0].at[0, pl.ds(0, NP - 1)], gxy_recv.at[0])
    send(whole[0].at[c], whole[0].at[c], c_sent.at[9], gc_recv.at[0], sibling)
    wait_bytes(mass_all.at[0], pair_recv.at[8])
    m0 = column(mass_all, 0)
    mass_out[...] = column(mass_all, 1)
    wait_bytes(whole[0].at[0], gc_recv.at[0])
    resid0 = pieces_to_whole(whole0)
    resid0_out[...] = resid0
    proj0 = project(resid0, m0)
    wait_bytes(whole[1].at[0, pl.ds(0, NP - 1)], gxy_recv.at[1])
    wait_bytes(whole[2].at[0, pl.ds(0, NP - 1)], gxy_recv.at[2])
    own_rows = pl.ds(pl.multiple_of(c * 128, 128), 128)
    resid1_out[own_rows, :] = rows_of(whole1, c) - RATE * dot(rows_of(whole2, c), proj0, precision=HI)
    send(resid1_out.at[own_rows], resid1_out.at[own_rows], c_sent.at[10], gc_recv.at[1], sibling)
    coef_half[...] = cf_v[...] - RATE * grad(wt0_high[...], wt0_low[...], proj0)
    wait_bytes(resid1_out.at[pl.ds(0, 128)], gc_recv.at[1])

    wait_bytes(parts.at[pl.ds(0, ND - 1)], a_sent.at[0])
    wait_bytes(parts.at[pl.ds(0, 5)], a_sent.at[1])
    wait_bytes(xy_recv[2].at[pl.ds(0, NP - 1)], a_sent.at[2])
    wait_bytes(xy_recv[2].at[pl.ds(0, NP - 1)], a_sent.at[3])
    wait_bytes(rows.at[pl.ds(0, 2)], a_sent.at[4])
    for n, ref in enumerate((
        cen_v.at[0], cf_high.at[0], cf_low.at[0], cnorm_v.at[0], w0_other_high, w0_other_low, None, None,
        mass_all.at[0],
    )):
        if ref is not None:
            wait_bytes(ref, pair_sent.at[n])
    for n in range(3):
        wait_bytes(xy_recv[n].at[pl.ds(0, NP - 1)], c_sent.at[n])
        wait_bytes(z_buf[n].at[pl.ds(0, NZ - 1)], c_sent.at[3 + n])
        wait_bytes(whole[n].at[0, pl.ds(0, NP - 1)], c_sent.at[6 + n])
    wait_bytes(whole[0].at[0], c_sent.at[9])
    wait_bytes(resid1_out.at[pl.ds(0, 128)], c_sent.at[10])


def update(
    resid1, mass, wt_high, wt_low, coef_half, resid0, coef_out, resid_out, coef_v, out_sem
):
    copies = [pltpu.make_async_copy(resid0, resid_out.at[0], out_sem.at[0])]
    copies[0].start()
    copies.append(pltpu.make_async_copy(resid1, resid_out.at[1], out_sem.at[1]))
    copies[1].start()
    proj1 = project(resid1[...], mass[...])
    for m in range(2):
        at = pl.ds(m * 256, 256)
        coef_v[at, :] = coef_half[at, :] - RATE * grad(wt_high[at, :], wt_low[at, :], proj1)
        copies.append(pltpu.make_async_copy(coef_v.at[at], coef_out.at[at], out_sem.at[2 + m]))
        copies[2 + m].start()
    for copy in copies:
        copy.wait()


def body(table, target_table, centres, coefficients, batch_index):
    dma = pltpu.SemaphoreType.DMA
    vmem = pl.BlockSpec(memory_space=pltpu.VMEM)
    square = jax.ShapeDtypeStruct((256, 256), F32)
    turned = jax.ShapeDtypeStruct((512, 256), BF16)
    per_peer = [pltpu.VMEM((NP, n, 128), F32) for n in SHARE]
    sums = pl.pallas_call(
        exchange,
        name="exchange",
        out_shape=(
            square,
            square,
            turned,
            turned,
            jax.ShapeDtypeStruct((512, 256), F32),
            square,
        ),
        in_specs=[pl.BlockSpec(memory_space=pl.ANY)] * 5,
        out_specs=(vmem,) * 6,
        scratch_shapes=[
            pltpu.VMEM((512, 256), BF16),
            pltpu.VMEM((512, 256), BF16),
            pltpu.VMEM((NC, 512, 1024), BF16),
            pltpu.VMEM((NC, 8, 512), F32),
            pltpu.VMEM((512, 256), F32),
            pltpu.VMEM((2, 256), jnp.int32),
            pltpu.VMEM((256, 256), F32),
            pltpu.VMEM((NC, 512, 256), BF16),
            pltpu.VMEM((NC, 512, 256), BF16),
            pltpu.VMEM((NZ, NY, 16, 128), BF16),
            pltpu.VMEM((ND, 16, 128), BF16),
            pltpu.VMEM((NZ, NX, NY, 16, 128), BF16),
            *[pltpu.VMEM((NC, 256, 512), BF16) for _ in range(2)],
            *[pltpu.VMEM((NC, 128, 512), BF16) for _ in range(6)],
            *[pltpu.VMEM((512, 256), BF16) for _ in range(2)],
            pltpu.VMEM((NC, 8, 128), F32),
            *per_peer, *per_peer,
            *[pltpu.VMEM((NZ, n, 128), F32) for n in SHARE],
            *[pltpu.VMEM((2, NP, 16, 128), F32) for _ in range(3)],
            dma((5,)), dma((5,)), dma, dma((NZ,)), dma((4,)), dma((9,)), dma((9,)),
            dma((11,)), dma((3,)), dma((3,)), dma((3,)), dma((2,)),
        ],
        compiler_params=pltpu.CompilerParams(
            collective_id=0, has_side_effects=True, vmem_limit_bytes=40 * 2**20
        ),
    )(*[
        pltpu.with_memory_space_constraint(a, pltpu.HBM)
        for a in (table, target_table, centres, coefficients, batch_index)
    ])
    return pl.pallas_call(
        update,
        name="update",
        out_shape=(
            jax.ShapeDtypeStruct((512, 256), F32),
            jax.ShapeDtypeStruct((2, 256, 256), F32),
        ),
        in_specs=[vmem] * 6,
        out_specs=(pl.BlockSpec(memory_space=pl.ANY), pl.BlockSpec(memory_space=pl.ANY)),
        scratch_shapes=[pltpu.VMEM((512, 256), F32), dma((4,))],
        compiler_params=pltpu.CompilerParams(vmem_limit_bytes=24 * 2**20),
    )(*sums)


def solution(mesh):
    in_specs = (
        P("dev", None),
        P("dev", None),
        P(("grp", "dev"), None),
        P(("grp", "dev"), None),
        P(),
    )
    out_specs = (P(("grp", "dev"), None), P())
    return jax.shard_map(body, mesh=mesh, in_specs=in_specs, out_specs=out_specs, check_vma=False)
```

```python
import math

import jax
import jax.numpy as jnp
from jax import lax
from jax.experimental import pallas as pl
from jax.experimental.pallas import tpu as pltpu
from jax.sharding import PartitionSpec as P

MESH = pl.DeviceIdType.MESH
SPREAD = 2.0
RATE = 2.0
NX, NC, NY, NZ = 4, 2, 4, 8
NP = NX * NY
ND = NY * NZ
F32 = jnp.float32
BF16 = jnp.bfloat16
HI = lax.Precision.HIGHEST
NN = (((1,), (0,)), ((), ()))
NT = (((1,), (1,)), ((), ()))
TN = (((0,), (0,)), ((), ()))


def hops(k, n):
    return min(k, n - k)


Z_FAR = sorted(range(1, NZ), key=lambda k: -hops(k, NZ))
Z_NEAR = Z_FAR[::-1]
XY_FAR = sorted(
    [(i, j) for i in range(NX) for j in range(NY) if i or j],
    key=lambda o: -hops(o[0], NX) - hops(o[1], NY),
)
YZ_FAR = sorted(
    [(j, k) for j in range(NY) for k in range(NZ) if j or k],
    key=lambda o: -hops(o[0], NY) - hops(o[1], NZ),
)


def dot(a, b, dims=NN, precision=None):
    return lax.dot_general(a, b, dims, precision=precision, preferred_element_type=F32)


def split(a):
    high = a.astype(BF16)
    return high, (a - high.astype(F32)).astype(BF16)


SLOTS = [0, 2, 6, 3, 5, 4, 1, 7]
GROUPS = [(0, 1), (1, 2), (2, 3), (3, 6)]
SHARE = (16, 16, 24)


def rows_of(whole, h):
    return jnp.concatenate([whole[h, :, m * 8 : m * 8 + 8, :].reshape(128, 128) for m in range(2)], axis=1)


def pieces_to_whole(whole):
    return jnp.concatenate([rows_of(whole, h) for h in range(2)], axis=0)


def column(mass, s):
    tiles = [jnp.broadcast_to(mass[h, s : s + 1, :], (128, 128)).T for h in range(2)]
    tall = jnp.concatenate(tiles, axis=0)
    return jnp.concatenate([tall, tall], axis=1)


def project(resid, m):
    along = jnp.sum(m * resid, axis=0, keepdims=True) / jnp.sum(m * m, axis=0, keepdims=True)
    return resid - m * along


def grad(high, low, proj):
    ph, pw = split(proj)
    return dot(high, ph) + (dot(high, pw) + dot(low, ph))


def exchange(
    table, target, centres, coef, index,
    resid1_out, mass_out, wt_high, wt_low, coef_half, resid0_out,
    tab_v, tgt_v, cen_v, cnorm_v, cf_v, idx_v, aims_v, cf_high, cf_low,
    pick, parts, rows, w_high, w_low, w0_high, w0_low, w0_other_high, w0_other_low, w1_high, w1_low,
    wt0_high, wt0_low, mass_all,
    xy_send0, xy_send1, xy_send2, xy_recv0, xy_recv1, xy_recv2,
    z_buf0, z_buf1, z_buf2, whole0, whole1, whole2,
    load_sem, a_sent, a_recv, az_recv, axy_recv, pair_sent, pair_recv,
    c_sent, cxy_recv, cz_recv, gxy_recv, gc_recv,
):
    xy_send, xy_recv = (xy_send0, xy_send1, xy_send2), (xy_recv0, xy_recv1, xy_recv2)
    z_buf, whole = (z_buf0, z_buf1, z_buf2), (whole0, whole1, whole2)
    g = lax.axis_index("grp")
    d = lax.axis_index("dev")
    x, c = g // 2, g % 2
    y, z = d // NZ, d % NZ
    p = x * NY + y
    chunk = z * NY + y
    radius = math.sqrt(2.0 * 1024)
    scale = 1.0 / math.sqrt(131072)

    xs = [lax.rem(x + k, NX) for k in range(NX)]
    ys = [lax.rem(y + k, NY) for k in range(NY)]
    zs = [lax.rem(z + k, NZ) for k in range(NZ)]
    grps = [v * 2 + c for v in xs]
    bases = [v * NZ for v in ys]

    def at_xy(o):
        return {"grp": grps[o[0]], "dev": bases[o[1]] + z}

    def at_yz(o):
        return {"grp": g, "dev": bases[o[0]] + zs[o[1]]}

    sibling = {"grp": x * 2 + 1 - c, "dev": d}

    def send(src, dst, send_sem, recv_sem, to):
        copy = pltpu.make_async_remote_copy(
            src_ref=src, dst_ref=dst, send_sem=send_sem, recv_sem=recv_sem,
            device_id=to, device_id_type=MESH,
        )
        copy.start()
        return copy

    def wait_bytes(ref, sem):
        pltpu.make_async_copy(ref, ref, sem).wait()

    barrier = pltpu.get_barrier_semaphore()
    greeted = [at_yz(o) for o in YZ_FAR] + [at_xy(o) for o in XY_FAR if o[0]] + [sibling]
    for to in greeted:
        pl.semaphore_signal(barrier, inc=1, device_id=to, device_id_type=MESH)

    loads = [
        pltpu.make_async_copy(index, idx_v, load_sem.at[0]),
        pltpu.make_async_copy(
            table.at[:, pl.ds(pl.multiple_of(x * 256, 256), 256)], tab_v, load_sem.at[1]
        ),
        pltpu.make_async_copy(target, tgt_v, load_sem.at[2]),
        pltpu.make_async_copy(centres, cen_v.at[c], load_sem.at[3]),
        pltpu.make_async_copy(coef, cf_v, load_sem.at[4]),
    ]
    for load in loads:
        load.start()

    loads[0].wait()
    here = lax.broadcasted_iota(jnp.int32, (512, 128), 0) + d * 512
    half = pl.ds(pl.multiple_of(c * 128, 128), 128)
    hot = jnp.concatenate(
        [(here == idx_v[s : s + 1, half]).astype(F32).astype(BF16) for s in range(2)], axis=1
    )
    loads[1].wait()
    mine = dot(hot, tab_v[...], TN).astype(BF16).reshape(NZ, 2, 16, 256)
    for k in range(NY):
        pick[:, k] = mine[:, k // 2, :, k % 2 * 128 : k % 2 * 128 + 128]
    parts[chunk] = pick[z, y]

    pl.semaphore_wait(barrier, len(greeted))

    for o in YZ_FAR:
        send(
            pick.at[zs[o[1]], ys[o[0]]], parts.at[chunk], a_sent.at[0], a_recv, at_yz(o)
        )

    def to_sibling(src, dst, n):
        send(src, dst, pair_sent.at[n], pair_recv.at[n], sibling)

    loads[3].wait()
    to_sibling(cen_v.at[c], cen_v.at[c], 0)
    loads[4].wait()
    cf_high[c], cf_low[c] = split(cf_v[...])
    to_sibling(cf_high.at[c], cf_high.at[c], 1)
    to_sibling(cf_low.at[c], cf_low.at[c], 2)
    high, low = split(jnp.square(cen_v[c].astype(F32)))
    ones = jnp.ones((8, 1024), BF16)
    cnorm_v[c] = dot(ones, high, NT) + dot(ones, low, NT)
    to_sibling(cnorm_v.at[c], cnorm_v.at[c], 3)
    loads[2].wait()
    aims_v[...] = dot(hot, tgt_v[...], TN) * (x == 0).astype(F32)

    wait_bytes(parts.at[pl.ds(0, ND - 1)], a_recv)
    own = jnp.sum(parts[...].astype(F32), axis=0).astype(BF16)
    rows[0, x, y] = own

    mine = rows.at[0, x, y]
    for k in Z_FAR:
        slot = SLOTS.index(NZ - k)
        if slot < 6:
            send(mine, rows.at[slot, x, y], a_sent.at[1], az_recv.at[NZ - k], at_yz((0, k)))
    for n, (b, e) in enumerate(GROUPS):
        for r in SLOTS[b:e]:
            if r:
                wait_bytes(parts.at[0], az_recv.at[r])
        group = rows.at[pl.ds(b, e - b), x, y]
        for o in XY_FAR:
            send(group, group, a_sent.at[2 + n // 3], axy_recv.at[n], at_xy(o))

    def arrived(n):
        if n == 3:
            wait_bytes(xy_recv[2].at[pl.ds(0, NP - 1)], axy_recv.at[n])
        else:
            wait_bytes(parts.at[pl.ds(0, NP - 1)], axy_recv.at[n])

    arrived(0)
    for k, slot in ((1, 7), (7, 6)):
        send(rows.at[0], rows.at[slot], a_sent.at[4], az_recv.at[NZ - k], at_yz((0, k)))
    wait_bytes(cen_v.at[0], pair_recv.at[0])
    wait_bytes(cf_high.at[0], pair_recv.at[1])
    wait_bytes(cf_low.at[0], pair_recv.at[2])
    wait_bytes(cnorm_v.at[0], pair_recv.at[3])
    arrived(1)
    arrived(2)

    def values(b, e):
        n = e - b
        some = jnp.concatenate(
            [
                jnp.concatenate(
                    [rows[b:e, i, 2 * q + f].reshape(n * 16, 128) for i in range(NX) for f in range(2)],
                    axis=1,
                )
                for q in range(2)
            ],
            axis=0,
        )
        rnorm = jnp.sum(jnp.square(some.astype(F32)), axis=1, keepdims=True)
        for k in range(NC):
            cross = dot(some, cen_v[k], NT)
            dist = jnp.sqrt(jnp.maximum(rnorm + cnorm_v[k, 0:1, :] - 2.0 * cross, 0.0))
            high, low = split(jnp.exp((radius - dist) / SPREAD) * scale)
            for q in range(2):
                for r in range(b, e):
                    at = pl.ds(pl.multiple_of(zs[SLOTS[r]] * 32 + q * 16, 16), 16)
                    o = (q * n + r - b) * 16
                    w_high[k, at, :] = high[o : o + 16]
                    w_low[k, at, :] = low[o : o + 16]

    values(0, 3)
    for slot in (6, 7):
        wait_bytes(rows.at[0], az_recv.at[SLOTS[slot]])
    values(6, 8)
    arrived(3)
    values(3, 6)

    first, second = pl.ds(0, 128), pl.ds(128, 128)
    to_sibling(w_high.at[:, first], w0_other_high, 4)
    to_sibling(w_low.at[:, first], w0_other_low, 5)

    def put(part, dst, lane):
        dst[:, lane, :] = part.reshape(NP, 8, 128)

    def share_out(n):
        for o in XY_FAR:
            send(
                xy_send[n].at[xs[o[0]] * NY + ys[o[1]]], xy_recv[n].at[p],
                c_sent.at[n], cxy_recv.at[n], at_xy(o),
            )
        xy_recv[n][p] = xy_send[n][p]

    for s in range(2):
        at = pl.ds(s * 128, 128)
        part = -aims_v[at, :]
        for k in range(NC):
            high, low = w_high[k, at, :], w_low[k, at, :]
            ch, cl = cf_high[k], cf_low[k]
            part = part + (dot(high, ch) + (dot(high, cl) + dot(low, ch)))
        for m in range(2):
            put(part[:, m * 128 : m * 128 + 128], xy_send[s], pl.ds(m * 8, 8))
        share_out(s)
    to_sibling(w_high.at[1 - c, second], w1_high.at[c], 6)
    to_sibling(w_low.at[1 - c, second], w1_low.at[c], 7)

    ones = jnp.ones((8, 512), BF16)
    mass = sum(dot(ones, w_high[k], NT) + dot(ones, w_low[k], NT) for k in range(NC))
    mass = jnp.concatenate([mass[0:1, 0:128], mass[0:1, 128:256], jnp.zeros((6, 128), F32)], axis=0)
    xy_send[2][:, 16:24, :] = jnp.broadcast_to(mass[None], (NP, 8, 128))

    def gram(others):
        part = jnp.zeros((128, 128), F32)
        for k in range(NC):
            high, low = w_high[k, second, :], w_low[k, second, :]
            gh, gl = others(k)
            part = part + (dot(high, gh, NT) + (dot(high, gl, NT) + dot(low, gh, NT)))
        return part

    own_lanes = pl.ds(pl.multiple_of(c * 8, 8), 8)
    other_lanes = pl.ds(pl.multiple_of(8 - c * 8, 8), 8)
    put(gram(lambda k: (w_high[k, first, :], w_low[k, first, :])), xy_send[2], own_lanes)
    wait_bytes(w0_other_high, pair_recv.at[4])
    wait_bytes(w0_other_low, pair_recv.at[5])
    put(gram(lambda k: (w0_other_high[k], w0_other_low[k])), xy_send[2], other_lanes)
    share_out(2)

    w0_high[c], w0_low[c] = w_high[c, first, :], w_low[c, first, :]
    w0_high[1 - c], w0_low[1 - c] = w0_other_high[c], w0_other_low[c]
    wt0_high[...] = w0_high[...].reshape(256, 512).T
    wt0_low[...] = w0_low[...].reshape(256, 512).T
    wait_bytes(w1_high.at[0], pair_recv.at[6])
    wait_bytes(w1_low.at[0], pair_recv.at[7])
    wait_bytes(w1_high.at[0], pair_sent.at[6])
    wait_bytes(w1_low.at[0], pair_sent.at[7])
    w1_high[c], w1_low[c] = w_high[c, second, :], w_low[c, second, :]
    wt_high[...] = w1_high[...].reshape(256, 512).T
    wt_low[...] = w1_low[...].reshape(256, 512).T

    for n in range(3):
        wait_bytes(xy_recv[n].at[pl.ds(0, NP - 1)], cxy_recv.at[n])
        z_buf[n][z] = jnp.sum(xy_recv[n][...], axis=0)
        for k in Z_FAR:
            send(z_buf[n].at[z], z_buf[n].at[z], c_sent.at[3 + n], cz_recv.at[n], at_yz((0, k)))
    for n in range(3):
        wait_bytes(z_buf[n].at[pl.ds(0, NZ - 1)], cz_recv.at[n])
        total = jnp.sum(z_buf[n][...], axis=0)
        whole[n][c, p] = total[0:16]
        for o in XY_FAR:
            send(whole[n].at[c, p], whole[n].at[c, p], c_sent.at[6 + n], gxy_recv.at[n], at_xy(o))
        if n == 2:
            mass_all[c] = total[16:24]
            to_sibling(mass_all.at[c], mass_all.at[c], 8)
    wait_bytes(whole[0].at[0, pl.ds(0, NP - 1)], gxy_recv.at[0])
    send(whole[0].at[c], whole[0].at[c], c_sent.at[9], gc_recv.at[0], sibling)
    wait_bytes(mass_all.at[0], pair_recv.at[8])
    m0 = column(mass_all, 0)
    mass_out[...] = column(mass_all, 1)
    wait_bytes(whole[0].at[0], gc_recv.at[0])
    resid0 = pieces_to_whole(whole0)
    resid0_out[...] = resid0
    proj0 = project(resid0, m0)
    wait_bytes(whole[1].at[0, pl.ds(0, NP - 1)], gxy_recv.at[1])
    wait_bytes(whole[2].at[0, pl.ds(0, NP - 1)], gxy_recv.at[2])
    own_rows = pl.ds(pl.multiple_of(c * 128, 128), 128)
    resid1_out[own_rows, :] = rows_of(whole1, c) - RATE * dot(rows_of(whole2, c), proj0, precision=HI)
    send(resid1_out.at[own_rows], resid1_out.at[own_rows], c_sent.at[10], gc_recv.at[1], sibling)
    coef_half[...] = cf_v[...] - RATE * grad(wt0_high[...], wt0_low[...], proj0)
    wait_bytes(resid1_out.at[pl.ds(0, 128)], gc_recv.at[1])

    wait_bytes(parts.at[pl.ds(0, ND - 1)], a_sent.at[0])
    wait_bytes(parts.at[pl.ds(0, 5)], a_sent.at[1])
    wait_bytes(xy_recv[2].at[pl.ds(0, NP - 1)], a_sent.at[2])
    wait_bytes(xy_recv[2].at[pl.ds(0, NP - 1)], a_sent.at[3])
    wait_bytes(rows.at[pl.ds(0, 2)], a_sent.at[4])
    for n, ref in enumerate((
        cen_v.at[0], cf_high.at[0], cf_low.at[0], cnorm_v.at[0], w0_other_high, w0_other_low, None, None,
        mass_all.at[0],
    )):
        if ref is not None:
            wait_bytes(ref, pair_sent.at[n])
    for n in range(3):
        wait_bytes(xy_recv[n].at[pl.ds(0, NP - 1)], c_sent.at[n])
        wait_bytes(z_buf[n].at[pl.ds(0, NZ - 1)], c_sent.at[3 + n])
        wait_bytes(whole[n].at[0, pl.ds(0, NP - 1)], c_sent.at[6 + n])
    wait_bytes(whole[0].at[0], c_sent.at[9])
    wait_bytes(resid1_out.at[pl.ds(0, 128)], c_sent.at[10])


def update(
    resid1, mass, wt_high, wt_low, coef_half, resid0, coef_out, resid_out, coef_v, out_sem
):
    copies = [pltpu.make_async_copy(resid0, resid_out.at[0], out_sem.at[0])]
    copies[0].start()
    copies.append(pltpu.make_async_copy(resid1, resid_out.at[1], out_sem.at[1]))
    copies[1].start()
    proj1 = project(resid1[...], mass[...])
    for m in range(2):
        at = pl.ds(m * 256, 256)
        coef_v[at, :] = coef_half[at, :] - RATE * grad(wt_high[at, :], wt_low[at, :], proj1)
        copies.append(pltpu.make_async_copy(coef_v.at[at], coef_out.at[at], out_sem.at[2 + m]))
        copies[2 + m].start()
    for copy in copies:
        copy.wait()


def body(table, target_table, centres, coefficients, batch_index):
    dma = pltpu.SemaphoreType.DMA
    vmem = pl.BlockSpec(memory_space=pltpu.VMEM)
    square = jax.ShapeDtypeStruct((256, 256), F32)
    turned = jax.ShapeDtypeStruct((512, 256), BF16)
    per_peer = [pltpu.VMEM((NP, n, 128), F32) for n in SHARE]
    sums = pl.pallas_call(
        exchange,
        name="exchange",
        out_shape=(
            square,
            square,
            turned,
            turned,
            jax.ShapeDtypeStruct((512, 256), F32),
            square,
        ),
        in_specs=[pl.BlockSpec(memory_space=pl.ANY)] * 5,
        out_specs=(vmem,) * 6,
        scratch_shapes=[
            pltpu.VMEM((512, 256), BF16),
            pltpu.VMEM((512, 256), BF16),
            pltpu.VMEM((NC, 512, 1024), BF16),
            pltpu.VMEM((NC, 8, 512), F32),
            pltpu.VMEM((512, 256), F32),
            pltpu.VMEM((2, 256), jnp.int32),
            pltpu.VMEM((256, 256), F32),
            pltpu.VMEM((NC, 512, 256), BF16),
            pltpu.VMEM((NC, 512, 256), BF16),
            pltpu.VMEM((NZ, NY, 16, 128), BF16),
            pltpu.VMEM((ND, 16, 128), BF16),
            pltpu.VMEM((NZ, NX, NY, 16, 128), BF16),
            *[pltpu.VMEM((NC, 256, 512), BF16) for _ in range(2)],
            *[pltpu.VMEM((NC, 128, 512), BF16) for _ in range(6)],
            *[pltpu.VMEM((512, 256), BF16) for _ in range(2)],
            pltpu.VMEM((NC, 8, 128), F32),
            *per_peer, *per_peer,
            *[pltpu.VMEM((NZ, n, 128), F32) for n in SHARE],
            *[pltpu.VMEM((2, NP, 16, 128), F32) for _ in range(3)],
            dma((5,)), dma((5,)), dma, dma((NZ,)), dma((4,)), dma((9,)), dma((9,)),
            dma((11,)), dma((3,)), dma((3,)), dma((3,)), dma((2,)),
        ],
        compiler_params=pltpu.CompilerParams(
            collective_id=0, has_side_effects=True, vmem_limit_bytes=40 * 2**20
        ),
    )(*[
        pltpu.with_memory_space_constraint(a, pltpu.HBM)
        for a in (table, target_table, centres, coefficients, batch_index)
    ])
    return pl.pallas_call(
        update,
        name="update",
        out_shape=(
            jax.ShapeDtypeStruct((512, 256), F32),
            jax.ShapeDtypeStruct((2, 256, 256), F32),
        ),
        in_specs=[vmem] * 6,
        out_specs=(pl.BlockSpec(memory_space=pl.ANY), pl.BlockSpec(memory_space=pl.ANY)),
        scratch_shapes=[pltpu.VMEM((512, 256), F32), dma((4,))],
        compiler_params=pltpu.CompilerParams(vmem_limit_bytes=24 * 2**20),
    )(*sums)


def solution(mesh):
    in_specs = (
        P("dev", None),
        P("dev", None),
        P(("grp", "dev"), None),
        P(("grp", "dev"), None),
        P(),
    )
    out_specs = (P(("grp", "dev"), None), P())
    return jax.shard_map(body, mesh=mesh, in_specs=in_specs, out_specs=out_specs, check_vma=False)
```

```python
import math

import jax
import jax.numpy as jnp
from jax import lax
from jax.experimental import pallas as pl
from jax.experimental.pallas import tpu as pltpu
from jax.sharding import PartitionSpec as P

MESH = pl.DeviceIdType.MESH
SPREAD = 2.0
RATE = 2.0
NX, NC, NY, NZ = 4, 2, 4, 8
NP = NX * NY
ND = NY * NZ
F32 = jnp.float32
BF16 = jnp.bfloat16
HI = lax.Precision.HIGHEST
NN = (((1,), (0,)), ((), ()))
NT = (((1,), (1,)), ((), ()))
TN = (((0,), (0,)), ((), ()))


def hops(k, n):
    return min(k, n - k)


Z_FAR = sorted(range(1, NZ), key=lambda k: -hops(k, NZ))
Z_NEAR = Z_FAR[::-1]
XY_FAR = sorted(
    [(i, j) for i in range(NX) for j in range(NY) if i or j],
    key=lambda o: -hops(o[0], NX) - hops(o[1], NY),
)
YZ_FAR = sorted(
    [(j, k) for j in range(NY) for k in range(NZ) if j or k],
    key=lambda o: -hops(o[0], NY) - hops(o[1], NZ),
)


def dot(a, b, dims=NN, precision=None):
    return lax.dot_general(a, b, dims, precision=precision, preferred_element_type=F32)


def split(a):
    high = a.astype(BF16)
    return high, (a - high.astype(F32)).astype(BF16)


SLOTS = [0, 2, 6, 3, 5, 4, 1, 7]
GROUPS = [(0, 1), (1, 2), (2, 3), (3, 6)]
SHARE = (16, 16, 24)


def rows_of(whole, h):
    return jnp.concatenate([whole[h, :, m * 8 : m * 8 + 8, :].reshape(128, 128) for m in range(2)], axis=1)


def pieces_to_whole(whole):
    return jnp.concatenate([rows_of(whole, h) for h in range(2)], axis=0)


def column(mass, s):
    tiles = [jnp.broadcast_to(mass[h, s : s + 1, :], (128, 128)).T for h in range(2)]
    tall = jnp.concatenate(tiles, axis=0)
    return jnp.concatenate([tall, tall], axis=1)


def project(resid, m):
    along = jnp.sum(m * resid, axis=0, keepdims=True) / jnp.sum(m * m, axis=0, keepdims=True)
    return resid - m * along


def grad(high, low, proj):
    ph, pw = split(proj)
    return dot(high, ph) + (dot(high, pw) + dot(low, ph))


def exchange(
    table, target, centres, coef, index,
    resid1_out, mass_out, wt_high, wt_low, coef_half, resid0_out,
    tab_v, tgt_v, cen_v, cnorm_v, cf_v, idx_v, aims_v, cf_high, cf_low,
    pick, parts, rows, w_high, w_low, w0_high, w0_low, w0_other_high, w0_other_low, w1_high, w1_low,
    wt0_high, wt0_low, mass_all,
    xy_send0, xy_send1, xy_send2, xy_recv0, xy_recv1, xy_recv2,
    z_buf0, z_buf1, z_buf2, whole0, whole1, whole2,
    load_sem, a_sent, a_recv, az_recv, axy_recv, pair_sent, pair_recv,
    c_sent, cxy_recv, cz_recv, gxy_recv, gc_recv,
):
    xy_send, xy_recv = (xy_send0, xy_send1, xy_send2), (xy_recv0, xy_recv1, xy_recv2)
    z_buf, whole = (z_buf0, z_buf1, z_buf2), (whole0, whole1, whole2)
    g = lax.axis_index("grp")
    d = lax.axis_index("dev")
    x, c = g // 2, g % 2
    y, z = d // NZ, d % NZ
    p = x * NY + y
    chunk = z * NY + y
    radius = math.sqrt(2.0 * 1024)
    scale = 1.0 / math.sqrt(131072)

    xs = [lax.rem(x + k, NX) for k in range(NX)]
    ys = [lax.rem(y + k, NY) for k in range(NY)]
    zs = [lax.rem(z + k, NZ) for k in range(NZ)]
    grps = [v * 2 + c for v in xs]
    bases = [v * NZ for v in ys]

    def at_xy(o):
        return {"grp": grps[o[0]], "dev": bases[o[1]] + z}

    def at_yz(o):
        return {"grp": g, "dev": bases[o[0]] + zs[o[1]]}

    sibling = {"grp": x * 2 + 1 - c, "dev": d}

    def send(src, dst, send_sem, recv_sem, to):
        copy = pltpu.make_async_remote_copy(
            src_ref=src, dst_ref=dst, send_sem=send_sem, recv_sem=recv_sem,
            device_id=to, device_id_type=MESH,
        )
        copy.start()
        return copy

    def wait_bytes(ref, sem):
        pltpu.make_async_copy(ref, ref, sem).wait()

    barrier = pltpu.get_barrier_semaphore()
    greeted = [at_yz(o) for o in YZ_FAR] + [at_xy(o) for o in XY_FAR if o[0]] + [sibling]
    for to in greeted:
        pl.semaphore_signal(barrier, inc=1, device_id=to, device_id_type=MESH)

    loads = [
        pltpu.make_async_copy(index, idx_v, load_sem.at[0]),
        pltpu.make_async_copy(
            table.at[:, pl.ds(pl.multiple_of(x * 256, 256), 256)], tab_v, load_sem.at[1]
        ),
        pltpu.make_async_copy(target, tgt_v, load_sem.at[2]),
        pltpu.make_async_copy(centres, cen_v.at[c], load_sem.at[3]),
        pltpu.make_async_copy(coef, cf_v, load_sem.at[4]),
    ]
    for load in loads:
        load.start()

    loads[0].wait()
    here = lax.broadcasted_iota(jnp.int32, (512, 128), 0) + d * 512
    half = pl.ds(pl.multiple_of(c * 128, 128), 128)
    hot = jnp.concatenate(
        [(here == idx_v[s : s + 1, half]).astype(F32).astype(BF16) for s in range(2)], axis=1
    )
    loads[1].wait()
    mine = dot(hot, tab_v[...], TN).astype(BF16).reshape(NZ, 2, 16, 256)
    for k in range(NY):
        pick[:, k] = mine[:, k // 2, :, k % 2 * 128 : k % 2 * 128 + 128]
    parts[chunk] = pick[z, y]

    pl.semaphore_wait(barrier, len(greeted))

    for o in YZ_FAR:
        send(
            pick.at[zs[o[1]], ys[o[0]]], parts.at[chunk], a_sent.at[0], a_recv, at_yz(o)
        )

    def to_sibling(src, dst, n):
        send(src, dst, pair_sent.at[n], pair_recv.at[n], sibling)

    loads[3].wait()
    to_sibling(cen_v.at[c], cen_v.at[c], 0)
    loads[4].wait()
    cf_high[c], cf_low[c] = split(cf_v[...])
    to_sibling(cf_high.at[c], cf_high.at[c], 1)
    to_sibling(cf_low.at[c], cf_low.at[c], 2)
    high, low = split(jnp.square(cen_v[c].astype(F32)))
    ones = jnp.ones((8, 1024), BF16)
    cnorm_v[c] = dot(ones, high, NT) + dot(ones, low, NT)
    to_sibling(cnorm_v.at[c], cnorm_v.at[c], 3)
    loads[2].wait()
    aims_v[...] = dot(hot, tgt_v[...], TN) * (x == 0).astype(F32)

    wait_bytes(parts.at[pl.ds(0, ND - 1)], a_recv)
    own = jnp.sum(parts[...].astype(F32), axis=0).astype(BF16)
    rows[0, x, y] = own

    mine = rows.at[0, x, y]
    for k in Z_FAR:
        slot = SLOTS.index(NZ - k)
        if slot < 6:
            send(mine, rows.at[slot, x, y], a_sent.at[1], az_recv.at[NZ - k], at_yz((0, k)))
    for n, (b, e) in enumerate(GROUPS):
        for r in SLOTS[b:e]:
            if r:
                wait_bytes(parts.at[0], az_recv.at[r])
        group = rows.at[pl.ds(b, e - b), x, y]
        for o in XY_FAR:
            send(group, group, a_sent.at[2 + n // 3], axy_recv.at[n], at_xy(o))

    def arrived(n):
        if n == 3:
            wait_bytes(xy_recv[2].at[pl.ds(0, NP - 1)], axy_recv.at[n])
        else:
            wait_bytes(parts.at[pl.ds(0, NP - 1)], axy_recv.at[n])

    arrived(0)
    for k, slot in ((1, 7), (7, 6)):
        send(rows.at[0], rows.at[slot], a_sent.at[4], az_recv.at[NZ - k], at_yz((0, k)))
    wait_bytes(cen_v.at[0], pair_recv.at[0])
    wait_bytes(cf_high.at[0], pair_recv.at[1])
    wait_bytes(cf_low.at[0], pair_recv.at[2])
    wait_bytes(cnorm_v.at[0], pair_recv.at[3])
    arrived(1)
    arrived(2)

    def values(b, e):
        n = e - b
        some = jnp.concatenate(
            [
                jnp.concatenate(
                    [rows[b:e, i, 2 * q + f].reshape(n * 16, 128) for i in range(NX) for f in range(2)],
                    axis=1,
                )
                for q in range(2)
            ],
            axis=0,
        )
        rnorm = jnp.sum(jnp.square(some.astype(F32)), axis=1, keepdims=True)
        for k in range(NC):
            cross = dot(some, cen_v[k], NT)
            dist = jnp.sqrt(jnp.maximum(rnorm + cnorm_v[k, 0:1, :] - 2.0 * cross, 0.0))
            high, low = split(jnp.exp((radius - dist) / SPREAD) * scale)
            for q in range(2):
                for r in range(b, e):
                    at = pl.ds(pl.multiple_of(zs[SLOTS[r]] * 32 + q * 16, 16), 16)
                    o = (q * n + r - b) * 16
                    w_high[k, at, :] = high[o : o + 16]
                    w_low[k, at, :] = low[o : o + 16]

    values(0, 3)
    for slot in (6, 7):
        wait_bytes(rows.at[0], az_recv.at[SLOTS[slot]])
    values(6, 8)
    arrived(3)
    values(3, 6)

    first, second = pl.ds(0, 128), pl.ds(128, 128)
    to_sibling(w_high.at[:, first], w0_other_high, 4)
    to_sibling(w_low.at[:, first], w0_other_low, 5)

    def put(part, dst, lane):
        dst[:, lane, :] = part.reshape(NP, 8, 128)

    def share_out(n):
        for o in XY_FAR:
            send(
                xy_send[n].at[xs[o[0]] * NY + ys[o[1]]], xy_recv[n].at[p],
                c_sent.at[n], cxy_recv.at[n], at_xy(o),
            )
        xy_recv[n][p] = xy_send[n][p]

    part = -aims_v[...]
    for k in range(NC):
        high, low, ch, cl = w_high[k], w_low[k], cf_high[k], cf_low[k]
        part = part + (dot(high, ch) + (dot(high, cl) + dot(low, ch)))
    for n in range(2):
        for m in range(2):
            put(part[n * 128 : n * 128 + 128, m * 128 : m * 128 + 128], xy_send[n], pl.ds(m * 8, 8))
        share_out(n)
    to_sibling(w_high.at[1 - c, second], w1_high.at[c], 6)
    to_sibling(w_low.at[1 - c, second], w1_low.at[c], 7)

    ones = jnp.ones((8, 512), BF16)
    mass = sum(dot(ones, w_high[k], NT) + dot(ones, w_low[k], NT) for k in range(NC))
    mass = jnp.concatenate([mass[0:1, 0:128], mass[0:1, 128:256], jnp.zeros((6, 128), F32)], axis=0)
    xy_send[2][:, 16:24, :] = jnp.broadcast_to(mass[None], (NP, 8, 128))

    def gram(others):
        part = jnp.zeros((128, 128), F32)
        for k in range(NC):
            high, low = w_high[k, second, :], w_low[k, second, :]
            gh, gl = others(k)
            part = part + (dot(high, gh, NT) + (dot(high, gl, NT) + dot(low, gh, NT)))
        return part

    own_lanes = pl.ds(pl.multiple_of(c * 8, 8), 8)
    other_lanes = pl.ds(pl.multiple_of(8 - c * 8, 8), 8)
    put(gram(lambda k: (w_high[k, first, :], w_low[k, first, :])), xy_send[2], own_lanes)
    wait_bytes(w0_other_high, pair_recv.at[4])
    wait_bytes(w0_other_low, pair_recv.at[5])
    put(gram(lambda k: (w0_other_high[k], w0_other_low[k])), xy_send[2], other_lanes)
    share_out(2)

    w0_high[c], w0_low[c] = w_high[c, first, :], w_low[c, first, :]
    w0_high[1 - c], w0_low[1 - c] = w0_other_high[c], w0_other_low[c]
    wt0_high[...] = w0_high[...].reshape(256, 512).T
    wt0_low[...] = w0_low[...].reshape(256, 512).T
    wait_bytes(w1_high.at[0], pair_recv.at[6])
    wait_bytes(w1_low.at[0], pair_recv.at[7])
    wait_bytes(w1_high.at[0], pair_sent.at[6])
    wait_bytes(w1_low.at[0], pair_sent.at[7])
    w1_high[c], w1_low[c] = w_high[c, second, :], w_low[c, second, :]
    wt_high[...] = w1_high[...].reshape(256, 512).T
    wt_low[...] = w1_low[...].reshape(256, 512).T

    for n in range(3):
        wait_bytes(xy_recv[n].at[pl.ds(0, NP - 1)], cxy_recv.at[n])
        z_buf[n][z] = jnp.sum(xy_recv[n][...], axis=0)
        for k in Z_FAR:
            send(z_buf[n].at[z], z_buf[n].at[z], c_sent.at[3 + n], cz_recv.at[n], at_yz((0, k)))
    for n in range(3):
        wait_bytes(z_buf[n].at[pl.ds(0, NZ - 1)], cz_recv.at[n])
        total = jnp.sum(z_buf[n][...], axis=0)
        whole[n][c, p] = total[0:16]
        for o in XY_FAR:
            send(whole[n].at[c, p], whole[n].at[c, p], c_sent.at[6 + n], gxy_recv.at[n], at_xy(o))
        if n == 2:
            mass_all[c] = total[16:24]
            to_sibling(mass_all.at[c], mass_all.at[c], 8)
    wait_bytes(whole[0].at[0, pl.ds(0, NP - 1)], gxy_recv.at[0])
    send(whole[0].at[c], whole[0].at[c], c_sent.at[9], gc_recv.at[0], sibling)
    wait_bytes(mass_all.at[0], pair_recv.at[8])
    m0 = column(mass_all, 0)
    mass_out[...] = column(mass_all, 1)
    wait_bytes(whole[0].at[0], gc_recv.at[0])
    resid0 = pieces_to_whole(whole0)
    resid0_out[...] = resid0
    proj0 = project(resid0, m0)
    wait_bytes(whole[1].at[0, pl.ds(0, NP - 1)], gxy_recv.at[1])
    wait_bytes(whole[2].at[0, pl.ds(0, NP - 1)], gxy_recv.at[2])
    own_rows = pl.ds(pl.multiple_of(c * 128, 128), 128)
    resid1_out[own_rows, :] = rows_of(whole1, c) - RATE * dot(rows_of(whole2, c), proj0, precision=HI)
    send(resid1_out.at[own_rows], resid1_out.at[own_rows], c_sent.at[10], gc_recv.at[1], sibling)
    coef_half[...] = cf_v[...] - RATE * grad(wt0_high[...], wt0_low[...], proj0)
    wait_bytes(resid1_out.at[pl.ds(0, 128)], gc_recv.at[1])

    wait_bytes(parts.at[pl.ds(0, ND - 1)], a_sent.at[0])
    wait_bytes(parts.at[pl.ds(0, 5)], a_sent.at[1])
    wait_bytes(xy_recv[2].at[pl.ds(0, NP - 1)], a_sent.at[2])
    wait_bytes(xy_recv[2].at[pl.ds(0, NP - 1)], a_sent.at[3])
    wait_bytes(rows.at[pl.ds(0, 2)], a_sent.at[4])
    for n, ref in enumerate((
        cen_v.at[0], cf_high.at[0], cf_low.at[0], cnorm_v.at[0], w0_other_high, w0_other_low, None, None,
        mass_all.at[0],
    )):
        if ref is not None:
            wait_bytes(ref, pair_sent.at[n])
    for n in range(3):
        wait_bytes(xy_recv[n].at[pl.ds(0, NP - 1)], c_sent.at[n])
        wait_bytes(z_buf[n].at[pl.ds(0, NZ - 1)], c_sent.at[3 + n])
        wait_bytes(whole[n].at[0, pl.ds(0, NP - 1)], c_sent.at[6 + n])
    wait_bytes(whole[0].at[0], c_sent.at[9])
    wait_bytes(resid1_out.at[pl.ds(0, 128)], c_sent.at[10])


def update(
    resid1, mass, wt_high, wt_low, coef_half, resid0, coef_out, resid_out, coef_v, out_sem
):
    copies = [pltpu.make_async_copy(resid0, resid_out.at[0], out_sem.at[0])]
    copies[0].start()
    copies.append(pltpu.make_async_copy(resid1, resid_out.at[1], out_sem.at[1]))
    copies[1].start()
    proj1 = project(resid1[...], mass[...])
    for m in range(2):
        at = pl.ds(m * 256, 256)
        coef_v[at, :] = coef_half[at, :] - RATE * grad(wt_high[at, :], wt_low[at, :], proj1)
        copies.append(pltpu.make_async_copy(coef_v.at[at], coef_out.at[at], out_sem.at[2 + m]))
        copies[2 + m].start()
    for copy in copies:
        copy.wait()


def body(table, target_table, centres, coefficients, batch_index):
    dma = pltpu.SemaphoreType.DMA
    vmem = pl.BlockSpec(memory_space=pltpu.VMEM)
    square = jax.ShapeDtypeStruct((256, 256), F32)
    turned = jax.ShapeDtypeStruct((512, 256), BF16)
    per_peer = [pltpu.VMEM((NP, n, 128), F32) for n in SHARE]
    sums = pl.pallas_call(
        exchange,
        name="exchange",
        out_shape=(
            square,
            square,
            turned,
            turned,
            jax.ShapeDtypeStruct((512, 256), F32),
            square,
        ),
        in_specs=[pl.BlockSpec(memory_space=pl.ANY)] * 5,
        out_specs=(vmem,) * 6,
        scratch_shapes=[
            pltpu.VMEM((512, 256), BF16),
            pltpu.VMEM((512, 256), BF16),
            pltpu.VMEM((NC, 512, 1024), BF16),
            pltpu.VMEM((NC, 8, 512), F32),
            pltpu.VMEM((512, 256), F32),
            pltpu.VMEM((2, 256), jnp.int32),
            pltpu.VMEM((256, 256), F32),
            pltpu.VMEM((NC, 512, 256), BF16),
            pltpu.VMEM((NC, 512, 256), BF16),
            pltpu.VMEM((NZ, NY, 16, 128), BF16),
            pltpu.VMEM((ND, 16, 128), BF16),
            pltpu.VMEM((NZ, NX, NY, 16, 128), BF16),
            *[pltpu.VMEM((NC, 256, 512), BF16) for _ in range(2)],
            *[pltpu.VMEM((NC, 128, 512), BF16) for _ in range(6)],
            *[pltpu.VMEM((512, 256), BF16) for _ in range(2)],
            pltpu.VMEM((NC, 8, 128), F32),
            *per_peer, *per_peer,
            *[pltpu.VMEM((NZ, n, 128), F32) for n in SHARE],
            *[pltpu.VMEM((2, NP, 16, 128), F32) for _ in range(3)],
            dma((5,)), dma((5,)), dma, dma((NZ,)), dma((4,)), dma((9,)), dma((9,)),
            dma((11,)), dma((3,)), dma((3,)), dma((3,)), dma((2,)),
        ],
        compiler_params=pltpu.CompilerParams(
            collective_id=0, has_side_effects=True, vmem_limit_bytes=40 * 2**20
        ),
    )(*[
        pltpu.with_memory_space_constraint(a, pltpu.HBM)
        for a in (table, target_table, centres, coefficients, batch_index)
    ])
    return pl.pallas_call(
        update,
        name="update",
        out_shape=(
            jax.ShapeDtypeStruct((512, 256), F32),
            jax.ShapeDtypeStruct((2, 256, 256), F32),
        ),
        in_specs=[vmem] * 6,
        out_specs=(pl.BlockSpec(memory_space=pl.ANY), pl.BlockSpec(memory_space=pl.ANY)),
        scratch_shapes=[pltpu.VMEM((512, 256), F32), dma((4,))],
        compiler_params=pltpu.CompilerParams(vmem_limit_bytes=24 * 2**20),
    )(*sums)


def solution(mesh):
    in_specs = (
        P("dev", None),
        P("dev", None),
        P(("grp", "dev"), None),
        P(("grp", "dev"), None),
        P(),
    )
    out_specs = (P(("grp", "dev"), None), P())
    return jax.shard_map(body, mesh=mesh, in_specs=in_specs, out_specs=out_specs, check_vma=False)
```
